32 devices in a mesh: dp: 2 (over core), fsdp: 16 (over z, y, x).
Axes of the slice: x: 2, y: 2, z: 4, core: 2. Of those that a mesh axis runs over, the one named last changes fastest.
Arguments:
- tokens_in: float32 [174080, 256], P(('dp', 'fsdp')), may hold values from -6 to 6
- cotangent: float32 [174080, 256], P(('dp', 'fsdp')), may hold values from -6 to 6
- crop_count: int32 [256], P(('dp', 'fsdp')), may hold values from 1 to 8
- wide_w: float32 [256, 2048], P('fsdp'), may hold values from -0.375 to 0.375
- wide_m: float32 [256, 2048], P('fsdp'), may hold values from -125.168686 to 125.168686
- wide_v: float32 [256, 2048], P('fsdp'), may hold values from 34.816 to 696.32
- wide_ema: float32 [256, 2048], P('fsdp'), may hold values from -0.375 to 0.375
- down_w: float32 [1024, 256], P('fsdp'), may hold values from -0.1875 to 0.1875
- down_m: float32 [1024, 256], P('fsdp'), may hold values from -125.168686 to 125.168686
- down_v: float32 [1024, 256], P('fsdp'), may hold values from 34.816 to 696.32
- down_ema: float32 [1024, 256], P('fsdp'), may hold values from -0.1875 to 0.1875
- small_p: float32 [5888], P('fsdp'), may hold values from -1 to 2, as said below
- small_m: float32 [5888], P('fsdp'), may hold values from -125.168686 to 125.168686
- small_v: float32 [5888], P('fsdp'), may hold values from 34.816 to 696.32
- small_ema: float32 [5888], P('fsdp'), may hold values from -1 to 2, as said below
Outputs:
- block_out: float32 [174080, 256], P(('dp', 'fsdp'))
- grad_in: float32 [174080, 256], P(('dp', 'fsdp'))
- wide_new: float32 [256, 2048], P('fsdp')
- wide_first: float32 [256, 2048], P('fsdp')
- wide_second: float32 [256, 2048], P('fsdp')
- wide_avg: float32 [256, 2048], P('fsdp')
- down_new: float32 [1024, 256], P('fsdp')
- down_first: float32 [1024, 256], P('fsdp')
- down_second: float32 [1024, 256], P('fsdp')
- down_avg: float32 [1024, 256], P('fsdp')
- small_new: float32 [5888], P('fsdp')
- small_first: float32 [5888], P('fsdp')
- small_second: float32 [5888], P('fsdp')
- small_avg: float32 [5888], P('fsdp')
- norms: float32 [2, 4], replicated
The draws below stay inside these ranges and needn't reach their ends.
Inputs may be any that keep to these rules, and one draw needn't show every extreme that they name: Local crop slots from crop_count onward hold tokens whose output gets no cotangent. `small_p`: gains about one, other entries of either sign. `small_ema`: gains about one, other entries of either sign.
All inputs are finite; a program needn't handle non-finite values.
Results may differ from the reference program's by a relative error of at most 0.0086.
Values may be sent and summed in bfloat16 or wider, within the bound.
No kernel may reach another device: no remote copies, remote signals or barrier semaphores. Data moves between devices by JAX's collectives and lax.ppermute only.
A program may use at most 320 MiB of HBM per device.

```python
import math
import jax
import jax.numpy as jnp
from jax import lax

D = 256
FF = 1024
HEAD = 32
STRIPE = 7
GRID_L = 14
GRID_S = 6
SMALL = 8
STEP = 10
TOK_IMG = 680
TOK_DEV = 5440
IMAGES = 256
TOKENS = 174080
WIDE = 2048
SMALL_P = 5888


def small_centre():
    return jnp.concatenate([jnp.ones((D,), jnp.float32), jnp.zeros((15 * D,), jnp.float32), jnp.ones((D,), jnp.float32), jnp.zeros((FF + 2 * D,), jnp.float32)])


def draw_small_p(key, part):
    key = jax.random.fold_in(key, 11)
    noise = 0.3 * jnp.clip(jax.random.normal(key, (SMALL_P,), jnp.float32), -2.5, 2.5)
    return small_centre() + noise


def draw_small_ema(key, part):
    key = jax.random.fold_in(key, 12)
    noise = 0.3 * jnp.clip(jax.random.normal(key, (SMALL_P,), jnp.float32), -2.5, 2.5)
    return small_centre() + noise


def place_ends(entries, rng, smallest, largest):
    shape = entries.shape
    index_at = [jax.random.randint(jax.random.fold_in(rng, axis), (), 0, shape[axis]) for axis in range(len(shape))]
    entries = entries.at[tuple(index_at)].set(smallest)
    longest = shape.index(max(shape))
    index_at[longest] = (index_at[longest] + 1) % shape[longest]
    return entries.at[tuple(index_at)].set(largest)


def block_scale(key, shape, shards, low, high):
    level = 1.0
    for dim, shards_of in shards:
        steps = jax.random.uniform(jax.random.fold_in(jax.random.fold_in(key, 6), dim), (shards_of,), jnp.float32, low / len(shards), high / len(shards))
        level = level * jnp.repeat(jnp.exp(steps), shape[dim] // shards_of).reshape((-1,) + (1,) * (len(shape) - 1 - dim))
    return level


def centred(own_key, shape, deviation, limit, shards=(), kind=jnp.bfloat16):
    array = deviation * jax.random.normal(own_key, shape, jnp.float32)
    if shards:
        array = array * block_scale(own_key, shape, shards, -0.22, 0.18)
    return jnp.clip(array, -limit, limit).astype(kind)


def setup_inputs(seed: int = 0) -> dict:
    key_list = jax.random.split(jax.random.key(seed), 16)
    tokens_in = centred(key_list[0], (TOKENS, D), 1.0, 6.0, ((0, 32),), jnp.float32)
    cotangent = centred(key_list[1], (TOKENS, D), 1.0, 6.0, ((0, 32),), jnp.float32)
    crop_count = place_ends(jax.random.randint(key_list[2], (IMAGES,), 1, SMALL + 1), jax.random.fold_in(key_list[2], 1), 1, SMALL).astype(jnp.int32)
    wide_w = centred(key_list[3], (D, WIDE), D ** -0.5, 0.375, ((0, 16),), jnp.float32)
    wide_m = centred(key_list[4], (D, WIDE), (0.05 * TOKENS ** 0.5), 125.168686, ((0, 16),), jnp.float32)
    wide_v = jnp.clip(jnp.exp(math.log(696.32) - 2.9957322 * jax.random.uniform(key_list[5], (D, WIDE), jnp.float32) ** block_scale(key_list[5], (D, WIDE), ((0, 16),), -0.2, 0.2)), 34.816, 696.32)
    wide_ema = centred(key_list[6], (D, WIDE), D ** -0.5, 0.375, ((0, 16),), jnp.float32)
    down_w = centred(key_list[7], (FF, D), FF ** -0.5, 0.1875, ((0, 16),), jnp.float32)
    down_m = centred(key_list[8], (FF, D), (0.05 * TOKENS ** 0.5), 125.168686, ((0, 16),), jnp.float32)
    down_v = jnp.clip(jnp.exp(math.log(696.32) - 2.9957322 * jax.random.uniform(key_list[9], (FF, D), jnp.float32) ** block_scale(key_list[9], (FF, D), ((0, 16),), -0.2, 0.2)), 34.816, 696.32)
    down_ema = centred(key_list[10], (FF, D), FF ** -0.5, 0.1875, ((0, 16),), jnp.float32)
    small_p = draw_small_p(jax.random.fold_in(key_list[15], 71), 0)
    small_m = centred(key_list[12], (SMALL_P,), (0.05 * TOKENS ** 0.5), 125.168686, ((0, 16),), jnp.float32)
    small_v = jnp.clip(jnp.exp(math.log(696.32) - 2.9957322 * jax.random.uniform(key_list[13], (SMALL_P,), jnp.float32) ** block_scale(key_list[13], (SMALL_P,), ((0, 16),), -0.2, 0.2)), 34.816, 696.32)
    small_ema = draw_small_ema(jax.random.fold_in(key_list[15], 71), 0)
    return dict(tokens_in=tokens_in, cotangent=cotangent, crop_count=crop_count, wide_w=wide_w, wide_m=wide_m, wide_v=wide_v, wide_ema=wide_ema, down_w=down_w, down_m=down_m, down_v=down_v, down_ema=down_ema, small_p=small_p, small_m=small_m, small_v=small_v, small_ema=small_ema)


EPSILON = 1e-05
BETA_ONE = 0.9
BETA_TWO = 0.999
ADAM_EPS = 1e-06
DECAY = 0.05
RATE = 0.25
EMA_CEILING = 0.9999

@jax.custom_vjp
def low(v):
    return lax.optimization_barrier(v.astype(jnp.bfloat16)).astype(jnp.float32)

@jax.custom_vjp
def low_back(v):
    return v

def low_keep(v):
    return (low(v), None)

def low_pass(kept, grad):
    return (grad,)

def back_keep(v):
    return (v, None)

def back_low(kept, grad):
    return (low(grad),)
low.defvjp(low_keep, low_pass)
low_back.defvjp(back_keep, back_low)

def matmul(left_side, right_side):
    return jnp.dot(left_side, right_side, precision=lax.Precision.HIGHEST, preferred_element_type=jnp.float32)

def layer_norm(values, gain, shift):
    center = values - lax.optimization_barrier(jnp.mean(values, axis=-1, keepdims=True))
    spread = lax.optimization_barrier(jnp.mean(center * center, axis=-1, keepdims=True))
    return center * lax.rsqrt(spread + EPSILON) * gain + shift

def lepe_conv(values, kernel, offset):
    height, breadth = (values.shape[1], values.shape[2])
    padded = jnp.pad(values, ((0, 0), (1, 1), (1, 1), (0, 0)))
    result = jnp.zeros_like(values) + offset
    for row_shift in range(3):
        for col_shift in range(3):
            result = result + kernel[row_shift, col_shift] * padded[:, row_shift:row_shift + height, col_shift:col_shift + breadth]
    return result

def to_windows(crop_grid, stripe, vertical):
    number, height, breadth, channels = crop_grid.shape
    if vertical:
        reshaped = crop_grid.reshape(number, height, breadth // stripe, stripe, channels).transpose(0, 2, 1, 3, 4)
        return reshaped.reshape(number * (breadth // stripe), height, stripe, channels)
    return crop_grid.reshape(number * (height // stripe), stripe, breadth, channels)

def from_windows(windows, number, height, breadth, stripe, vertical):
    channels = windows.shape[-1]
    if vertical:
        reshaped = windows.reshape(number, breadth // stripe, height, stripe, channels).transpose(0, 2, 1, 3, 4)
        return reshaped.reshape(number, height, breadth, channels)
    return windows.reshape(number, height, breadth, channels)

def unpack(vector):
    bounds = [D, D, 3 * D, 9 * D, D, D, D, D, FF, D]
    pieces = []
    position = 0
    for extent in bounds:
        pieces.append(vector[position:position + extent])
        position = position + extent
    return pieces

def split_crops(flat):
    channels = flat.shape[-1]
    images = flat.reshape(-1, TOK_IMG, channels)
    large_count = 2 * GRID_L * GRID_L
    large_grid = images[:, :large_count].reshape(-1, GRID_L, GRID_L, channels)
    small_grid = images[:, large_count:].reshape(-1, GRID_S, GRID_S, channels)
    return (large_grid, small_grid)

def join_crops(large_grid, small_grid):
    channels = large_grid.shape[-1]
    image_count = large_grid.shape[0] // 2
    joined = jnp.concatenate([large_grid.reshape(image_count, -1, channels), small_grid.reshape(image_count, -1, channels)], axis=1)
    return joined.reshape(-1, channels)

def stripe_mix(queries, keys_in, values_in, kernel, offset):
    number, height, breadth, channels = queries.shape
    length = height * breadth
    head_count = channels // HEAD
    query_heads = queries.reshape(number, length, head_count, HEAD)
    key_heads = keys_in.reshape(number, length, head_count, HEAD)
    value_heads = values_in.reshape(number, length, head_count, HEAD)
    raw_scores = jnp.einsum('nlhd,nmhd->nhlm', query_heads, key_heads, precision=lax.Precision.HIGHEST)
    scores = low_back(raw_scores) * HEAD ** (-0.5)
    row_peak = lax.optimization_barrier(jnp.max(scores, axis=-1, keepdims=True))
    exponent = jnp.exp(scores - row_peak)
    row_total = lax.optimization_barrier(jnp.sum(exponent, axis=-1, keepdims=True))
    weights_soft = low(exponent / row_total)
    mixture = jnp.einsum('nhlm,nmhd->nlhd', weights_soft, value_heads, precision=lax.Precision.HIGHEST)
    return mixture.reshape(number, height, breadth, channels) + lepe_conv(values_in, kernel, offset)

def attend(crop_grid, kernel, offset):
    number, height, breadth, triple = crop_grid.shape
    half = triple // 6
    stripe = min(STRIPE, height)
    outputs = []
    for branch in range(2):
        vertical = branch == 1
        pieces = [to_windows(crop_grid[..., column_base + branch * half:column_base + (branch + 1) * half], stripe, vertical) for column_base in (0, 2 * half, 4 * half)]
        mixture = stripe_mix(pieces[0], pieces[1], pieces[2], kernel[:, :, branch * half:(branch + 1) * half], offset[branch * half:(branch + 1) * half])
        outputs.append(from_windows(mixture, number, height, breadth, stripe, vertical))
    return jnp.concatenate(outputs, axis=-1)

def forward(tokens, wide, down, small):
    wide_low = low(wide)
    down_low = low(down)
    small_low = low(small)
    gain_one, shift_one, bias_qkv, kernel_flat, kernel_bias, bias_out, gain_two, shift_two, bias_up, bias_down = unpack(small_low)
    kernel = kernel_flat.reshape(3, 3, D)
    normed = low(layer_norm(tokens, gain_one, shift_one))
    projected = low(low_back(matmul(normed, wide_low[:, :3 * D]) + bias_qkv))
    large_grid, small_grid = split_crops(projected)
    mixed = join_crops(attend(large_grid, kernel, kernel_bias), attend(small_grid, kernel, kernel_bias))
    mixed_low = low(low_back(mixed))
    residual = tokens + low_back(matmul(mixed_low, wide_low[:, 3 * D:4 * D]) + bias_out)
    second = low(layer_norm(residual, gain_two, shift_two))
    hidden = low_back(matmul(second, wide_low[:, 4 * D:]) + bias_up)
    activated = low(jax.nn.gelu(hidden, approximate=False))
    return residual + low_back(matmul(activated, down_low) + bias_down)

def crop_mask(counts):
    slots = jnp.arange(SMALL, dtype=jnp.int32)
    live_slots = (slots[None, :] < counts[:, None]).astype(jnp.float32)
    small_part = jnp.repeat(live_slots, GRID_S * GRID_S, axis=1)
    large_part = jnp.ones((counts.shape[0], 2 * GRID_L * GRID_L), jnp.float32)
    return jnp.concatenate([large_part, small_part], axis=1)

def moments(grad, first, second):
    first_new = BETA_ONE * first + (1.0 - BETA_ONE) * grad
    second_new = BETA_TWO * second + (1.0 - BETA_TWO) * grad * grad
    direction = first_new / (1.0 - BETA_ONE ** STEP) / (jnp.sqrt(second_new / (1.0 - BETA_TWO ** STEP)) + ADAM_EPS)
    return (first_new, second_new, direction)

def matrix_squares(wide, down):
    column_sq = lax.optimization_barrier(jnp.sum(wide * wide, axis=0))
    return jnp.stack([jnp.sum(column_sq[:3 * D]), jnp.sum(column_sq[3 * D:4 * D]), jnp.sum(column_sq[4 * D:]), jnp.sum(down * down)])

def reference(tokens_in, cotangent, crop_count, wide_w, wide_m, wide_v, wide_ema, down_w, down_m, down_v, down_ema, small_p, small_m, small_v, small_ema):
    live = crop_mask(crop_count).reshape(-1, TOK_DEV)
    groups = tokens_in.reshape(-1, TOK_DEV, D)
    group_cot = cotangent.reshape(-1, TOK_DEV, D) * live[..., None]

    def one_group(carry, inputs):
        group_tokens, weighted_cot = inputs
        output, pullback = jax.vjp(forward, group_tokens, wide_w, down_w, small_p)
        grad_tokens, grad_wide, grad_down, grad_small = pullback(weighted_cot)
        return ((carry[0] + grad_wide, carry[1] + grad_down, carry[2] + grad_small), (output, grad_tokens))
    start = (jnp.zeros_like(wide_w), jnp.zeros_like(down_w), jnp.zeros_like(small_p))
    totals, (outputs, grads) = lax.scan(one_group, start, (groups, group_cot))
    grad_wide, grad_down, grad_small = totals
    wide_first, wide_second, wide_dir = moments(grad_wide, wide_m, wide_v)
    down_first, down_second, down_dir = moments(grad_down, down_m, down_v)
    small_first, small_second, small_dir = moments(grad_small, small_m, small_v)
    wide_upd = wide_dir + DECAY * wide_w
    down_upd = down_dir + DECAY * down_w
    weight_norm = jnp.sqrt(matrix_squares(wide_w, down_w))
    update_norm = jnp.sqrt(matrix_squares(wide_upd, down_upd))
    ratio = weight_norm / update_norm
    column_ratio = jnp.concatenate([ratio[0] * jnp.ones((3 * D,), jnp.float32), ratio[1] * jnp.ones((D,), jnp.float32), ratio[2] * jnp.ones((FF,), jnp.float32)])
    wide_new = wide_w - RATE * column_ratio * wide_upd
    down_new = down_w - RATE * ratio[3] * down_upd
    small_new = small_p - RATE * small_dir
    ema_keep = min(EMA_CEILING, (1.0 + STEP) / (10.0 + STEP))
    wide_avg = ema_keep * wide_ema + (1.0 - ema_keep) * wide_new
    down_avg = ema_keep * down_ema + (1.0 - ema_keep) * down_new
    small_avg = ema_keep * small_ema + (1.0 - ema_keep) * small_new
    norms = jnp.stack([weight_norm, update_norm])
    return (outputs.reshape(-1, D), grads.reshape(-1, D), wide_new, wide_first, wide_second, wide_avg, down_new, down_first, down_second, down_avg, small_new, small_first, small_second, small_avg, norms)
```

```python
import functools

import jax
import jax.numpy as jnp
import numpy as np
from jax import lax
from jax.experimental import pallas as pl
from jax.experimental.pallas import tpu as pltpu
from jax.sharding import PartitionSpec as P

D = 256
FF = 1024
HEAD = 32
STRIPE = 7
GRID_L = 14
GRID_S = 6
SMALL = 8
STEP = 10
TOK_IMG = 680

EPSILON = 1e-05
BETA_ONE = 0.9
BETA_TWO = 0.999
ADAM_EPS = 1e-06
DECAY = 0.05
RATE = 0.25
EMA_CEILING = 0.9999

ROWS = 688
BIG = 2 * GRID_L * GRID_L
PAIRS = 7
WIN = 128
QROWS = 112
HALF = 128
HEADS = 4
SCALE = HEAD**-0.5
LOG2E = 1.4426950408889634
LN2 = 0.6931471805599453
CHUNKS = ((0, 176), (176, 352), (352, 528), (528, 688))
BLOCKS = ((0, 208), (192, 400), (384, 512), (496, 608), (608, 688))
FIRST = (0, 196, 392, 500, 608)
GROUP = (3, 3, 2)
VMEM = 62 * 1024 * 1024

BF = jnp.bfloat16
F32 = jnp.float32


def window_tokens(block, branch):
    if block < 2:
        index = np.full((2, WIN), -1)
        for window in range(2):
            for r in range(GRID_L):
                for c in range(GRID_L):
                    if branch == 0:
                        w, at = divmod(r * GRID_L + c, STRIPE * GRID_L)
                    else:
                        w, at = c // STRIPE, r * STRIPE + c % STRIPE
                    index[w, at] = FIRST[block] + r * GRID_L + c
        return index.reshape(-1)
    count = GROUP[block - 2] * GRID_S * GRID_S
    index = np.full((WIN,), -1)
    index[:count] = FIRST[block] + np.arange(count)
    return index


def select_matrix(block, branch):
    low, high = BLOCKS[block]
    index = window_tokens(block, branch)
    return (index[:, None] == np.arange(low, high)[None, :]).astype(np.float32)


def tap_matrix(kind):
    shape = ((STRIPE, GRID_L), (GRID_L, STRIPE), (GRID_S, GRID_S))[kind]
    copies = (1, 1, 3)[kind]
    size = shape[0] * shape[1]
    out = np.zeros((9, QROWS, WIN), np.float32)
    for copy in range(copies):
        for r in range(shape[0]):
            for c in range(shape[1]):
                for tap in range(9):
                    rr, cc = r + tap // 3 - 1, c + tap % 3 - 1
                    if 0 <= rr < shape[0] and 0 <= cc < shape[1]:
                        out[tap, copy * size + r * shape[1] + c, copy * size + rr * shape[1] + cc] = 1
    return out


def mask_operands():
    size = GRID_S * GRID_S
    rows = np.zeros((3, QROWS, HALF), np.float32)
    keys = np.zeros((3, WIN, HALF), np.float32)
    rows[0, :, 0] = 1
    keys[0, STRIPE * GRID_L :, 0] = -1e30
    for kind, crops in ((1, 3), (2, 2)):
        for at in range(QROWS):
            rows[kind, at, at // size if at < crops * size else 0] = 1
        for at in range(WIN):
            for crop in range(crops):
                if at >= crops * size or at // size != crop:
                    keys[kind, at, crop] = -1e30
    return rows, np.tile(keys, (1, HEADS, 1))


def bf(array):
    return jnp.asarray(array, BF)


def dot(left, right):
    return jnp.dot(left, right, preferred_element_type=F32)


def dot_nt(left, right):
    return lax.dot_general(left, right, (((1,), (1,)), ((), ())), preferred_element_type=F32)


def dot_tn(left, right):
    return lax.dot_general(left, right, (((0,), (0,)), ((), ())), preferred_element_type=F32)


def normalise(values):
    center = values - jnp.mean(values, axis=-1, keepdims=True)
    spread = jnp.mean(center * center, axis=-1, keepdims=True)
    scale = lax.rsqrt(spread + EPSILON)
    return center * scale, scale


def norm_back(grad_hat, hat, scale):
    mean_grad = jnp.mean(grad_hat, axis=-1, keepdims=True)
    mean_dot = jnp.mean(grad_hat * hat, axis=-1, keepdims=True)
    return scale * (grad_hat - mean_grad - hat * mean_dot)


def rows_of(ref, low, high):
    if high <= TOK_IMG:
        return ref[low:high, :]
    tail = jnp.zeros((high - TOK_IMG, ref.shape[1]), F32)
    return jnp.concatenate([ref[low:TOK_IMG, :], tail], axis=0)


def store_rows(ref, low, high, values):
    last = min(high, TOK_IMG)
    ref[low:last, :] = values[: last - low]


def fold(values):
    return jnp.sum(values.reshape(values.shape[0] // 8, 8, values.shape[1]), axis=0)


def head_lanes(head):
    lanes = lax.broadcasted_iota(jnp.int32, (1, HALF), 1)
    return jnp.where(lanes // HEAD == head, 1.0, 0.0).astype(BF)


def by_head(values):
    return jnp.concatenate([values * head_lanes(h) for h in range(HEADS)], axis=0)


def head_block(rows):
    return jnp.concatenate(
        [jnp.broadcast_to(head_lanes(h), (rows, HALF)) for h in range(HEADS)], axis=0
    )


def attend_kernel(
    x_ref,
    w_ref,
    s_ref,
    k_ref,
    p0h_ref,
    p0v_ref,
    p1h_ref,
    p1v_ref,
    pg0_ref,
    pg1_ref,
    pg2_ref,
    tap_ref,
    mrow_ref,
    mkey_ref,
    a_ref,
    att_ref,
    win_ref,
    e_ref,
    il_ref,
    o_ref,
    qkv_scr,
    attw_scr,
    attf_scr,
):
    gain, shift = s_ref[0:1, :], s_ref[1:2, :]
    for low, high in CHUNKS:
        hat, _ = normalise(rows_of(x_ref, low, high))
        a = (hat * gain + shift).astype(BF)
        a_ref[0, low:high, :] = a
        qkv = dot(a, w_ref[...])
        for part in range(3):
            piece = qkv[:, part * D : (part + 1) * D] + s_ref[2 + part : 3 + part, :]
            if part == 0:
                piece = piece * (SCALE * LOG2E)
            piece = piece.astype(BF)
            for branch in range(2):
                qkv_scr[branch, low:high, part * HALF : (part + 1) * HALF] = piece[
                    :, branch * HALF : (branch + 1) * HALF
                ]
    attf_scr[...] = jnp.zeros_like(attf_scr)
    attw_scr[...] = jnp.zeros_like(attw_scr)
    crops = ((p0h_ref, p0v_ref), (p1h_ref, p1v_ref))
    groups = (pg0_ref, pg1_ref, pg2_ref)
    for branch in range(2):
        for crop in range(2):
            low, high = BLOCKS[crop]
            got = dot(crops[crop][branch][...], qkv_scr[branch, low:high, :]).astype(BF)
            at = 4 * branch + 2 * crop
            win_ref[0, at] = got[:WIN]
            win_ref[0, at + 1] = got[WIN:]
        for group in range(3):
            low, high = BLOCKS[2 + group]
            got = dot(groups[group][...], qkv_scr[branch, low:high, :]).astype(BF)
            win_ref[0, 8 + 2 * group + branch] = got

    ones = head_block(WIN)

    def one_pair(pair, carry):
        kind = jnp.minimum(pair // 2, 2)
        mask_kind = jnp.maximum(pair - 4, 0)
        mask_kind = jnp.where(pair < 4, 0, jnp.where(pair < 6, 1, 2))
        taps = []
        mixed = []
        for member in range(2):
            at = 2 * pair + member
            branch = jnp.where(pair < 2, 0, jnp.where(pair < 4, 1, member))
            q = win_ref[0, at, :QROWS, 0:HALF]
            k = win_ref[0, at, :, HALF : 2 * HALF]
            v = win_ref[0, at, :, 2 * HALF :]
            left = jnp.concatenate([q, mrow_ref[mask_kind]], axis=1)
            right = jnp.concatenate([by_head(k), mkey_ref[mask_kind]], axis=1)
            scores = dot_nt(left, right)
            exps = []
            for h in range(HEADS):
                part = scores[:, h * WIN : (h + 1) * WIN]
                peak = jnp.max(part, axis=-1, keepdims=True)
                exps.append(jnp.exp2(part - peak).astype(BF))
            e = jnp.concatenate(exps, axis=1)
            e_ref[0, at] = e
            both = dot(e, jnp.concatenate([by_head(v), ones], axis=1))
            inv = 1.0 / both[:, HALF:]
            o = both[:, :HALF] * inv
            il_ref[0, at] = inv
            o_ref[0, at] = o.astype(BF)
            kernel = k_ref[branch]
            mixed.append(o + kernel[9:10])
            taps.append(
                jnp.concatenate(
                    [
                        v * kernel[tap : tap + 1].astype(BF) for tap in range(9)
                    ],
                    axis=0,
                )
            )
        conv = dot(tap_ref[kind], jnp.concatenate(taps, axis=1))
        for member in range(2):
            piece = mixed[member] + conv[:, member * HALF : (member + 1) * HALF]
            attw_scr[2 * pair + member, :QROWS, :] = piece.astype(BF)
        return carry

    lax.fori_loop(0, PAIRS, one_pair, 0)

    for branch in range(2):
        lanes = slice(branch * HALF, (branch + 1) * HALF)
        for crop in range(2):
            low, high = BLOCKS[crop]
            at = 4 * branch + 2 * crop
            rows = attw_scr[at : at + 2].reshape(2 * WIN, HALF)
            attf_scr[low:high, lanes] += dot_tn(crops[crop][branch][...], rows)
        for group in range(3):
            low, high = BLOCKS[2 + group]
            attf_scr[low:high, lanes] += dot_tn(
                groups[group][...], attw_scr[8 + 2 * group + branch]
            )
    att_ref[0] = attf_scr[...].astype(BF)


def gelu_parts(u):
    size = jnp.abs(u)
    t = 1.0 / (1.0 + (0.3275911 * 2**-0.5) * size)
    decay = jnp.exp2((-0.5 * LOG2E) * (u * u))
    poly = 0.5 * 1.061405429
    for term in (-1.453152027, 1.421413741, -0.284496736, 0.254829592):
        poly = poly * t + 0.5 * term
    tail = poly * t * decay
    phi = jnp.where(u >= 0, 1.0 - tail, tail)
    slope = phi + (u * 0.3989422804014327) * decay
    return phi, slope


def feed_kernel(
    cnt_ref,
    x_ref,
    c_ref,
    att_ref,
    w_ref,
    down_ref,
    s_ref,
    out_ref,
    dx_ref,
    datt_ref,
    gup_ref,
    gdn_ref,
    gout_ref,
    sums_ref,
    bup_ref,
    h2_scr,
    u_scr,
    dg_scr,
    g_scr,
    du_scr,
    dy_scr,
    dz_scr,
    x1_scr,
):
    image = pl.program_id(0)

    @pl.when(image == 0)
    def _():
        for ref in (gup_ref, gdn_ref, gout_ref, sums_ref, bup_ref):
            ref[...] = jnp.zeros_like(ref)

    bound = BIG + GRID_S * GRID_S * cnt_ref[image]
    bias_out, gain, shift = s_ref[15:16, :], s_ref[16:17, :], s_ref[17:18, :]
    w_out, w_up = w_ref[:, 3 * D : 4 * D], w_ref[:, 4 * D :]
    for low, high in CHUNKS:
        att = att_ref[0, low:high, :]
        x1 = rows_of(x_ref, low, high) + dot(att, w_out) + bias_out
        x1_scr[low:high, :] = x1
        hat, scale = normalise(x1)
        h2 = (hat * gain + shift).astype(BF)
        h2_scr[low:high, :] = h2
        u_scr[low:high, :] = dot(h2, w_up)
        row = low + lax.broadcasted_iota(jnp.int32, (high - low, 1), 0)
        dy = jnp.where(row < bound, rows_of(c_ref, low, high), 0.0)
        dyr = dy.astype(BF)
        dy_scr[low:high, :] = dyr
        sums_ref[0] += fold(dyr.astype(F32))
        dg_scr[low:high, :] = dot_nt(dyr, down_ref[...])
        for part in range(4):
            lanes = slice(part * D, (part + 1) * D)
            bias = s_ref[18 + part : 19 + part, :]
            total = jnp.zeros((8, D), F32)
            for at in range(low, high, 16):
                u = u_scr[at : at + 16, lanes] + bias
                phi, slope = gelu_parts(u)
                g_scr[at : at + 16, lanes] = (u * phi).astype(BF)
                du = dg_scr[at : at + 16, lanes] * slope
                total = total + fold(du)
                du_scr[at : at + 16, lanes] = du.astype(BF)
            bup_ref[:, lanes] += total
        block = x1_scr[low:high, :] + dot(g_scr[low:high, :], down_ref[...]) + s_ref[22:23, :]
        store_rows(out_ref, low, high, block)
        dh2 = dot_nt(du_scr[low:high, :], w_up)
        hat, scale = normalise(x1_scr[low:high, :])
        sums_ref[1] += fold(dh2 * hat)
        sums_ref[2] += fold(dh2)
        row = low + lax.broadcasted_iota(jnp.int32, (high - low, 1), 0)
        dy = jnp.where(row < bound, rows_of(c_ref, low, high), 0.0)
        dx = dy + norm_back(dh2 * gain, hat, scale)
        store_rows(dx_ref, low, high, dx)
        dz = dx.astype(BF)
        dz_scr[low:high, :] = dz
        sums_ref[3] += fold(dz.astype(F32))
        datt = dot_nt(dz, w_out)
        sums_ref[4] += fold(datt)
        datt_ref[0, low:high, :] = datt.astype(BF)
    gup_ref[...] += dot_tn(h2_scr[...], du_scr[...])
    gdn_ref[...] += dot_tn(dy_scr[...], g_scr[...])
    gout_ref[...] += dot_tn(att_ref[0], dz_scr[...])


def back_kernel(
    datt_ref,
    win_ref,
    e_ref,
    il_ref,
    o_ref,
    a_ref,
    k_ref,
    p0h_ref,
    p0v_ref,
    p1h_ref,
    p1v_ref,
    pg0_ref,
    pg1_ref,
    pg2_ref,
    tap_ref,
    rows_ref,
    dqkv_ref,
    g_ref,
    kern_ref,
    sums_ref,
    dw_scr,
    dqkvw_scr,
    dqkvf_scr,
):
    image = pl.program_id(0)

    @pl.when(image == 0)
    def _():
        for ref in (g_ref, kern_ref, sums_ref):
            ref[...] = jnp.zeros_like(ref)

    crops = ((p0h_ref, p0v_ref), (p1h_ref, p1v_ref))
    groups = (pg0_ref, pg1_ref, pg2_ref)
    for branch in range(2):
        lanes = slice(branch * HALF, (branch + 1) * HALF)
        for crop in range(2):
            low, high = BLOCKS[crop]
            got = dot(crops[crop][branch][...], datt_ref[0, low:high, lanes]).astype(BF)
            at = 4 * branch + 2 * crop
            dw_scr[at] = got[:WIN]
            dw_scr[at + 1] = got[WIN:]
        for group in range(3):
            low, high = BLOCKS[2 + group]
            got = dot(groups[group][...], datt_ref[0, low:high, lanes]).astype(BF)
            dw_scr[8 + 2 * group + branch] = got
    dqkvw_scr[...] = jnp.zeros_like(dqkvw_scr)
    dqkvf_scr[...] = jnp.zeros_like(dqkvf_scr)
    minus = -head_block(WIN)

    def one_pair(pair, carry):
        kind = jnp.minimum(pair // 2, 2)
        taps, values, grads, dvs = [], [], [], []
        for member in range(2):
            at = 2 * pair + member
            branch = jnp.where(pair < 2, 0, jnp.where(pair < 4, 1, member))
            q = win_ref[0, at, :QROWS, 0:HALF]
            k = win_ref[0, at, :, HALF : 2 * HALF]
            v = win_ref[0, at, :, 2 * HALF :]
            dwin = dw_scr[at]
            dwf = dwin[:QROWS].astype(F32)
            dn = dwf * il_ref[0, at]
            z = (dn * o_ref[0, at].astype(F32)).astype(BF)
            dn = dn.astype(BF)
            left = jnp.concatenate([dn, z], axis=1)
            right = jnp.concatenate([by_head(v), minus], axis=1)
            ds = (dot_nt(left, right) * e_ref[0, at].astype(F32)).astype(BF)
            dq = dot(ds, by_head(k)) * SCALE
            dqkvw_scr[at, :QROWS, 0:HALF] = dq.astype(BF)
            dks, dvt = [], []
            for h in range(HEADS):
                lanes = slice(h * WIN, (h + 1) * WIN)
                own = slice(h * HEAD, (h + 1) * HEAD)
                dks.append(dot_tn(q, ds[:, lanes])[own])
                dvt.append(dot_tn(dn, e_ref[0, at, :, lanes])[own])
            dk = jnp.concatenate(dks, axis=0).T * LN2
            dqkvw_scr[at, :, HALF : 2 * HALF] = dk.astype(BF)
            dvs.append(jnp.concatenate(dvt, axis=0).T)
            kernel = k_ref[branch]
            taps.append(
                jnp.concatenate(
                    [
                        dwin * kernel[8 - tap : 9 - tap].astype(BF) for tap in range(9)
                    ],
                    axis=0,
                )
            )
            values.append(v)
            grads.append(dwf)
        conv = dot(tap_ref[kind], jnp.concatenate(taps, axis=1))
        for member in range(2):
            piece = dvs[member][:QROWS] + conv[:, member * HALF : (member + 1) * HALF]
            dqkvw_scr[2 * pair + member, :QROWS, 2 * HALF :] = piece.astype(BF)
        both = jnp.concatenate(values, axis=1)
        grad = jnp.concatenate(grads, axis=1)
        for tap in range(9):
            moved = dot(rows_ref[kind, tap], both)
            kern_ref[kind, tap] += fold(moved * grad)
        return carry

    lax.fori_loop(0, PAIRS, one_pair, 0)

    for branch in range(2):
        for crop in range(2):
            low, high = BLOCKS[crop]
            at = 4 * branch + 2 * crop
            rows = dqkvw_scr[at : at + 2].reshape(2 * WIN, 3 * HALF)
            dqkvf_scr[branch, low:high, :] += dot_tn(crops[crop][branch][...], rows)
        for group in range(3):
            low, high = BLOCKS[2 + group]
            dqkvf_scr[branch, low:high, :] += dot_tn(
                groups[group][...], dqkvw_scr[8 + 2 * group + branch]
            )
    for part in range(3):
        for branch in range(2):
            value = dqkvf_scr[branch, :, part * HALF : (part + 1) * HALF]
            lanes = slice(part * D + branch * HALF, part * D + (branch + 1) * HALF)
            sums_ref[:, lanes] += fold(value)
            dqkv_ref[0, :, lanes] = value.astype(BF)
    g_ref[...] += dot_tn(a_ref[0], dqkv_ref[0])


def input_kernel(x_ref, dqkv_ref, dx_ref, w_ref, s_ref, out_ref, sums_ref):
    @pl.when(pl.program_id(0) == 0)
    def _():
        sums_ref[...] = jnp.zeros_like(sums_ref)

    for low, high in CHUNKS:
        dh = dot_nt(dqkv_ref[0, low:high, :], w_ref[...])
        hat, scale = normalise(rows_of(x_ref, low, high))
        sums_ref[0] += fold(dh * hat)
        sums_ref[1] += fold(dh)
        grad = rows_of(dx_ref, low, high) + norm_back(dh * s_ref[0:1, :], hat, scale)
        store_rows(out_ref, low, high, grad)


def whole(shape):
    return pl.BlockSpec(shape, lambda i, *_: (0,) * len(shape))


def image_of(shape):
    return pl.BlockSpec((1,) + shape, lambda i, *_: (i,) + (0,) * len(shape))


def tokens():
    return pl.BlockSpec((TOK_IMG, D), lambda i, *_: (i, 0))


def params():
    return pltpu.CompilerParams(
        vmem_limit_bytes=VMEM, dimension_semantics=("arbitrary",)
    )


def sds(shape, dtype):
    return jax.ShapeDtypeStruct(shape, dtype)


def small_tables(small):
    rows = small.reshape(-1, D)
    taps = rows[5:15].reshape(10, 2, HALF).transpose(1, 0, 2)
    return jnp.pad(rows, ((0, 1), (0, 0))), jnp.pad(taps, ((0, 0), (0, 6), (0, 0)))


def matrices():
    selects = [bf(select_matrix(b, br)) for b in range(2) for br in range(2)]
    selects += [bf(select_matrix(2 + g, 0)) for g in range(3)]
    taps = np.stack([tap_matrix(kind) for kind in range(3)])
    side = bf(taps.transpose(0, 2, 1, 3).reshape(3, QROWS, 9 * WIN))
    return selects, side, bf(taps)


def run_attend(tokens_in, w_qkv, table, kernels, selects, side):
    images = tokens_in.shape[0] // TOK_IMG
    mrow, mkey = mask_operands()
    consts = [table, kernels, *selects, side, bf(mrow), bf(mkey)]
    outs = [
        ((ROWS, D), BF),
        ((ROWS, D), BF),
        ((2 * PAIRS, WIN, 3 * HALF), BF),
        ((2 * PAIRS, QROWS, HEADS * WIN), BF),
        ((2 * PAIRS, QROWS, HALF), F32),
        ((2 * PAIRS, QROWS, HALF), BF),
    ]
    return pl.pallas_call(
        attend_kernel,
        grid=(images,),
        in_specs=[tokens(), whole(w_qkv.shape)] + [whole(c.shape) for c in consts],
        out_specs=[image_of(shape) for shape, _ in outs],
        out_shape=[sds((images,) + shape, dtype) for shape, dtype in outs],
        scratch_shapes=[
            pltpu.VMEM((2, ROWS, 3 * HALF), BF),
            pltpu.VMEM((2 * PAIRS, WIN, HALF), BF),
            pltpu.VMEM((ROWS, D), F32),
        ],
        compiler_params=params(),
        name="attend",
    )(tokens_in, w_qkv, *consts)


def run_feed(counts, tokens_in, cotangent, att, wide, down, table):
    images = tokens_in.shape[0] // TOK_IMG
    return pl.pallas_call(
        feed_kernel,
        grid_spec=pltpu.PrefetchScalarGridSpec(
            num_scalar_prefetch=1,
            grid=(images,),
            in_specs=[
                tokens(),
                tokens(),
                image_of((ROWS, D)),
                whole(wide.shape),
                whole(down.shape),
                whole(table.shape),
            ],
            out_specs=[
                tokens(),
                tokens(),
                image_of((ROWS, D)),
                whole((D, FF)),
                whole((D, FF)),
                whole((D, D)),
                whole((5, 8, D)),
                whole((8, FF)),
            ],
            scratch_shapes=[
                pltpu.VMEM((ROWS, D), BF),
                pltpu.VMEM((ROWS, FF), F32),
                pltpu.VMEM((ROWS, FF), F32),
                pltpu.VMEM((ROWS, FF), BF),
                pltpu.VMEM((ROWS, FF), BF),
                pltpu.VMEM((ROWS, D), BF),
                pltpu.VMEM((ROWS, D), BF),
                pltpu.VMEM((ROWS, D), F32),
            ],
        ),
        out_shape=[
            sds(tokens_in.shape, F32),
            sds(tokens_in.shape, F32),
            sds((images, ROWS, D), BF),
            sds((D, FF), F32),
            sds((D, FF), F32),
            sds((D, D), F32),
            sds((5, 8, D), F32),
            sds((8, FF), F32),
        ],
        compiler_params=params(),
        name="feed",
    )(counts, tokens_in, cotangent, att, wide, down, table)


def run_back(datt, win, e, il, o, a, kernels, selects, side, taps):
    images = datt.shape[0]
    consts = [kernels, *selects, side, taps]
    blocks = [datt, win, e, il, o, a]
    return pl.pallas_call(
        back_kernel,
        grid=(images,),
        in_specs=[image_of(b.shape[1:]) for b in blocks] + [whole(c.shape) for c in consts],
        out_specs=[
            image_of((ROWS, 3 * D)),
            whole((D, 3 * D)),
            whole((3, 9, 8, D)),
            whole((8, 3 * D)),
        ],
        out_shape=[
            sds((images, ROWS, 3 * D), BF),
            sds((D, 3 * D), F32),
            sds((3, 9, 8, D), F32),
            sds((8, 3 * D), F32),
        ],
        scratch_shapes=[
            pltpu.VMEM((2 * PAIRS, WIN, HALF), BF),
            pltpu.VMEM((2 * PAIRS, WIN, 3 * HALF), BF),
            pltpu.VMEM((2, ROWS, 3 * HALF), F32),
        ],
        compiler_params=params(),
        name="back",
    )(*blocks, *consts)


def run_input(tokens_in, dqkv, dx, w_qkv, table):
    images = dqkv.shape[0]
    return pl.pallas_call(
        input_kernel,
        grid=(images,),
        in_specs=[
            tokens(),
            image_of((ROWS, 3 * D)),
            tokens(),
            whole(w_qkv.shape),
            whole(table.shape),
        ],
        out_specs=[tokens(), whole((2, 8, D))],
        out_shape=[sds(tokens_in.shape, F32), sds((2, 8, D), F32)],
        compiler_params=params(),
        name="input_grad",
    )(tokens_in, dqkv, dx, w_qkv, table)


def moments(grad, first, second):
    first_new = BETA_ONE * first + (1.0 - BETA_ONE) * grad
    second_new = BETA_TWO * second + (1.0 - BETA_TWO) * grad * grad
    direction = (
        first_new
        / (1.0 - BETA_ONE**STEP)
        / (jnp.sqrt(second_new / (1.0 - BETA_TWO**STEP)) + ADAM_EPS)
    )
    return (first_new, second_new, direction)


def matrix_squares(wide, down):
    column_sq = jnp.sum(wide * wide, axis=0)
    return jnp.stack(
        [
            jnp.sum(column_sq[: 3 * D]),
            jnp.sum(column_sq[3 * D : 4 * D]),
            jnp.sum(column_sq[4 * D :]),
            jnp.sum(down * down),
        ]
    )


def on_device(
    tokens_in,
    cotangent,
    crop_count,
    wide_w,
    wide_m,
    wide_v,
    wide_ema,
    down_w,
    down_m,
    down_v,
    down_ema,
    small_p,
    small_m,
    small_v,
    small_ema,
):
    weight_sq = matrix_squares(wide_w, down_w)
    wide_all = lax.all_gather(wide_w.astype(BF), "fsdp", axis=0, tiled=True)
    down_all = lax.all_gather(down_w.astype(BF), "fsdp", axis=0, tiled=True)
    small_all = lax.all_gather(small_p.astype(BF), "fsdp", axis=0, tiled=True)
    table, kernels = small_tables(small_all.astype(F32))
    w_qkv = wide_all[:, : 3 * D]
    selects, side, taps = matrices()
    a, att, win, e, il, o = run_attend(tokens_in, w_qkv, table, kernels, selects, side)
    block_out, dx, datt, g_up, g_down_t, g_out, sums, b_up = run_feed(
        crop_count, tokens_in, cotangent, att, wide_all, down_all, table
    )
    dqkv, g_qkv, kern, b_qkv = run_back(datt, win, e, il, o, a, kernels, selects, side, taps)
    grad_in, sums_in = run_input(tokens_in, dqkv, dx, w_qkv, table)
    sums = jnp.sum(sums, axis=1)
    sums_in = jnp.sum(sums_in, axis=1)
    kern = jnp.sum(kern, axis=2)
    side_h = kern[0, :, :HALF] + kern[0, :, HALF:] + kern[2, :, :HALF]
    side_v = kern[1, :, :HALF] + kern[1, :, HALF:] + kern[2, :, HALF:]
    small_terms = jnp.concatenate(
        [
            sums_in[0],
            sums_in[1],
            jnp.sum(b_qkv, axis=0),
            jnp.concatenate([side_h, side_v], axis=1).reshape(-1),
            sums[4],
            sums[3],
            sums[1],
            sums[2],
            jnp.sum(b_up, axis=0),
            sums[0],
        ]
    )
    wide_terms = jnp.concatenate([g_qkv, g_out, g_up], axis=1)
    shard_wide, shard_down, shard_small = (
        lax.psum_scatter(wide_terms, "fsdp", scatter_dimension=0, tiled=True),
        lax.psum_scatter(g_down_t.T, "fsdp", scatter_dimension=0, tiled=True),
        lax.psum_scatter(small_terms, "fsdp", scatter_dimension=0, tiled=True),
    )
    shard_wide, shard_down, shard_small = lax.psum((shard_wide, shard_down, shard_small), "dp")
    wide_first, wide_second, wide_dir = moments(shard_wide, wide_m, wide_v)
    down_first, down_second, down_dir = moments(shard_down, down_m, down_v)
    small_first, small_second, small_dir = moments(shard_small, small_m, small_v)
    wide_upd = wide_dir + DECAY * wide_w
    down_upd = down_dir + DECAY * down_w
    update_sq = matrix_squares(wide_upd, down_upd)
    weight_total, update_total = lax.psum((weight_sq, update_sq), "fsdp")
    weight_norm = jnp.sqrt(weight_total)
    update_norm = jnp.sqrt(update_total)
    ratio = weight_norm / update_norm
    column_ratio = jnp.concatenate(
        [
            ratio[0] * jnp.ones((3 * D,), jnp.float32),
            ratio[1] * jnp.ones((D,), jnp.float32),
            ratio[2] * jnp.ones((FF,), jnp.float32),
        ]
    )
    wide_new = wide_w - RATE * column_ratio * wide_upd
    down_new = down_w - RATE * ratio[3] * down_upd
    small_new = small_p - RATE * small_dir
    ema_keep = min(EMA_CEILING, (1.0 + STEP) / (10.0 + STEP))
    wide_avg = ema_keep * wide_ema + (1.0 - ema_keep) * wide_new
    down_avg = ema_keep * down_ema + (1.0 - ema_keep) * down_new
    small_avg = ema_keep * small_ema + (1.0 - ema_keep) * small_new
    norms = jnp.stack([weight_norm, update_norm])
    return (
        block_out,
        grad_in,
        wide_new,
        wide_first,
        wide_second,
        wide_avg,
        down_new,
        down_first,
        down_second,
        down_avg,
        small_new,
        small_first,
        small_second,
        small_avg,
        norms,
    )


def solution(mesh):
    tok, row, vec = P(("dp", "fsdp"), None), P("fsdp", None), P("fsdp")
    in_specs = (tok, tok, P(("dp", "fsdp"))) + (row,) * 8 + (vec,) * 4
    out_specs = (tok, tok) + (row,) * 8 + (vec,) * 4 + (P(),)
    return jax.shard_map(
        on_device, mesh=mesh, in_specs=in_specs, out_specs=out_specs, check_vma=False
    )
```

```python
import functools

import jax
import jax.numpy as jnp
import numpy as np
from jax import lax
from jax.experimental import pallas as pl
from jax.experimental.pallas import tpu as pltpu
from jax.sharding import PartitionSpec as P

D = 256
FF = 1024
HEAD = 32
STRIPE = 7
GRID_L = 14
GRID_S = 6
SMALL = 8
STEP = 10
TOK_IMG = 680

EPSILON = 1e-05
BETA_ONE = 0.9
BETA_TWO = 0.999
ADAM_EPS = 1e-06
DECAY = 0.05
RATE = 0.25
EMA_CEILING = 0.9999

ROWS = 688
BIG = 2 * GRID_L * GRID_L
PAIRS = 7
WIN = 128
QROWS = 112
HALF = 128
HEADS = 4
SCALE = HEAD**-0.5
LOG2E = 1.4426950408889634
LN2 = 0.6931471805599453
CHUNKS = ((0, 176), (176, 352), (352, 528), (528, 688))
BLOCKS = ((0, 208), (192, 400), (384, 512), (496, 608), (608, 688))
FIRST = (0, 196, 392, 500, 608)
GROUP = (3, 3, 2)
VMEM = 62 * 1024 * 1024

BF = jnp.bfloat16
F32 = jnp.float32


def window_tokens(block, branch):
    if block < 2:
        index = np.full((2, WIN), -1)
        for window in range(2):
            for r in range(GRID_L):
                for c in range(GRID_L):
                    if branch == 0:
                        w, at = divmod(r * GRID_L + c, STRIPE * GRID_L)
                    else:
                        w, at = c // STRIPE, r * STRIPE + c % STRIPE
                    index[w, at] = FIRST[block] + r * GRID_L + c
        return index.reshape(-1)
    count = GROUP[block - 2] * GRID_S * GRID_S
    index = np.full((WIN,), -1)
    index[:count] = FIRST[block] + np.arange(count)
    return index


def select_matrix(block, branch):
    low, high = BLOCKS[block]
    index = window_tokens(block, branch)
    return (index[:, None] == np.arange(low, high)[None, :]).astype(np.float32)


def tap_matrix(kind):
    shape = ((STRIPE, GRID_L), (GRID_L, STRIPE), (GRID_S, GRID_S))[kind]
    copies = (1, 1, 3)[kind]
    size = shape[0] * shape[1]
    out = np.zeros((9, QROWS, WIN), np.float32)
    for copy in range(copies):
        for r in range(shape[0]):
            for c in range(shape[1]):
                for tap in range(9):
                    rr, cc = r + tap // 3 - 1, c + tap % 3 - 1
                    if 0 <= rr < shape[0] and 0 <= cc < shape[1]:
                        out[tap, copy * size + r * shape[1] + c, copy * size + rr * shape[1] + cc] = 1
    return out


def mask_operands():
    size = GRID_S * GRID_S
    rows = np.zeros((3, QROWS, HALF), np.float32)
    keys = np.zeros((3, WIN, HALF), np.float32)
    rows[0, :, 0] = 1
    keys[0, STRIPE * GRID_L :, 0] = -1e30
    for kind, crops in ((1, 3), (2, 2)):
        for at in range(QROWS):
            rows[kind, at, at // size if at < crops * size else 0] = 1
        for at in range(WIN):
            for crop in range(crops):
                if at >= crops * size or at // size != crop:
                    keys[kind, at, crop] = -1e30
    return rows, np.tile(keys, (1, HEADS, 1))


def bf(array):
    return jnp.asarray(array, BF)


def dot(left, right):
    return jnp.dot(left, right, preferred_element_type=F32)


def dot_nt(left, right):
    return lax.dot_general(left, right, (((1,), (1,)), ((), ())), preferred_element_type=F32)


def dot_tn(left, right):
    return lax.dot_general(left, right, (((0,), (0,)), ((), ())), preferred_element_type=F32)


def normalise(values):
    center = values - jnp.mean(values, axis=-1, keepdims=True)
    spread = jnp.mean(center * center, axis=-1, keepdims=True)
    scale = lax.rsqrt(spread + EPSILON)
    return center * scale, scale


def norm_back(grad_hat, hat, scale):
    mean_grad = jnp.mean(grad_hat, axis=-1, keepdims=True)
    mean_dot = jnp.mean(grad_hat * hat, axis=-1, keepdims=True)
    return scale * (grad_hat - mean_grad - hat * mean_dot)


def rows_of(ref, low, high):
    if high <= TOK_IMG:
        return ref[low:high, :]
    tail = jnp.zeros((high - TOK_IMG, ref.shape[1]), F32)
    return jnp.concatenate([ref[low:TOK_IMG, :], tail], axis=0)


def store_rows(ref, low, high, values):
    last = min(high, TOK_IMG)
    ref[low:last, :] = values[: last - low]


def fold(values):
    return jnp.sum(values.reshape(values.shape[0] // 8, 8, values.shape[1]), axis=0)


def head_lanes(head):
    lanes = lax.broadcasted_iota(jnp.int32, (1, HALF), 1)
    return jnp.where(lanes // HEAD == head, 1.0, 0.0).astype(BF)


def by_head(values):
    return jnp.concatenate([values * head_lanes(h) for h in range(HEADS)], axis=0)


def head_block(rows):
    return jnp.concatenate(
        [jnp.broadcast_to(head_lanes(h), (rows, HALF)) for h in range(HEADS)], axis=0
    )


def attend_kernel(
    x_ref,
    w_ref,
    s_ref,
    k_ref,
    p0h_ref,
    p0v_ref,
    p1h_ref,
    p1v_ref,
    pg0_ref,
    pg1_ref,
    pg2_ref,
    tap_ref,
    mrow_ref,
    mkey_ref,
    a_ref,
    att_ref,
    win_ref,
    e_ref,
    il_ref,
    o_ref,
    qkv_scr,
    attw_scr,
    attf_scr,
):
    gain, shift = s_ref[0:1, :], s_ref[1:2, :]
    for low, high in CHUNKS:
        hat, _ = normalise(rows_of(x_ref, low, high))
        a = (hat * gain + shift).astype(BF)
        a_ref[0, low:high, :] = a
        qkv = dot(a, w_ref[...])
        for part in range(3):
            piece = qkv[:, part * D : (part + 1) * D] + s_ref[2 + part : 3 + part, :]
            if part == 0:
                piece = piece * (SCALE * LOG2E)
            piece = piece.astype(BF)
            for branch in range(2):
                qkv_scr[branch, low:high, part * HALF : (part + 1) * HALF] = piece[
                    :, branch * HALF : (branch + 1) * HALF
                ]
    attf_scr[...] = jnp.zeros_like(attf_scr)
    attw_scr[...] = jnp.zeros_like(attw_scr)
    crops = ((p0h_ref, p0v_ref), (p1h_ref, p1v_ref))
    groups = (pg0_ref, pg1_ref, pg2_ref)
    for branch in range(2):
        for crop in range(2):
            low, high = BLOCKS[crop]
            got = dot(crops[crop][branch][...], qkv_scr[branch, low:high, :]).astype(BF)
            at = 4 * branch + 2 * crop
            win_ref[0, at] = got[:WIN]
            win_ref[0, at + 1] = got[WIN:]
        for group in range(3):
            low, high = BLOCKS[2 + group]
            got = dot(groups[group][...], qkv_scr[branch, low:high, :]).astype(BF)
            win_ref[0, 8 + 2 * group + branch] = got

    ones = head_block(WIN)

    def one_pair(pair, carry):
        kind = jnp.minimum(pair // 2, 2)
        mask_kind = jnp.maximum(pair - 4, 0)
        mask_kind = jnp.where(pair < 4, 0, jnp.where(pair < 6, 1, 2))
        taps = []
        mixed = []
        for member in range(2):
            at = 2 * pair + member
            branch = jnp.where(pair < 2, 0, jnp.where(pair < 4, 1, member))
            q = win_ref[0, at, :QROWS, 0:HALF]
            k = win_ref[0, at, :, HALF : 2 * HALF]
            v = win_ref[0, at, :, 2 * HALF :]
            left = jnp.concatenate([q, mrow_ref[mask_kind]], axis=1)
            right = jnp.concatenate([by_head(k), mkey_ref[mask_kind]], axis=1)
            scores = dot_nt(left, right)
            exps = []
            for h in range(HEADS):
                part = scores[:, h * WIN : (h + 1) * WIN]
                peak = jnp.max(part, axis=-1, keepdims=True)
                exps.append(jnp.exp2(part - peak).astype(BF))
            e = jnp.concatenate(exps, axis=1)
            e_ref[0, at] = e
            both = dot(e, jnp.concatenate([by_head(v), ones], axis=1))
            inv = 1.0 / both[:, HALF:]
            o = both[:, :HALF] * inv
            il_ref[0, at] = inv
            o_ref[0, at] = o.astype(BF)
            kernel = k_ref[branch]
            mixed.append(o + kernel[9:10])
            taps.append(
                jnp.concatenate(
                    [
                        v * kernel[tap : tap + 1].astype(BF) for tap in range(9)
                    ],
                    axis=0,
                )
            )
        conv = dot(tap_ref[kind], jnp.concatenate(taps, axis=1))
        for member in range(2):
            piece = mixed[member] + conv[:, member * HALF : (member + 1) * HALF]
            attw_scr[2 * pair + member, :QROWS, :] = piece.astype(BF)
        return carry

    lax.fori_loop(0, PAIRS, one_pair, 0)

    for branch in range(2):
        lanes = slice(branch * HALF, (branch + 1) * HALF)
        for crop in range(2):
            low, high = BLOCKS[crop]
            at = 4 * branch + 2 * crop
            rows = attw_scr[at : at + 2].reshape(2 * WIN, HALF)
            attf_scr[low:high, lanes] += dot_tn(crops[crop][branch][...], rows)
        for group in range(3):
            low, high = BLOCKS[2 + group]
            attf_scr[low:high, lanes] += dot_tn(
                groups[group][...], attw_scr[8 + 2 * group + branch]
            )
    att_ref[0] = attf_scr[...].astype(BF)


def gelu_parts(u):
    size = jnp.abs(u)
    t = 1.0 / (1.0 + (0.3275911 * 2**-0.5) * size)
    decay = jnp.exp2((-0.5 * LOG2E) * (u * u))
    poly = 0.5 * 1.061405429
    for term in (-1.453152027, 1.421413741, -0.284496736, 0.254829592):
        poly = poly * t + 0.5 * term
    tail = poly * t * decay
    phi = jnp.where(u >= 0, 1.0 - tail, tail)
    slope = phi + (u * 0.3989422804014327) * decay
    return phi, slope


def feed_kernel(
    cnt_ref,
    x_ref,
    c_ref,
    att_ref,
    w_ref,
    down_ref,
    s_ref,
    out_ref,
    dx_ref,
    datt_ref,
    glate_ref,
    gdn_ref,
    sums_ref,
    bup_ref,
    h2_scr,
    u_scr,
    dg_scr,
    g_scr,
    du_scr,
    dy_scr,
    dz_scr,
    x1_scr,
    gup_scr,
    gdn_scr,
    gout_scr,
):
    image = pl.program_id(0)

    @pl.when(image == 0)
    def _():
        for ref in (gup_scr, gdn_scr, gout_scr, sums_ref, bup_ref):
            ref[...] = jnp.zeros_like(ref)

    bound = BIG + GRID_S * GRID_S * cnt_ref[image]
    bias_out, gain, shift = s_ref[15:16, :], s_ref[16:17, :], s_ref[17:18, :]
    w_out, w_up = w_ref[:, :D], w_ref[:, D : D + FF]
    for low, high in CHUNKS:
        att = att_ref[0, low:high, :]
        x1 = rows_of(x_ref, low, high) + dot(att, w_out) + bias_out
        x1_scr[low:high, :] = x1
        hat, scale = normalise(x1)
        h2 = (hat * gain + shift).astype(BF)
        h2_scr[low:high, :] = h2
        u_scr[low:high, :] = dot(h2, w_up)
        row = low + lax.broadcasted_iota(jnp.int32, (high - low, 1), 0)
        dy = jnp.where(row < bound, rows_of(c_ref, low, high), 0.0)
        dyr = dy.astype(BF)
        dy_scr[low:high, :] = dyr
        sums_ref[0] += fold(dyr.astype(F32))
        dg_scr[low:high, :] = dot_nt(dyr, down_ref[...])
        for part in range(4):
            lanes = slice(part * D, (part + 1) * D)
            bias = s_ref[18 + part : 19 + part, :]
            total = jnp.zeros((8, D), F32)
            for at in range(low, high, 16):
                u = u_scr[at : at + 16, lanes] + bias
                phi, slope = gelu_parts(u)
                g_scr[at : at + 16, lanes] = (u * phi).astype(BF)
                du = dg_scr[at : at + 16, lanes] * slope
                total = total + fold(du)
                du_scr[at : at + 16, lanes] = du.astype(BF)
            bup_ref[:, lanes] += total
        block = x1_scr[low:high, :] + dot(g_scr[low:high, :], down_ref[...]) + s_ref[22:23, :]
        store_rows(out_ref, low, high, block)
        dh2 = dot_nt(du_scr[low:high, :], w_up)
        hat, scale = normalise(x1_scr[low:high, :])
        sums_ref[1] += fold(dh2 * hat)
        sums_ref[2] += fold(dh2)
        row = low + lax.broadcasted_iota(jnp.int32, (high - low, 1), 0)
        dy = jnp.where(row < bound, rows_of(c_ref, low, high), 0.0)
        dx = dy + norm_back(dh2 * gain, hat, scale)
        store_rows(dx_ref, low, high, dx)
        dz = dx.astype(BF)
        dz_scr[low:high, :] = dz
        sums_ref[3] += fold(dz.astype(F32))
        datt = dot_nt(dz, w_out)
        sums_ref[4] += fold(datt)
        datt_ref[0, low:high, :] = datt.astype(BF)
    gup_scr[...] += dot_tn(h2_scr[...], du_scr[...])
    gdn_scr[...] += dot_tn(dy_scr[...], g_scr[...])
    gout_scr[...] += dot_tn(att_ref[0], dz_scr[...])

    @pl.when(image == pl.num_programs(0) - 1)
    def _():
        gdn_ref[...] = gdn_scr[...].T.astype(BF)
        glate_ref[:, :D] = gout_scr[...].astype(BF)
        glate_ref[:, D:] = gup_scr[...].astype(BF)


def back_kernel(
    datt_ref,
    win_ref,
    e_ref,
    il_ref,
    o_ref,
    a_ref,
    x_ref,
    dx_ref,
    w_ref,
    s_ref,
    k_ref,
    p0h_ref,
    p0v_ref,
    p1h_ref,
    p1v_ref,
    pg0_ref,
    pg1_ref,
    pg2_ref,
    tap_ref,
    rows_ref,
    out_ref,
    g_ref,
    kern_ref,
    bias_ref,
    sums_ref,
    dw_scr,
    dqkvw_scr,
    dqkvf_scr,
    dqkv_scr,
):
    image = pl.program_id(0)

    @pl.when(image == 0)
    def _():
        for ref in (g_ref, kern_ref, bias_ref, sums_ref):
            ref[...] = jnp.zeros_like(ref)

    crops = ((p0h_ref, p0v_ref), (p1h_ref, p1v_ref))
    groups = (pg0_ref, pg1_ref, pg2_ref)
    for branch in range(2):
        lanes = slice(branch * HALF, (branch + 1) * HALF)
        for crop in range(2):
            low, high = BLOCKS[crop]
            got = dot(crops[crop][branch][...], datt_ref[0, low:high, lanes]).astype(BF)
            at = 4 * branch + 2 * crop
            dw_scr[at] = got[:WIN]
            dw_scr[at + 1] = got[WIN:]
        for group in range(3):
            low, high = BLOCKS[2 + group]
            got = dot(groups[group][...], datt_ref[0, low:high, lanes]).astype(BF)
            dw_scr[8 + 2 * group + branch] = got
    dqkvw_scr[...] = jnp.zeros_like(dqkvw_scr)
    dqkvf_scr[...] = jnp.zeros_like(dqkvf_scr)
    minus = -head_block(WIN)

    def one_pair(pair, carry):
        kind = jnp.minimum(pair // 2, 2)
        taps, values, grads, dvs = [], [], [], []
        for member in range(2):
            at = 2 * pair + member
            branch = jnp.where(pair < 2, 0, jnp.where(pair < 4, 1, member))
            q = win_ref[0, at, :QROWS, 0:HALF]
            k = win_ref[0, at, :, HALF : 2 * HALF]
            v = win_ref[0, at, :, 2 * HALF :]
            dwin = dw_scr[at]
            dwf = dwin[:QROWS].astype(F32)
            dn = dwf * il_ref[0, at]
            z = (dn * o_ref[0, at].astype(F32)).astype(BF)
            dn = dn.astype(BF)
            left = jnp.concatenate([dn, z], axis=1)
            right = jnp.concatenate([by_head(v), minus], axis=1)
            ds = (dot_nt(left, right) * e_ref[0, at].astype(F32)).astype(BF)
            dq = dot(ds, by_head(k)) * SCALE
            dqkvw_scr[at, :QROWS, 0:HALF] = dq.astype(BF)
            dks, dvt = [], []
            for h in range(HEADS):
                lanes = slice(h * WIN, (h + 1) * WIN)
                own = slice(h * HEAD, (h + 1) * HEAD)
                dks.append(dot_tn(q, ds[:, lanes])[own])
                dvt.append(dot_tn(dn, e_ref[0, at, :, lanes])[own])
            dk = jnp.concatenate(dks, axis=0).T * LN2
            dqkvw_scr[at, :, HALF : 2 * HALF] = dk.astype(BF)
            dvs.append(jnp.concatenate(dvt, axis=0).T)
            kernel = k_ref[branch]
            taps.append(
                jnp.concatenate(
                    [
                        dwin * kernel[8 - tap : 9 - tap].astype(BF) for tap in range(9)
                    ],
                    axis=0,
                )
            )
            values.append(v)
            grads.append(dwf)
        conv = dot(tap_ref[kind], jnp.concatenate(taps, axis=1))
        for member in range(2):
            piece = dvs[member][:QROWS] + conv[:, member * HALF : (member + 1) * HALF]
            dqkvw_scr[2 * pair + member, :QROWS, 2 * HALF :] = piece.astype(BF)
        both = jnp.concatenate(values, axis=1)
        grad = jnp.concatenate(grads, axis=1)
        for tap in range(9):
            moved = dot(rows_ref[kind, tap], both)
            kern_ref[kind, tap] += fold(moved * grad)
        return carry

    lax.fori_loop(0, PAIRS, one_pair, 0)

    for branch in range(2):
        for crop in range(2):
            low, high = BLOCKS[crop]
            at = 4 * branch + 2 * crop
            rows = dqkvw_scr[at : at + 2].reshape(2 * WIN, 3 * HALF)
            dqkvf_scr[branch, low:high, :] += dot_tn(crops[crop][branch][...], rows)
        for group in range(3):
            low, high = BLOCKS[2 + group]
            dqkvf_scr[branch, low:high, :] += dot_tn(
                groups[group][...], dqkvw_scr[8 + 2 * group + branch]
            )
    for part in range(3):
        for branch in range(2):
            value = dqkvf_scr[branch, :, part * HALF : (part + 1) * HALF]
            lanes = slice(part * D + branch * HALF, part * D + (branch + 1) * HALF)
            bias_ref[:, lanes] += fold(value)
            dqkv_scr[:, lanes] = value.astype(BF)
    g_ref[...] += dot_tn(a_ref[0], dqkv_scr[...])
    for low, high in CHUNKS:
        dh = dot_nt(dqkv_scr[low:high, :], w_ref[...])
        hat, scale = normalise(rows_of(x_ref, low, high))
        sums_ref[0] += fold(dh * hat)
        sums_ref[1] += fold(dh)
        grad = rows_of(dx_ref, low, high) + norm_back(dh * s_ref[0:1, :], hat, scale)
        store_rows(out_ref, low, high, grad)


def whole(shape):
    return pl.BlockSpec(shape, lambda i, *_: (0,) * len(shape))


def image_of(shape):
    return pl.BlockSpec((1,) + shape, lambda i, *_: (i,) + (0,) * len(shape))


def tokens():
    return pl.BlockSpec((TOK_IMG, D), lambda i, *_: (i, 0))


def params():
    return pltpu.CompilerParams(
        vmem_limit_bytes=VMEM, dimension_semantics=("arbitrary",)
    )


def sds(shape, dtype):
    return jax.ShapeDtypeStruct(shape, dtype)


def small_tables(small):
    rows = small.reshape(-1, D)
    taps = rows[5:15].reshape(10, 2, HALF).transpose(1, 0, 2)
    return jnp.pad(rows, ((0, 1), (0, 0))), jnp.pad(taps, ((0, 0), (0, 6), (0, 0)))


def matrices():
    selects = [bf(select_matrix(b, br)) for b in range(2) for br in range(2)]
    selects += [bf(select_matrix(2 + g, 0)) for g in range(3)]
    taps = np.stack([tap_matrix(kind) for kind in range(3)])
    side = bf(taps.transpose(0, 2, 1, 3).reshape(3, QROWS, 9 * WIN))
    return selects, side, bf(taps)


def run_attend(tokens_in, w_qkv, table, kernels, selects, side):
    images = tokens_in.shape[0] // TOK_IMG
    mrow, mkey = mask_operands()
    consts = [table, kernels, *selects, side, bf(mrow), bf(mkey)]
    outs = [
        ((ROWS, D), BF),
        ((ROWS, D), BF),
        ((2 * PAIRS, WIN, 3 * HALF), BF),
        ((2 * PAIRS, QROWS, HEADS * WIN), BF),
        ((2 * PAIRS, QROWS, HALF), F32),
        ((2 * PAIRS, QROWS, HALF), BF),
    ]
    return pl.pallas_call(
        attend_kernel,
        grid=(images,),
        in_specs=[tokens(), whole(w_qkv.shape)] + [whole(c.shape) for c in consts],
        out_specs=[image_of(shape) for shape, _ in outs],
        out_shape=[sds((images,) + shape, dtype) for shape, dtype in outs],
        scratch_shapes=[
            pltpu.VMEM((2, ROWS, 3 * HALF), BF),
            pltpu.VMEM((2 * PAIRS, WIN, HALF), BF),
            pltpu.VMEM((ROWS, D), F32),
        ],
        compiler_params=params(),
        name="attend",
    )(tokens_in, w_qkv, *consts)


def run_feed(counts, tokens_in, cotangent, att, wide, down, table):
    images = tokens_in.shape[0] // TOK_IMG
    return pl.pallas_call(
        feed_kernel,
        grid_spec=pltpu.PrefetchScalarGridSpec(
            num_scalar_prefetch=1,
            grid=(images,),
            in_specs=[
                tokens(),
                tokens(),
                image_of((ROWS, D)),
                whole(wide.shape),
                whole(down.shape),
                whole(table.shape),
            ],
            out_specs=[
                tokens(),
                tokens(),
                image_of((ROWS, D)),
                whole((D, D + FF)),
                whole((FF, D)),
                whole((5, 8, D)),
                whole((8, FF)),
            ],
            scratch_shapes=[
                pltpu.VMEM((ROWS, D), BF),
                pltpu.VMEM((ROWS, FF), F32),
                pltpu.VMEM((ROWS, FF), F32),
                pltpu.VMEM((ROWS, FF), BF),
                pltpu.VMEM((ROWS, FF), BF),
                pltpu.VMEM((ROWS, D), BF),
                pltpu.VMEM((ROWS, D), BF),
                pltpu.VMEM((ROWS, D), F32),
                pltpu.VMEM((D, FF), F32),
                pltpu.VMEM((D, FF), F32),
                pltpu.VMEM((D, D), F32),
            ],
        ),
        out_shape=[
            sds(tokens_in.shape, F32),
            sds(tokens_in.shape, F32),
            sds((images, ROWS, D), BF),
            sds((D, D + FF), BF),
            sds((FF, D), BF),
            sds((5, 8, D), F32),
            sds((8, FF), F32),
        ],
        compiler_params=params(),
        name="feed",
    )(counts, tokens_in, cotangent, att, wide, down, table)


def run_back(blocks, tokens_in, dx, w_qkv, table, kernels, selects, side, taps):
    images = blocks[0].shape[0]
    consts = [w_qkv, table, kernels, *selects, side, taps]
    outs = [(D, 3 * D), (3, 9, 8, D), (8, 3 * D), (2, 8, D)]
    return pl.pallas_call(
        back_kernel,
        grid=(images,),
        in_specs=[image_of(b.shape[1:]) for b in blocks]
        + [tokens(), tokens()]
        + [whole(c.shape) for c in consts],
        out_specs=[tokens()] + [whole(shape) for shape in outs],
        out_shape=[sds(tokens_in.shape, F32)] + [sds(shape, F32) for shape in outs],
        scratch_shapes=[
            pltpu.VMEM((2 * PAIRS, WIN, HALF), BF),
            pltpu.VMEM((2 * PAIRS, WIN, 3 * HALF), BF),
            pltpu.VMEM((2, ROWS, 3 * HALF), F32),
            pltpu.VMEM((ROWS, 3 * D), BF),
        ],
        compiler_params=params(),
        name="back",
    )(*blocks, tokens_in, dx, *consts)


def moments(grad, first, second):
    first_new = BETA_ONE * first + (1.0 - BETA_ONE) * grad
    second_new = BETA_TWO * second + (1.0 - BETA_TWO) * grad * grad
    direction = (
        first_new
        / (1.0 - BETA_ONE**STEP)
        / (jnp.sqrt(second_new / (1.0 - BETA_TWO**STEP)) + ADAM_EPS)
    )
    return (first_new, second_new, direction)


MATRICES = (slice(0, 3 * D), slice(3 * D, 4 * D), slice(4 * D, 4 * D + FF))


def lane_sums(values):
    column = jnp.sum(values * values, axis=0, keepdims=True)
    parts = [column[:, at : at + HALF] for at in range(0, column.shape[1], HALF)]
    return functools.reduce(jnp.add, parts)


def moment_kernel(
    gq_ref,
    gq_other_ref,
    gl_ref,
    gl_other_ref,
    ww_ref,
    wm_ref,
    wv_ref,
    dw_ref,
    dm_ref,
    dv_ref,
    wf_ref,
    ws_ref,
    wu_ref,
    df_ref,
    ds_ref,
    du_ref,
    sq_ref,
):
    for lanes, own, other in (
        (slice(0, 3 * D), gq_ref[:, : 3 * D], gq_other_ref[:, : 3 * D]),
        (slice(3 * D, 4 * D + FF), gl_ref[:, : D + FF], gl_other_ref[:, : D + FF]),
    ):
        first, second, way = moments(own + other, wm_ref[:, lanes], wv_ref[:, lanes])
        wf_ref[:, lanes] = first
        ws_ref[:, lanes] = second
        wu_ref[:, lanes] = way + DECAY * ww_ref[:, lanes]
    count = ww_ref.shape[0]
    for part in range(FF // D):
        lanes = slice(D + FF + part * D, D + FF + (part + 1) * D)
        own = slice(part * count, (part + 1) * count)
        grad = gl_ref[:, lanes] + gl_other_ref[:, lanes]
        first, second, way = moments(grad, dm_ref[own, :], dv_ref[own, :])
        df_ref[own, :] = first
        ds_ref[own, :] = second
        du_ref[own, :] = way + DECAY * dw_ref[own, :]
    for base, wide, down in ((0, ww_ref, dw_ref), (4, wu_ref, du_ref)):
        for at, lanes in enumerate(MATRICES):
            sq_ref[base + at : base + at + 1, :] = lane_sums(wide[:, lanes])
        sq_ref[base + 3 : base + 4, :] = lane_sums(down[...])


def update_kernel(
    sq_ref,
    ww_ref,
    wu_ref,
    we_ref,
    dw_ref,
    du_ref,
    de_ref,
    wn_ref,
    wa_ref,
    dn_ref,
    da_ref,
    norm_ref,
):
    total = jnp.sum(sq_ref[...], axis=1, keepdims=True)
    norm = jnp.sqrt(total)
    norm_ref[...] = jnp.broadcast_to(norm, norm_ref.shape)
    ratio = norm[0:4] / norm[4:8]
    keep = min(EMA_CEILING, (1.0 + STEP) / (10.0 + STEP))
    for at, lanes in enumerate(MATRICES):
        new = ww_ref[:, lanes] - (RATE * ratio[at : at + 1]) * wu_ref[:, lanes]
        wn_ref[:, lanes] = new
        wa_ref[:, lanes] = keep * we_ref[:, lanes] + (1.0 - keep) * new
    new = dw_ref[...] - (RATE * ratio[3:4]) * du_ref[...]
    dn_ref[...] = new
    da_ref[...] = keep * de_ref[...] + (1.0 - keep) * new


def plain(kernel, name, out_shape, *operands):
    return pl.pallas_call(kernel, out_shape=out_shape, compiler_params=pltpu.CompilerParams(
        vmem_limit_bytes=VMEM), name=name)(*operands)


def to_other(values):
    return lax.ppermute(values, "dp", [(0, 1), (1, 0)])


def side_by_side(wide, down):
    rows = wide.shape[0]
    blocks = [down[at : at + rows] for at in range(0, down.shape[0], rows)]
    return jnp.concatenate([wide] + blocks, axis=1)


def gather(values, count):
    copies = jnp.broadcast_to(values[None], (count,) + values.shape)
    return lax.all_to_all(copies, "fsdp", 0, 0).reshape(-1, values.shape[1])


def scatter_sum(values, count):
    terms = values.reshape(count, -1, values.shape[1])
    return jnp.sum(lax.all_to_all(terms, "fsdp", 0, 0).astype(F32), axis=0)


def add_all(values, count):
    step = 1
    while step < count:
        values = values + lax.ppermute(values, "fsdp", [(i, i ^ step) for i in range(count)])
        step *= 2
    return values


def on_device(
    count,
    tokens_in,
    cotangent,
    crop_count,
    wide_w,
    wide_m,
    wide_v,
    wide_ema,
    down_w,
    down_m,
    down_v,
    down_ema,
    small_p,
    small_m,
    small_v,
    small_ema,
):
    rows = wide_w.shape[0]
    narrow = small_p.shape[0] // rows
    wide_low = wide_w.astype(BF)
    small_low = jnp.pad(small_p.astype(BF).reshape(rows, narrow), ((0, 0), (0, HALF - narrow)))
    first = jnp.concatenate([wide_low[:, : 3 * D], small_low], axis=1)
    first = gather(first, count)
    late_all = gather(side_by_side(wide_low[:, 3 * D :], down_w.astype(BF)), count)
    down_all = late_all[:, D + FF :].reshape(count, rows, FF // D, D)
    down_all = down_all.transpose(0, 2, 1, 3).reshape(FF, D)
    w_qkv = first[:, : 3 * D]
    table, kernels = small_tables(first[:, 3 * D : 3 * D + narrow].astype(F32).reshape(-1))
    selects, side, taps = matrices()
    a, att, win, e, il, o = run_attend(tokens_in, w_qkv, table, kernels, selects, side)
    block_out, dx, datt, g_late, g_down, sums, b_up = run_feed(
        crop_count, tokens_in, cotangent, att, late_all, down_all, table
    )
    g_down = g_down.reshape(count, FF // D, rows, D).transpose(0, 2, 1, 3).reshape(D, FF)
    late = scatter_sum(jnp.concatenate([g_late, g_down], axis=1), count)
    grad_in, g_qkv, kern, b_qkv, sums_in = run_back(
        [datt, win, e, il, o, a], tokens_in, dx, w_qkv, table, kernels, selects, side, taps
    )
    sums = jnp.sum(sums, axis=1)
    sums_in = jnp.sum(sums_in, axis=1)
    kern = jnp.sum(kern, axis=2)
    side_h = kern[0, :, :HALF] + kern[0, :, HALF:] + kern[2, :, :HALF]
    side_v = kern[1, :, :HALF] + kern[1, :, HALF:] + kern[2, :, HALF:]
    small_terms = jnp.concatenate(
        [
            sums_in[0],
            sums_in[1],
            jnp.sum(b_qkv, axis=0),
            jnp.concatenate([side_h, side_v], axis=1).reshape(-1),
            sums[4],
            sums[3],
            sums[1],
            sums[2],
            jnp.sum(b_up, axis=0),
            sums[0],
        ]
    ).reshape(D, narrow)
    small_terms = jnp.pad(small_terms, ((0, 0), (0, HALF - narrow)))
    last = jnp.concatenate([g_qkv, small_terms], axis=1).astype(BF)
    last = scatter_sum(last, count)
    last_other = to_other(last)
    late_other = to_other(late)
    wide_like, down_like = sds(wide_w.shape, F32), sds(down_w.shape, F32)
    wide_first, wide_second, wide_upd, down_first, down_second, down_upd, squares = plain(
        moment_kernel,
        "moment",
        [wide_like] * 3 + [down_like] * 3 + [sds((8, HALF), F32)],
        *(last, last_other, late, late_other),
        *(wide_w, wide_m, wide_v, down_w, down_m, down_v),
    )
    squares = add_all(squares, count)
    wide_new, wide_avg, down_new, down_avg, norms = plain(
        update_kernel,
        "update",
        [wide_like] * 2 + [down_like] * 2 + [sds((8, HALF), F32)],
        *(squares, wide_w, wide_upd, wide_ema, down_w, down_upd, down_ema),
    )
    shard_small = (last + last_other)[:, 3 * D : 3 * D + narrow].reshape(-1)
    small_first, small_second, small_dir = moments(shard_small, small_m, small_v)
    small_new = small_p - RATE * small_dir
    ema_keep = min(EMA_CEILING, (1.0 + STEP) / (10.0 + STEP))
    small_avg = ema_keep * small_ema + (1.0 - ema_keep) * small_new
    return (
        block_out,
        grad_in,
        wide_new,
        wide_first,
        wide_second,
        wide_avg,
        down_new,
        down_first,
        down_second,
        down_avg,
        small_new,
        small_first,
        small_second,
        small_avg,
        norms[:, 0].reshape(2, 4),
    )


def solution(mesh):
    tok, row, vec = P(("dp", "fsdp"), None), P("fsdp", None), P("fsdp")
    in_specs = (tok, tok, P(("dp", "fsdp"))) + (row,) * 8 + (vec,) * 4
    out_specs = (tok, tok) + (row,) * 8 + (vec,) * 4 + (P(),)
    return jax.shard_map(
        functools.partial(on_device, mesh.shape["fsdp"]),
        mesh=mesh,
        in_specs=in_specs,
        out_specs=out_specs,
        check_vma=False,
    )
```

```python
import functools

import jax
import jax.numpy as jnp
import numpy as np
from jax import lax
from jax.experimental import pallas as pl
from jax.experimental.pallas import tpu as pltpu
from jax.sharding import PartitionSpec as P

D = 256
FF = 1024
HEAD = 32
STRIPE = 7
GRID_L = 14
GRID_S = 6
SMALL = 8
STEP = 10
TOK_IMG = 680

EPSILON = 1e-05
BETA_ONE = 0.9
BETA_TWO = 0.999
ADAM_EPS = 1e-06
DECAY = 0.05
RATE = 0.25
EMA_CEILING = 0.9999

ROWS = 688
BIG = 2 * GRID_L * GRID_L
PAIRS = 7
WIN = 128
QROWS = 112
HALF = 128
HEADS = 4
SCALE = HEAD**-0.5
LOG2E = 1.4426950408889634
LN2 = 0.6931471805599453
CHUNKS = ((0, 240), (240, 464), (464, 688))
LONG = 744
EDGE = 16
COPIES = (3, 3, 2)
TAPS = tuple((dy, dx) for dy in (-1, 0, 1) for dx in (-1, 0, 1))
ORDER = (0, 2, 1, 3, 4, 5, 6)
VMEM = 62 * 1024 * 1024

BF = jnp.bfloat16
F32 = jnp.float32


def kind_of(pair):
    return 0 if pair < 2 else 1 if pair < 4 else 2


def branch_of(pair, member):
    return 0 if pair < 2 else 1 if pair < 4 else member


def first_of(pair, member):
    if pair < 2:
        return pair * GRID_L * GRID_L + member * STRIPE * GRID_L
    if pair < 4:
        return (pair - 2) * GRID_L * GRID_L + member * STRIPE
    return BIG + (pair - 4) * COPIES[0] * GRID_S * GRID_S


def tokens_of(pair):
    return STRIPE * GRID_L if pair < 4 else COPIES[pair - 4] * GRID_S * GRID_S


def shape_of(kind):
    return ((STRIPE, GRID_L), (GRID_L, STRIPE), (GRID_S, GRID_S))[kind]


def edge_masks():
    out = np.zeros((3, 9, QROWS, HALF), np.float32)
    for kind in range(3):
        high, broad = shape_of(kind)
        size = high * broad
        for copy in range(1 if kind < 2 else COPIES[0]):
            for at in range(size):
                r, c = divmod(at, broad)
                for tap, (dy, dx) in enumerate(TAPS):
                    if 0 <= r + dy < high and 0 <= c + dx < broad:
                        out[kind, tap, copy * size + at] = 1
    return out


def tap_matrix(kind):
    shape = shape_of(kind)
    copies = 1 if kind < 2 else COPIES[0]
    size = shape[0] * shape[1]
    out = np.zeros((9, QROWS, WIN), np.float32)
    for copy in range(copies):
        for r in range(shape[0]):
            for c in range(shape[1]):
                for tap in range(9):
                    rr, cc = r + tap // 3 - 1, c + tap % 3 - 1
                    if 0 <= rr < shape[0] and 0 <= cc < shape[1]:
                        out[tap, copy * size + r * shape[1] + c, copy * size + rr * shape[1] + cc] = 1
    return out


def mask_operands():
    size = GRID_S * GRID_S
    rows = np.zeros((3, QROWS, HALF), np.float32)
    keys = np.zeros((3, WIN, HALF), np.float32)
    rows[0, :, 0] = 1
    keys[0, STRIPE * GRID_L :, 0] = -1e30
    for kind, crops in ((1, 3), (2, 2)):
        for at in range(QROWS):
            rows[kind, at, at // size if at < crops * size else 0] = 1
        for at in range(WIN):
            for crop in range(crops):
                if at >= crops * size or at // size != crop:
                    keys[kind, at, crop] = -1e30
    return rows, np.tile(keys, (1, HEADS, 1))


def bf(array):
    return jnp.asarray(array, BF)


def dot(left, right):
    return jnp.dot(left, right, preferred_element_type=F32)


def dot_nt(left, right):
    return lax.dot_general(left, right, (((1,), (1,)), ((), ())), preferred_element_type=F32)


def dot_tn(left, right):
    return lax.dot_general(left, right, (((0,), (0,)), ((), ())), preferred_element_type=F32)


def normalise(values):
    center = values - jnp.mean(values, axis=-1, keepdims=True)
    spread = jnp.mean(center * center, axis=-1, keepdims=True)
    scale = lax.rsqrt(spread + EPSILON)
    return center * scale, scale


def norm_back(grad_hat, hat, scale):
    mean_grad = jnp.mean(grad_hat, axis=-1, keepdims=True)
    mean_dot = jnp.mean(grad_hat * hat, axis=-1, keepdims=True)
    return scale * (grad_hat - mean_grad - hat * mean_dot)


def rows_of(ref, low, high):
    if high <= TOK_IMG:
        return ref[low:high, :]
    tail = jnp.zeros((high - TOK_IMG, ref.shape[1]), F32)
    return jnp.concatenate([ref[low:TOK_IMG, :], tail], axis=0)


def store_rows(ref, low, high, values):
    last = min(high, TOK_IMG)
    ref[low:last, :] = values[: last - low]


def fold(values):
    return jnp.sum(values.reshape(values.shape[0] // 8, 8, values.shape[1]), axis=0)


def head_lanes(head):
    lanes = lax.broadcasted_iota(jnp.int32, (1, HALF), 1)
    return jnp.where(lanes // HEAD == head, 1.0, 0.0).astype(BF)


def by_head(values):
    return jnp.concatenate([values * head_lanes(h) for h in range(HEADS)], axis=0)


def head_block(rows):
    return jnp.concatenate(
        [jnp.broadcast_to(head_lanes(h), (rows, HALF)) for h in range(HEADS)], axis=0
    )


def first_rows(values, count):
    low = count // 16 * 16
    if low >= values.shape[0]:
        return values
    row = lax.broadcasted_iota(jnp.int32, (values.shape[0] - low, 1), 0)
    tail = jnp.where(row < count - low, values[low:], 0.0)
    return jnp.concatenate([values[:low], tail], axis=0)


def pieces_of(pair, member):
    low = first_of(pair, member)
    return [(low + r * GRID_L, r * STRIPE) for r in range(GRID_L)]


def pipelined(stages, order, extra=()):
    extra = dict(extra)
    state = {}
    for turn in range(len(order) + len(stages) - 1):
        if turn in extra:
            extra[turn]()
        for at, stage in enumerate(stages):
            item = turn - at
            if 0 <= item < len(order):
                state[order[item]] = stage(order[item], state.get(order[item]))


def attend_kernel(
    x_ref,
    w_ref,
    s_ref,
    k_ref,
    tap_ref,
    mrow_ref,
    mkey_ref,
    hat_ref,
    att_ref,
    win_ref,
    e_ref,
    il_ref,
    o_ref,
    qkv_scr,
    turn_scr,
    back_scr,
    att_scr,
):
    @pl.when(pl.program_id(0) == 0)
    def _():
        for branch in range(2):
            qkv_scr[branch, ROWS:, :] = jnp.zeros((LONG - ROWS, 3 * HALF), F32)
        turn_scr[...] = jnp.zeros_like(turn_scr)
        att_scr[TOK_IMG:, :] = jnp.zeros((ROWS - TOK_IMG, D), F32)

    gain, shift = s_ref[0:1, :], s_ref[1:2, :]
    ones = head_block(WIN)

    def project(chunk):
        low, high = CHUNKS[chunk]
        hat, _ = normalise(rows_of(x_ref, low, high))
        hat_ref[0, low:high, :] = hat.astype(BF)
        a = (hat * gain + shift).astype(BF)
        for part in range(3):
            lanes = slice(part * D, (part + 1) * D)
            piece = dot(a, w_ref[:, lanes]) + s_ref[2 + part : 3 + part, :]
            if part == 0:
                piece = piece * (SCALE * LOG2E)
            for branch in range(2):
                qkv_scr[branch, low:high, part * HALF : (part + 1) * HALF] = piece[
                    :, branch * HALF : (branch + 1) * HALF
                ]

    def score(pair, _):
        state = []
        mask = max(pair - 4, 0) if pair < 4 else (1 if pair < 6 else 2)
        for member in range(2):
            at = 2 * pair + member
            if kind_of(pair) == 1:
                for source, target in pieces_of(pair, member):
                    turn_scr[at - 4, target : target + STRIPE, :] = qkv_scr[
                        1, source : source + STRIPE, :
                    ]
                window = turn_scr[at - 4, :QROWS, :]
            else:
                low = first_of(pair, member)
                window = qkv_scr[branch_of(pair, member), low : low + QROWS, :]
            window = window.astype(BF)
            win_ref[0, at] = window
            q, k, v = (window[:, part * HALF : (part + 1) * HALF] for part in range(3))
            none = jnp.zeros((WIN - QROWS, HALF), BF)
            k = jnp.concatenate([k, none], axis=0)
            left = jnp.concatenate([q, mrow_ref[mask]], axis=1)
            right = jnp.concatenate([by_head(k), mkey_ref[mask]], axis=1)
            state.append((v, dot_nt(left, right)))
        return state

    def soften(pair, state):
        new = []
        for member, (v, scores) in enumerate(state):
            exps = []
            for h in range(HEADS):
                part = scores[:, h * WIN : (h + 1) * WIN]
                peak = jnp.max(part, axis=-1, keepdims=True)
                exps.append(jnp.exp2(part - peak).astype(BF))
            e = jnp.concatenate(exps, axis=1)
            e_ref[0, 2 * pair + member] = e
            new.append((v, e))
        return new

    def mix(pair, state):
        taps, mixed = [], []
        none = jnp.zeros((WIN - QROWS, HALF), BF)
        for member, (v, e) in enumerate(state):
            at = 2 * pair + member
            kernel = k_ref[branch_of(pair, member)]
            v = jnp.concatenate([v, none], axis=0)
            both = dot(e, jnp.concatenate([by_head(v), ones], axis=1))
            inv = 1.0 / both[:, HALF:]
            o = both[:, :HALF] * inv
            il_ref[0, at] = inv
            o_ref[0, at] = o.astype(BF)
            mixed.append(o + kernel[9:10])
            low = kernel.astype(BF)
            taps.append(jnp.concatenate([v * low[tap : tap + 1] for tap in range(9)], axis=0))
        conv = dot(tap_ref[kind_of(pair)], jnp.concatenate(taps, axis=1))
        for member in range(2):
            piece = mixed[member] + conv[:, member * HALF : (member + 1) * HALF]
            branch = branch_of(pair, member)
            lanes = slice(branch * HALF, (branch + 1) * HALF)
            if kind_of(pair) == 1:
                at = 2 * pair + member - 4
                back_scr[at] = piece
                for source, target in pieces_of(pair, member):
                    att_scr[source : source + STRIPE, lanes] = back_scr[
                        at, target : target + STRIPE, :
                    ]
            else:
                low, count = first_of(pair, member), tokens_of(pair)
                att_scr[low : low + count, lanes] = piece[:count]

    project(0)
    extra = {1: functools.partial(project, 1), 3: functools.partial(project, 2)}
    pipelined((score, soften, mix), ORDER, extra)
    att_ref[0] = att_scr[...].astype(BF)


def gelu_parts(u):
    phi = 0.5 * lax.erf(u * 2**-0.5) + 0.5
    decay = jnp.exp2((-0.5 * LOG2E) * (u * u))
    return phi, phi + (u * 0.3989422804014327) * decay


def beside(*streams):
    left = [[list(stream), 0] for stream in streams]
    total = max((len(steps) for steps, _ in left), default=0)
    for at in range(total):
        for entry in left:
            steps, done = entry
            goal = -(-len(steps) * (at + 1) // total)
            for step in steps[done:goal]:
                step()
            entry[1] = goal


def feed_kernel(
    shard,
    cnt_ref,
    x_ref,
    c_ref,
    att_ref,
    w_ref,
    down_ref,
    s_ref,
    out_ref,
    dx_ref,
    datt_ref,
    pack_ref,
    sums_ref,
    bup_ref,
    h2_scr,
    u_scr,
    dg_scr,
    g_scr,
    du_scr,
    dy_scr,
    dz_scr,
    x1_scr,
    hat_scr,
    rs_scr,
    gup_scr,
    gdn_scr,
    gout_scr,
    turn_scr,
    pack_scr,
):
    image = pl.program_id(0)

    @pl.when(image == 0)
    def _():
        for ref in (gup_scr, gdn_scr, gout_scr, sums_ref, bup_ref):
            ref[...] = jnp.zeros_like(ref)

    bound = BIG + GRID_S * GRID_S * cnt_ref[image]
    bias_out, gain, shift = s_ref[15:16, :], s_ref[16:17, :], s_ref[17:18, :]

    def masked(low, high):
        row = low + lax.broadcasted_iota(jnp.int32, (high - low, 1), 0)
        return jnp.where(row < bound, rows_of(c_ref, low, high), 0.0)

    def enter(chunk):
        low, high = CHUNKS[chunk]

        def cot():
            dyr = masked(low, high).astype(BF)
            dy_scr[low:high, :] = dyr
            sums_ref[0] += fold(dyr.astype(F32))

        def norm():
            att = att_ref[0, low:high, :]
            x1 = rows_of(x_ref, low, high) + dot(att, w_ref[:, :D]) + bias_out
            x1_scr[low:high, :] = x1
            hat, scale = normalise(x1)
            hat_scr[low:high, :] = hat
            rs_scr[low:high, :] = scale
            h2_scr[low:high, :] = (hat * gain + shift).astype(BF)

        return [cot, norm]

    def expand(chunk):
        low, high = CHUNKS[chunk]

        def up(lanes):
            dy = dy_scr[low:high, :]
            dg_scr[low:high, lanes] = dot_nt(dy, down_ref[lanes, :])

        def hidden(lanes):
            cols = slice(D + lanes.start, D + lanes.stop)
            u_scr[low:high, lanes] = dot(h2_scr[low:high, :], w_ref[:, cols])

        steps = []
        for part in range(4):
            lanes = slice(part * D, (part + 1) * D)
            steps += [functools.partial(up, lanes), functools.partial(hidden, lanes)]
        return steps

    def gelu(chunk):
        low, high = CHUNKS[chunk]
        totals = {}

        def step(part, at):
            lanes = slice(part * D, (part + 1) * D)
            u = u_scr[at : at + 16, lanes] + s_ref[18 + part : 19 + part, :]
            phi, slope = gelu_parts(u)
            g_scr[at : at + 16, lanes] = (u * phi).astype(BF)
            du = dg_scr[at : at + 16, lanes] * slope
            totals[part] = fold(du) + totals[part] if part in totals else fold(du)
            du_scr[at : at + 16, lanes] = du.astype(BF)
            if at + 16 >= high:
                bup_ref[:, lanes] += totals[part]

        return [
            functools.partial(step, part, at) for part in range(4) for at in range(low, high, 16)
        ]

    def contract(chunk):
        low, high = CHUNKS[chunk]

        def back():
            dh2 = dot_nt(du_scr[low:high, :], w_ref[:, D : D + FF])
            hat = hat_scr[low:high, :]
            sums_ref[1] += fold(dh2 * hat)
            sums_ref[2] += fold(dh2)
            dx = masked(low, high) + norm_back(dh2 * gain, hat, rs_scr[low:high, :])
            store_rows(dx_ref, low, high, dx)
            dz = dx.astype(BF)
            dz_scr[low:high, :] = dz
            sums_ref[3] += fold(dz.astype(F32))

        def out():
            block = x1_scr[low:high, :] + dot(g_scr[low:high, :], down_ref[...])
            store_rows(out_ref, low, high, block + s_ref[22:23, :])

        def attention():
            datt = dot_nt(dz_scr[low:high, :], w_ref[:, :D])
            sums_ref[4] += fold(datt)
            datt_ref[0, low:high, :] = datt.astype(BF)

        return [back, out, attention]

    def weights(chunk):
        low, high = CHUNKS[chunk]

        def up(lanes):
            gup_scr[:, lanes] += dot_tn(h2_scr[low:high, :], du_scr[low:high, lanes])

        def down(lanes):
            gdn_scr[:, lanes] += dot_tn(dy_scr[low:high, :], g_scr[low:high, lanes])

        def out():
            gout_scr[...] += dot_tn(att_ref[0, low:high, :], dz_scr[low:high, :])

        steps = []
        for part in range(4):
            lanes = slice(part * D, (part + 1) * D)
            steps += [functools.partial(up, lanes), functools.partial(down, lanes)]
        return steps + [out]

    last = len(CHUNKS) - 1
    beside(enter(0) + expand(0))
    for chunk in range(last + 1):
        matrix = []
        if chunk < last:
            matrix += enter(chunk + 1) + expand(chunk + 1)
        if chunk > 0:
            matrix += contract(chunk - 1) + weights(chunk - 1)
        beside(gelu(chunk), matrix)
    beside(contract(last) + weights(last))

    @pl.when(image == pl.num_programs(0) - 1)
    def _():
        turn_scr[...] = gdn_scr[...].T
        for owner in range(D // shard):
            for part in range(FF // D):
                low = (owner * (FF // D) + part) * shard
                pack_scr[owner * shard : (owner + 1) * shard, part * D : (part + 1) * D] = turn_scr[
                    low : low + shard, :
                ]
        pack_ref[:, :D] = gout_scr[...].astype(BF)
        pack_ref[:, D : D + FF] = gup_scr[...].astype(BF)
        pack_ref[:, D + FF :] = pack_scr[...].astype(BF)


def small_spans(shard, narrow):
    count = D // shard
    own = shard * narrow
    rows = max((own * (i + 1) - 1) // HALF - own * i // HALF + 1 for i in range(count))
    return [(own * i // HALF, rows) for i in range(count)]


def back_kernel(
    spans,
    datt_ref,
    win_ref,
    e_ref,
    il_ref,
    o_ref,
    hat_ref,
    w_ref,
    s_ref,
    k_ref,
    feed_ref,
    bup_ref,
    tap_ref,
    edge_ref,
    dqkv_ref,
    pack_ref,
    g_scr,
    kern_scr,
    bias_scr,
    datt_scr,
    turn_scr,
    pad_scr,
    back_scr,
    dqkv_scr,
    small_scr,
    pack_scr,
):
    image = pl.program_id(0)

    @pl.when(image == 0)
    def _():
        for ref in (g_scr, kern_scr, bias_scr, turn_scr, pad_scr, small_scr, pack_scr):
            ref[...] = jnp.zeros_like(ref)
        datt_scr[ROWS:, :] = jnp.zeros((LONG - ROWS, D), F32)
        dqkv_scr[TOK_IMG:, :] = jnp.zeros((ROWS - TOK_IMG, 3 * D), F32)

    for low, high in CHUNKS:
        datt_scr[low:high, :] = datt_ref[0, low:high, :].astype(F32)
    minus = -head_block(WIN)
    none = jnp.zeros((WIN - QROWS, HALF), BF)

    def weigh(pair, _):
        state = []
        for member in range(2):
            at = 2 * pair + member
            branch = branch_of(pair, member)
            lanes = slice(branch * HALF, (branch + 1) * HALF)
            if kind_of(pair) == 1:
                for source, target in pieces_of(pair, member):
                    turn_scr[at - 4, target : target + STRIPE, :] = datt_scr[
                        source : source + STRIPE, lanes
                    ]
                grad = turn_scr[at - 4]
            else:
                low = first_of(pair, member)
                grad = first_rows(datt_scr[low : low + QROWS, lanes], tokens_of(pair))
            v = win_ref[0, at, :, 2 * HALF :]
            pad_scr[at, EDGE : EDGE + QROWS, :] = first_rows(v.astype(F32), tokens_of(pair))
            dn = grad * il_ref[0, at]
            z = (dn * o_ref[0, at].astype(F32)).astype(BF)
            dn = dn.astype(BF)
            left = jnp.concatenate([dn, z], axis=1)
            v = jnp.concatenate([v, none], axis=0)
            right = jnp.concatenate([by_head(v), minus], axis=1)
            state.append((grad, dn, dot_nt(left, right)))
        return state

    def score(pair, state):
        new = []
        for member, (grad, dn, weighed) in enumerate(state):
            e = e_ref[0, 2 * pair + member]
            ds = (weighed * e.astype(F32)).astype(BF)
            new.append((grad, dn, ds, e))
        return new

    def spread(pair, state):
        kind = kind_of(pair)
        taps, dvs = [], []
        for member, (grad, dn, ds, e) in enumerate(state):
            at = 2 * pair + member
            branch = branch_of(pair, member)
            kernel = k_ref[branch].astype(BF)
            q = win_ref[0, at, :, 0:HALF]
            k = jnp.concatenate([win_ref[0, at, :, HALF : 2 * HALF], none], axis=0)
            dq = dot(ds, by_head(k)) * SCALE
            q_t, dn_t = q.T, dn.T
            dk, dv = [], []
            for h in range(HEADS):
                lanes = slice(h * WIN, (h + 1) * WIN)
                own = slice(h * HEAD, (h + 1) * HEAD)
                dk.append(dot(q_t[own], ds[:, lanes]))
                dv.append(dot(dn_t[own], e[:, lanes]))
            dk = jnp.concatenate(dk, axis=0).T[:QROWS] * LN2
            dvs.append((dq, dk, jnp.concatenate(dv, axis=0).T[:QROWS]))
            low = jnp.concatenate([grad.astype(BF), none], axis=0)
            taps.append(
                jnp.concatenate([low * kernel[8 - tap : 9 - tap] for tap in range(9)], axis=0)
            )
            broad = shape_of(kind)[1]
            sides = {0: grad}
            if kind < 2:
                for dx in (-1, 1):
                    sides[dx] = grad * edge_ref[kind, 4 + dx]
            for tap, (dy, dx) in enumerate(TAPS):
                if kind < 2 or tap == 4:
                    side = sides[dx]
                else:
                    side = grad * edge_ref[kind, tap]
                start = EDGE + dy * broad + dx
                kern_scr[branch, tap] += fold(side * pad_scr[at, start : start + QROWS, :])
        conv = dot(tap_ref[kind], jnp.concatenate(taps, axis=1))
        for member in range(2):
            at = 2 * pair + member
            branch = branch_of(pair, member)
            dq, dk, dv = dvs[member]
            dv = dv + conv[:, member * HALF : (member + 1) * HALF]
            for part, piece in enumerate((dq, dk, dv)):
                lanes = slice(part * D + branch * HALF, part * D + (branch + 1) * HALF)
                if kind == 1:
                    back_scr[at - 4, part] = piece
                    for source, target in pieces_of(pair, member):
                        dqkv_scr[source : source + STRIPE, lanes] = back_scr[
                            at - 4, part, target : target + STRIPE, :
                        ]
                else:
                    low, count = first_of(pair, member), tokens_of(pair)
                    dqkv_scr[low : low + count, lanes] = piece[:count]

    pipelined((weigh, score, spread), ORDER)
    for low, high in CHUNKS:
        value = dqkv_scr[low:high, :]
        bias_scr[...] += fold(value)
        dqkv_ref[0, low:high, :] = value.astype(BF)
    g_scr[...] += dot_tn(hat_ref[0], dqkv_ref[0])

    @pl.when(image == pl.num_programs(0) - 1)
    def _():
        wide = w_ref[...].astype(F32)
        exact = functools.partial(
            lax.dot_general,
            dimension_numbers=(((1,), (1,)), ((), ())),
            precision=lax.Precision.HIGHEST,
            preferred_element_type=F32,
        )

        def put(row, terms):
            for at in range(0, terms.shape[1], HALF):
                small_scr[row : row + 1, :] = terms[:, at : at + HALF]
                row += 1

        total = lambda terms: jnp.sum(terms, axis=0, keepdims=True)
        bias = total(bias_scr[...])
        put(0, total(exact(jnp.ones((8, 3 * D), F32), wide * g_scr[...])) * 0.125)
        put(2, total(exact(bias_scr[...], wide)))
        put(4, bias)
        for tap in range(9):
            for branch in range(2):
                put(10 + 2 * tap + branch, total(kern_scr[branch, tap]))
        for row, entry in ((28, 4), (30, 3), (32, 1), (34, 2), (44, 0)):
            put(row, total(feed_ref[entry]))
        put(36, total(bup_ref[...]))
        for owner, (row, rows) in enumerate(spans):
            shard = D // len(spans)
            pack_scr[owner * shard : owner * shard + rows, :] = small_scr[row : row + rows, :]
        columns = s_ref[0:8, :].T
        grad = columns[:, 0:1] * g_scr[...] + columns[:, 1:2] * bias
        pack_ref[:, : 3 * D] = grad.astype(BF)
        pack_ref[:, 3 * D :] = pack_scr[...].astype(BF)


def input_kernel(x_ref, dqkv_ref, dx_ref, w_ref, s_ref, out_ref):
    for low, high in CHUNKS:
        dh = dot_nt(dqkv_ref[0, low:high, :], w_ref[...])
        hat, scale = normalise(rows_of(x_ref, low, high))
        grad = rows_of(dx_ref, low, high) + norm_back(dh * s_ref[0:1, :], hat, scale)
        store_rows(out_ref, low, high, grad)


def whole(shape):
    return pl.BlockSpec(shape, lambda i, *_: (0,) * len(shape))


def image_of(shape):
    return pl.BlockSpec((1,) + shape, lambda i, *_: (i,) + (0,) * len(shape))


def tokens():
    return pl.BlockSpec((TOK_IMG, D), lambda i, *_: (i, 0))


def params():
    return pltpu.CompilerParams(
        vmem_limit_bytes=VMEM, dimension_semantics=("arbitrary",)
    )


def sds(shape, dtype):
    return jax.ShapeDtypeStruct(shape, dtype)


def small_tables(small):
    rows = small.reshape(-1, D)
    taps = rows[5:15].reshape(10, 2, HALF).transpose(1, 0, 2)
    return jnp.pad(rows, ((0, 1), (0, 0))), jnp.pad(taps, ((0, 0), (0, 6), (0, 0)))


def run_attend(tokens_in, w_qkv, table, kernels, side):
    images = tokens_in.shape[0] // TOK_IMG
    mrow, mkey = mask_operands()
    consts = [table, kernels, side, bf(mrow), bf(mkey)]
    outs = [
        ((ROWS, D), BF),
        ((ROWS, D), BF),
        ((2 * PAIRS, QROWS, 3 * HALF), BF),
        ((2 * PAIRS, QROWS, HEADS * WIN), BF),
        ((2 * PAIRS, QROWS, HALF), F32),
        ((2 * PAIRS, QROWS, HALF), BF),
    ]
    return pl.pallas_call(
        attend_kernel,
        grid=(images,),
        in_specs=[tokens(), whole(w_qkv.shape)] + [whole(c.shape) for c in consts],
        out_specs=[image_of(shape) for shape, _ in outs],
        out_shape=[sds((images,) + shape, dtype) for shape, dtype in outs],
        scratch_shapes=[
            pltpu.VMEM((2, LONG, 3 * HALF), F32),
            pltpu.VMEM((4, QROWS, 3 * HALF), F32),
            pltpu.VMEM((4, QROWS, HALF), F32),
            pltpu.VMEM((ROWS, D), F32),
        ],
        compiler_params=params(),
        name="attend",
    )(tokens_in, w_qkv, *consts)


def run_feed(shard, counts, tokens_in, cotangent, att, wide, down, table):
    images = tokens_in.shape[0] // TOK_IMG
    return pl.pallas_call(
        functools.partial(feed_kernel, shard),
        grid_spec=pltpu.PrefetchScalarGridSpec(
            num_scalar_prefetch=1,
            grid=(images,),
            in_specs=[
                tokens(),
                tokens(),
                image_of((ROWS, D)),
                whole(wide.shape),
                whole(down.shape),
                whole(table.shape),
            ],
            out_specs=[
                tokens(),
                tokens(),
                image_of((ROWS, D)),
                whole((D, D + 2 * FF)),
                whole((5, 8, D)),
                whole((8, FF)),
            ],
            scratch_shapes=[
                pltpu.VMEM((ROWS, D), BF),
                pltpu.VMEM((ROWS, FF), F32),
                pltpu.VMEM((ROWS, FF), F32),
                pltpu.VMEM((ROWS, FF), BF),
                pltpu.VMEM((ROWS, FF), BF),
                pltpu.VMEM((ROWS, D), BF),
                pltpu.VMEM((ROWS, D), BF),
                pltpu.VMEM((ROWS, D), F32),
                pltpu.VMEM((ROWS, D), F32),
                pltpu.VMEM((ROWS, 1), F32),
                pltpu.VMEM((D, FF), F32),
                pltpu.VMEM((D, FF), F32),
                pltpu.VMEM((D, D), F32),
                pltpu.VMEM((FF, D), F32),
                pltpu.VMEM((D, FF), F32),
            ],
        ),
        out_shape=[
            sds(tokens_in.shape, F32),
            sds(tokens_in.shape, F32),
            sds((images, ROWS, D), BF),
            sds((D, D + 2 * FF), BF),
            sds((5, 8, D), F32),
            sds((8, FF), F32),
        ],
        compiler_params=params(),
        name="feed",
    )(counts, tokens_in, cotangent, att, wide, down, table)


def run_back(spans, blocks, w_qkv, table, kernels, sums, b_up, side):
    images = blocks[0].shape[0]
    consts = [w_qkv, table, kernels, sums, b_up, side, jnp.asarray(edge_masks())]
    return pl.pallas_call(
        functools.partial(back_kernel, spans),
        grid=(images,),
        in_specs=[image_of(b.shape[1:]) for b in blocks] + [whole(c.shape) for c in consts],
        out_specs=[image_of((ROWS, 3 * D)), whole((D, 3 * D + HALF))],
        out_shape=[sds((images, ROWS, 3 * D), BF), sds((D, 3 * D + HALF), BF)],
        scratch_shapes=[
            pltpu.VMEM((D, 3 * D), F32),
            pltpu.VMEM((2, 9, 8, HALF), F32),
            pltpu.VMEM((8, 3 * D), F32),
            pltpu.VMEM((LONG, D), F32),
            pltpu.VMEM((4, QROWS, HALF), F32),
            pltpu.VMEM((2 * PAIRS, QROWS + 2 * EDGE, HALF), F32),
            pltpu.VMEM((4, 3, QROWS, HALF), F32),
            pltpu.VMEM((ROWS, 3 * D), F32),
            pltpu.VMEM((56, HALF), F32),
            pltpu.VMEM((D, HALF), F32),
        ],
        compiler_params=params(),
        name="back",
    )(*blocks, *consts)


def run_input(tokens_in, dqkv, dx, w_qkv, table):
    return pl.pallas_call(
        input_kernel,
        grid=(dqkv.shape[0],),
        in_specs=[
            tokens(),
            image_of((ROWS, 3 * D)),
            tokens(),
            whole(w_qkv.shape),
            whole(table.shape),
        ],
        out_specs=tokens(),
        out_shape=sds(tokens_in.shape, F32),
        compiler_params=params(),
        name="input_grad",
    )(tokens_in, dqkv, dx, w_qkv, table)


def moments(grad, first, second):
    first_new = BETA_ONE * first + (1.0 - BETA_ONE) * grad
    second_new = BETA_TWO * second + (1.0 - BETA_TWO) * grad * grad
    direction = (
        first_new
        / (1.0 - BETA_ONE**STEP)
        / (jnp.sqrt(second_new / (1.0 - BETA_TWO**STEP)) + ADAM_EPS)
    )
    return (first_new, second_new, direction)


MATRICES = (slice(0, 3 * D), slice(3 * D, 4 * D), slice(4 * D, 4 * D + FF))


def lane_sums(values):
    column = jnp.sum(values * values, axis=0, keepdims=True)
    parts = [column[:, at : at + HALF] for at in range(0, column.shape[1], HALF)]
    return functools.reduce(jnp.add, parts)


def moment_kernel(
    gq_ref,
    gq_other_ref,
    gl_ref,
    gl_other_ref,
    ww_ref,
    wm_ref,
    wv_ref,
    dw_ref,
    dm_ref,
    dv_ref,
    wf_ref,
    ws_ref,
    wu_ref,
    df_ref,
    ds_ref,
    du_ref,
    sq_ref,
):
    for lanes, own, other in (
        (slice(0, 3 * D), gq_ref[:, : 3 * D], gq_other_ref[:, : 3 * D]),
        (slice(3 * D, 4 * D + FF), gl_ref[:, : D + FF], gl_other_ref[:, : D + FF]),
    ):
        first, second, way = moments(own + other, wm_ref[:, lanes], wv_ref[:, lanes])
        wf_ref[:, lanes] = first
        ws_ref[:, lanes] = second
        wu_ref[:, lanes] = way + DECAY * ww_ref[:, lanes]
    count = ww_ref.shape[0]
    for part in range(FF // D):
        lanes = slice(D + FF + part * D, D + FF + (part + 1) * D)
        own = slice(part * count, (part + 1) * count)
        grad = gl_ref[:, lanes] + gl_other_ref[:, lanes]
        first, second, way = moments(grad, dm_ref[own, :], dv_ref[own, :])
        df_ref[own, :] = first
        ds_ref[own, :] = second
        du_ref[own, :] = way + DECAY * dw_ref[own, :]
    for base, wide, down in ((0, ww_ref, dw_ref), (4, wu_ref, du_ref)):
        for at, lanes in enumerate(MATRICES):
            sq_ref[base + at : base + at + 1, :] = lane_sums(wide[:, lanes])
        sq_ref[base + 3 : base + 4, :] = lane_sums(down[...])


def update_kernel(
    sq_ref,
    ww_ref,
    wu_ref,
    we_ref,
    dw_ref,
    du_ref,
    de_ref,
    wn_ref,
    wa_ref,
    dn_ref,
    da_ref,
    norm_ref,
):
    total = jnp.sum(sq_ref[...], axis=1, keepdims=True)
    norm = jnp.sqrt(total)
    norm_ref[...] = jnp.broadcast_to(norm, norm_ref.shape)
    ratio = norm[0:4] / norm[4:8]
    keep = min(EMA_CEILING, (1.0 + STEP) / (10.0 + STEP))
    for at, lanes in enumerate(MATRICES):
        new = ww_ref[:, lanes] - (RATE * ratio[at : at + 1]) * wu_ref[:, lanes]
        wn_ref[:, lanes] = new
        wa_ref[:, lanes] = keep * we_ref[:, lanes] + (1.0 - keep) * new
    new = dw_ref[...] - (RATE * ratio[3:4]) * du_ref[...]
    dn_ref[...] = new
    da_ref[...] = keep * de_ref[...] + (1.0 - keep) * new


def plain(kernel, name, out_shape, *operands):
    return pl.pallas_call(kernel, out_shape=out_shape, compiler_params=pltpu.CompilerParams(
        vmem_limit_bytes=VMEM), name=name)(*operands)


def to_other(values):
    return lax.ppermute(values, "dp", [(0, 1), (1, 0)])


def side_by_side(wide, down):
    rows = wide.shape[0]
    blocks = [down[at : at + rows] for at in range(0, down.shape[0], rows)]
    return jnp.concatenate([wide] + blocks, axis=1)


def gather(values, count):
    copies = jnp.broadcast_to(values[None], (count,) + values.shape)
    return lax.all_to_all(copies, "fsdp", 0, 0).reshape(-1, values.shape[1])


def send_terms(values, count):
    return lax.all_to_all(values.reshape(count, -1, values.shape[1]), "fsdp", 0, 0)


def add_terms(terms):
    return jnp.sum(terms.astype(F32), axis=0)


def add_all(values, count):
    step = 1
    while step < count:
        values = values + lax.ppermute(values, "fsdp", [(i, i ^ step) for i in range(count)])
        step *= 2
    return values


def on_device(
    count,
    tokens_in,
    cotangent,
    crop_count,
    wide_w,
    wide_m,
    wide_v,
    wide_ema,
    down_w,
    down_m,
    down_v,
    down_ema,
    small_p,
    small_m,
    small_v,
    small_ema,
):
    rows = wide_w.shape[0]
    narrow = small_p.shape[0] // rows
    wide_low = wide_w.astype(BF)
    small_low = jnp.pad(small_p.astype(BF).reshape(rows, narrow), ((0, 0), (0, HALF - narrow)))
    first = jnp.concatenate([wide_low[:, : 3 * D], small_low], axis=1)
    first = gather(first, count)
    late_all = gather(side_by_side(wide_low[:, 3 * D :], down_w.astype(BF)), count)
    down_all = late_all[:, D + FF :].reshape(count, rows, FF // D, D)
    down_all = down_all.transpose(0, 2, 1, 3).reshape(FF, D)
    w_qkv = first[:, : 3 * D]
    table, kernels = small_tables(first[:, 3 * D : 3 * D + narrow].astype(F32).reshape(-1))
    side = np.stack([tap_matrix(kind) for kind in range(3)])
    side = bf(side.transpose(0, 2, 1, 3).reshape(3, QROWS, 9 * WIN))
    hat, att, win, e, il, o = run_attend(tokens_in, w_qkv, table, kernels, side)
    block_out, dx, datt, g_late, sums, b_up = run_feed(
        rows, crop_count, tokens_in, cotangent, att, late_all, down_all, table
    )
    late = send_terms(g_late, count)
    spans = small_spans(rows, narrow)
    dqkv, g_last = run_back(
        spans, [datt, win, e, il, o, hat], w_qkv, table, kernels, sums, b_up, side
    )
    late, g_last = lax.optimization_barrier((late, g_last))
    late = add_terms(late)
    last = send_terms(g_last, count)
    grad_in = run_input(tokens_in, dqkv, dx, w_qkv, table)
    last, grad_in = lax.optimization_barrier((last, grad_in))
    last = add_terms(last)
    last_other = to_other(last)
    late_other = to_other(late)
    wide_like, down_like = sds(wide_w.shape, F32), sds(down_w.shape, F32)
    wide_first, wide_second, wide_upd, down_first, down_second, down_upd, squares = plain(
        moment_kernel,
        "moment",
        [wide_like] * 3 + [down_like] * 3 + [sds((8, HALF), F32)],
        *(last, last_other, late, late_other),
        *(wide_w, wide_m, wide_v, down_w, down_m, down_v),
    )
    squares = add_all(squares, count)
    wide_new, wide_avg, down_new, down_avg, norms = plain(
        update_kernel,
        "update",
        [wide_like] * 2 + [down_like] * 2 + [sds((8, HALF), F32)],
        *(squares, wide_w, wide_upd, wide_ema, down_w, down_upd, down_ema),
    )
    shard_small = (last + last_other)[: spans[0][1], 3 * D :].reshape(-1)
    offset = lax.axis_index("fsdp") * (rows * narrow) % HALF
    shard_small = lax.dynamic_slice(shard_small, (offset,), (rows * narrow,))
    small_first, small_second, small_dir = moments(shard_small, small_m, small_v)
    small_new = small_p - RATE * small_dir
    ema_keep = min(EMA_CEILING, (1.0 + STEP) / (10.0 + STEP))
    small_avg = ema_keep * small_ema + (1.0 - ema_keep) * small_new
    return (
        block_out,
        grad_in,
        wide_new,
        wide_first,
        wide_second,
        wide_avg,
        down_new,
        down_first,
        down_second,
        down_avg,
        small_new,
        small_first,
        small_second,
        small_avg,
        norms[:, 0].reshape(2, 4),
    )


def solution(mesh):
    tok, row, vec = P(("dp", "fsdp"), None), P("fsdp", None), P("fsdp")
    in_specs = (tok, tok, P(("dp", "fsdp"))) + (row,) * 8 + (vec,) * 4
    out_specs = (tok, tok) + (row,) * 8 + (vec,) * 4 + (P(),)
    return jax.shard_map(
        functools.partial(on_device, mesh.shape["fsdp"]),
        mesh=mesh,
        in_specs=in_specs,
        out_specs=out_specs,
        check_vma=False,
    )
```

```python
import functools

import jax
import jax.numpy as jnp
import numpy as np
from jax import lax
from jax.experimental import pallas as pl
from jax.experimental.pallas import tpu as pltpu
from jax.sharding import PartitionSpec as P

D = 256
FF = 1024
HEAD = 32
STRIPE = 7
GRID_L = 14
GRID_S = 6
SMALL = 8
STEP = 10
TOK_IMG = 680

EPSILON = 1e-05
BETA_ONE = 0.9
BETA_TWO = 0.999
ADAM_EPS = 1e-06
DECAY = 0.05
RATE = 0.25
EMA_CEILING = 0.9999

ROWS = 688
BIG = 2 * GRID_L * GRID_L
PAIRS = 7
WIN = 128
QROWS = 112
HALF = 128
HEADS = 4
SCALE = HEAD**-0.5
LOG2E = 1.4426950408889634
LN2 = 0.6931471805599453
ROOT = 2**-0.5
CHUNKS = ((0, 240), (240, 464), (464, 688))
LONG = 744
EDGE = 16
COPIES = (3, 3, 2)
TAPS = tuple((dy, dx) for dy in (-1, 0, 1) for dx in (-1, 0, 1))
ORDER = (0, 2, 1, 3, 4, 5, 6)
VMEM = 62 * 1024 * 1024

BF = jnp.bfloat16
F32 = jnp.float32


def kind_of(pair):
    return 0 if pair < 2 else 1 if pair < 4 else 2


def branch_of(pair, member):
    return 0 if pair < 2 else 1 if pair < 4 else member


def first_of(pair, member):
    if pair < 2:
        return pair * GRID_L * GRID_L + member * STRIPE * GRID_L
    if pair < 4:
        return (pair - 2) * GRID_L * GRID_L + member * STRIPE
    return BIG + (pair - 4) * COPIES[0] * GRID_S * GRID_S


def tokens_of(pair):
    return STRIPE * GRID_L if pair < 4 else COPIES[pair - 4] * GRID_S * GRID_S


def shape_of(kind):
    return ((STRIPE, GRID_L), (GRID_L, STRIPE), (GRID_S, GRID_S))[kind]


def edge_masks():
    masks, places = [], {}
    for kind in range(3):
        high, broad = shape_of(kind)
        size = high * broad
        for dy, dx in TAPS:
            if (dy, dx) == (0, 0) or (kind < 2 and (dy != 0 or dx == 0)):
                continue
            mask = np.zeros((QROWS, HALF), np.float32)
            for at in range(size * (1 if kind < 2 else COPIES[0])):
                r, c = divmod(at % size, broad)
                mask[at] = 0 <= r + dy < high and 0 <= c + dx < broad
            places[kind, dy, dx] = len(masks)
            masks.append(mask)
    return np.stack(masks), places


def tap_matrix(kind):
    shape = shape_of(kind)
    copies = 1 if kind < 2 else COPIES[0]
    size = shape[0] * shape[1]
    out = np.zeros((9, QROWS, QROWS), np.float32)
    for copy in range(copies):
        for r in range(shape[0]):
            for c in range(shape[1]):
                for tap in range(9):
                    rr, cc = r + tap // 3 - 1, c + tap % 3 - 1
                    if 0 <= rr < shape[0] and 0 <= cc < shape[1]:
                        out[tap, copy * size + r * shape[1] + c, copy * size + rr * shape[1] + cc] = 1
    return out


def mask_operands():
    size = GRID_S * GRID_S
    rows = np.zeros((3, 2, QROWS, HALF), np.float32)
    keys = np.zeros((3, HALF // 2, WIN), np.float32)
    for kind, crops in ((0, 1), (1, 3), (2, 2)):
        count = STRIPE * GRID_L if kind == 0 else crops * size
        each = count // crops
        for at in range(QROWS):
            rows[kind, 0, at, HALF // 2 + (at // each if at < count else 0)] = 1
        for at in range(WIN):
            for crop in range(crops):
                if at >= count or at // each != crop:
                    keys[kind, crop, at] = -1e30
    rows[:, 1, :, : HALF // 2] = rows[:, 0, :, HALF // 2 :]
    return rows, np.tile(keys, (1, 1, 2))


def bf(array):
    return jnp.asarray(array, BF)


def dot(left, right):
    return jnp.dot(left, right, preferred_element_type=F32)


def dot_nt(left, right):
    return lax.dot_general(left, right, (((1,), (1,)), ((), ())), preferred_element_type=F32)


def dot_tn(left, right):
    return lax.dot_general(left, right, (((0,), (0,)), ((), ())), preferred_element_type=F32)


def normalise(values):
    center = values - jnp.mean(values, axis=-1, keepdims=True)
    spread = jnp.mean(center * center, axis=-1, keepdims=True)
    scale = lax.rsqrt(spread + EPSILON)
    return center * scale, scale


def norm_back(grad_hat, hat, scale):
    mean_grad = jnp.mean(grad_hat, axis=-1, keepdims=True)
    mean_dot = jnp.mean(grad_hat * hat, axis=-1, keepdims=True)
    return scale * (grad_hat - mean_grad - hat * mean_dot)


def rows_of(ref, low, high):
    if high <= TOK_IMG:
        return ref[low:high, :]
    tail = jnp.zeros((high - TOK_IMG, ref.shape[1]), F32)
    return jnp.concatenate([ref[low:TOK_IMG, :], tail], axis=0)


def store_rows(ref, low, high, values):
    last = min(high, TOK_IMG)
    ref[low:last, :] = values[: last - low]


def with_ones(turned):
    return jnp.concatenate([turned, jnp.ones((16, turned.shape[1]), turned.dtype)], axis=0)


def fold(values):
    return jnp.sum(values.reshape(values.shape[0] // 8, 8, values.shape[1]), axis=0)


def head_lanes(head):
    lanes = lax.broadcasted_iota(jnp.int32, (1, HALF), 1)
    return jnp.where(lanes // HEAD == head, 1.0, 0.0).astype(BF)


def by_head(values):
    return jnp.concatenate([values * head_lanes(h) for h in range(HEADS)], axis=0)


def lane_half(upper):
    lanes = lax.broadcasted_iota(jnp.int32, (1, HALF), 1)
    return jnp.where((lanes >= HALF // 2) == upper, 1.0, 0.0).astype(BF)


def two_heads(turned, pair):
    low = pair * 2 * HEAD
    none = jnp.zeros((HEAD, WIN), turned.dtype)
    first = jnp.concatenate([turned[low : low + HEAD], none], axis=1)
    second = jnp.concatenate([none, turned[low + HEAD : low + 2 * HEAD]], axis=1)
    return jnp.concatenate([first, second], axis=0)


def by_two_heads(left, other, turned, added):
    low, high = lane_half(False), lane_half(True)
    first = dot(
        left * low + other[0], jnp.concatenate([two_heads(turned, 0), added], axis=0)
    )
    second = dot(
        left * high + other[1], jnp.concatenate([added, two_heads(turned, 1)], axis=0)
    )
    return [first[:, :WIN], first[:, WIN:], second[:, :WIN], second[:, WIN:]]


def head_block(rows):
    return jnp.concatenate(
        [jnp.broadcast_to(head_lanes(h), (rows, HALF)) for h in range(HEADS)], axis=0
    )


def first_rows(values, count):
    low = count // 16 * 16
    if low >= values.shape[0]:
        return values
    row = lax.broadcasted_iota(jnp.int32, (values.shape[0] - low, 1), 0)
    tail = jnp.where(row < count - low, values[low:], 0.0)
    return jnp.concatenate([values[:low], tail], axis=0)


def pieces_of(pair, member):
    low = first_of(pair, member)
    return [(low + r * GRID_L, r * STRIPE) for r in range(GRID_L)]


def pipelined(stages, order, extra=()):
    extra = dict(extra)
    state = {item: {} for item in order}
    for turn in range(len(order) + len(stages) - 1):
        if turn in extra:
            extra[turn]()
        running = []
        for at, stage in enumerate(stages):
            if 0 <= turn - at < len(order):
                item = order[turn - at]
                running.append(stage(item, state[item]))
        while running:
            running = [stage for stage in running if next(stage, True) is None]


def norm_kernel(x_ref, hat_ref):
    for low in range(0, x_ref.shape[0], TOK_IMG // 5):
        hat_ref[low : low + TOK_IMG // 5, :] = normalise(x_ref[low : low + TOK_IMG // 5, :])[0]


def attend_kernel(
    x_ref,
    w_ref,
    s_ref,
    k_ref,
    tap_ref,
    mrow_ref,
    mkey_ref,
    hat_ref,
    att_ref,
    win_ref,
    e_ref,
    il_ref,
    o_ref,
    qkv_scr,
    turn_scr,
    back_scr,
    att_scr,
):
    @pl.when(pl.program_id(0) == 0)
    def _():
        for branch in range(2):
            qkv_scr[branch, ROWS:, :] = jnp.zeros((LONG - ROWS, 3 * HALF), F32)
        turn_scr[...] = jnp.zeros_like(turn_scr)
        att_scr[TOK_IMG:, :] = jnp.zeros((ROWS - TOK_IMG, D), F32)

    gain, shift = s_ref[0:1, :], s_ref[1:2, :]
    ones = head_block(WIN)

    def project(chunk):
        low, high = CHUNKS[chunk]
        hat = rows_of(x_ref, low, high)
        hat_ref[0, low:high, :] = hat.astype(BF)
        a = (hat * gain + shift).astype(BF)
        for part in range(3):
            lanes = slice(part * D, (part + 1) * D)
            piece = dot(a, w_ref[:, lanes]) + s_ref[2 + part : 3 + part, :]
            if part == 0:
                piece = piece * (SCALE * LOG2E)
            for branch in range(2):
                qkv_scr[branch, low:high, part * HALF : (part + 1) * HALF] = piece[
                    :, branch * HALF : (branch + 1) * HALF
                ]

    none = jnp.zeros((WIN - QROWS, HALF), BF)

    def cut(pair, state):
        for member in range(2):
            at = 2 * pair + member
            if kind_of(pair) == 1:
                for source, target in pieces_of(pair, member):
                    turn_scr[at - 4, target : target + STRIPE, :] = qkv_scr[
                        1, source : source + STRIPE, :
                    ]
                window = turn_scr[at - 4, :QROWS, :]
            else:
                low = first_of(pair, member)
                window = qkv_scr[branch_of(pair, member), low : low + QROWS, :]
            window = window.astype(BF)
            win_ref[0, at] = window
            state[member] = [window[:, part * HALF : (part + 1) * HALF] for part in range(3)]
            yield

    def score(pair, state):
        mask = 0 if pair < 4 else 1 if pair < 6 else 2
        for member in range(2):
            q, k, v = state[member]
            k = jnp.concatenate([k, none], axis=0).T
            rows = mrow_ref[mask, 0], mrow_ref[mask, 1]
            state[member] = v, by_two_heads(q, rows, k, mkey_ref[mask])
            yield

    def soften(pair, state):
        for member in range(2):
            v, scores = state[member]
            exps = []
            for part in scores:
                peak = jnp.max(part, axis=-1, keepdims=True)
                exps.append(jnp.exp2(part - peak).astype(BF))
            e = jnp.concatenate(exps, axis=1)
            e_ref[0, 2 * pair + member] = e
            state[member] = v, e
            yield

    def mix(pair, state):
        taps = []
        for member in range(2):
            v, e = state[member]
            low = k_ref[branch_of(pair, member)].astype(BF)
            keys = jnp.concatenate([v, none], axis=0)
            state[member] = dot(e, jnp.concatenate([by_head(keys), ones], axis=1))
            taps.append(jnp.concatenate([v * low[tap : tap + 1] for tap in range(9)], axis=0))
            yield
        state[2] = dot(tap_ref[kind_of(pair)], jnp.concatenate(taps, axis=1))
        yield

    def put(pair, state):
        for member in range(2):
            at = 2 * pair + member
            branch = branch_of(pair, member)
            lanes = slice(branch * HALF, (branch + 1) * HALF)
            both = state[member]
            inv = 1.0 / both[:, HALF:]
            o = both[:, :HALF] * inv
            il_ref[0, at] = inv
            o_ref[0, at] = o.astype(BF)
            conv = state[2][:, member * HALF : (member + 1) * HALF]
            piece = o + k_ref[branch, 9:10, :] + conv
            if kind_of(pair) == 1:
                back_scr[at - 4] = piece
                for source, target in pieces_of(pair, member):
                    att_scr[source : source + STRIPE, lanes] = back_scr[
                        at - 4, target : target + STRIPE, :
                    ]
            else:
                low, count = first_of(pair, member), tokens_of(pair)
                att_scr[low : low + count, lanes] = piece[:count]
            yield

    project(0)
    extra = {1: functools.partial(project, 1), 3: functools.partial(project, 2)}
    pipelined((cut, score, soften, mix, put), ORDER, extra)
    att_ref[0] = att_scr[...].astype(BF)


def gelu_parts(v):
    above = lax.erf(v) + 1.0
    decay = jnp.exp2((v * v) * -LOG2E)
    return v * above, above + (v * decay) * (2 / np.sqrt(np.pi))


def beside(*streams):
    left = [[list(stream), 0] for stream in streams]
    total = max((len(steps) for steps, _ in left), default=0)
    for at in range(total):
        for entry in left:
            steps, done = entry
            goal = -(-len(steps) * (at + 1) // total)
            for step in steps[done:goal]:
                step()
            entry[1] = goal


def weight_terms(grad, weight, bias):
    terms = []
    for value in (weight * bias,) if grad is None else (weight * grad, weight * bias):
        column = jnp.sum(value, axis=1, keepdims=True)
        terms.append(jnp.broadcast_to(column, (D, HALF)).T[0:1, :])
    return terms


def feed_kernel(
    shard,
    cnt_ref,
    x_ref,
    c_ref,
    att_ref,
    w_ref,
    down_ref,
    s_ref,
    out_ref,
    dx_ref,
    datt_ref,
    pack_ref,
    sums_ref,
    bup_ref,
    rs_scr,
    x1_scr,
    gup_scr,
    gdn_scr,
    gout_scr,
    turn_scr,
    pack_scr,
):
    image = pl.program_id(0)

    @pl.when(image == 0)
    def _():
        for ref in (gup_scr, gdn_scr, gout_scr, sums_ref, bup_ref):
            ref[...] = jnp.zeros_like(ref)

    bound = BIG + GRID_S * GRID_S * cnt_ref[image]
    bias_out, gain, shift = s_ref[15:16, :], s_ref[16:17, :], s_ref[17:18, :]
    lanes_of = [slice(part * D, (part + 1) * D) for part in range(FF // D)]
    count = 16
    rows = range(0, ROWS, count)
    biases = [s_ref[18 + part : 19 + part, :] * ROOT for part in range(FF // D)]
    sums = {}
    held = {}

    def add_sum(key, values, at, ref, *index):
        sums[key] = sums[key] + fold(values) if key in sums else fold(values)
        if at + count >= ROWS:
            ref[index] += sums[key]

    def keep(key, at, values):
        held.setdefault(key, []).append(values)
        if at + count >= ROWS:
            held[key] = jnp.concatenate(held[key], axis=0)

    def masked(at):
        row = at + lax.broadcasted_iota(jnp.int32, (count, 1), 0)
        return jnp.where(row < bound, rows_of(c_ref, at, at + count), 0.0)

    def cot(at):
        dy = masked(at)
        keep("dy", at, dy.astype(BF))
        add_sum("dy", dy, at, sums_ref, 0)

    def project():
        held["x1"] = dot(att_ref[0], w_ref[:, :D])

    def norm(at):
        own = slice(at, at + count)
        x1 = rows_of(x_ref, at, at + count) + held["x1"][own] + bias_out
        x1_scr[own, :] = x1
        hat, scale = normalise(x1)
        rs_scr[own, :] = scale
        keep("hat", at, hat.astype(BF))
        keep("h2", at, (hat * (gain * ROOT) + shift * ROOT).astype(BF))

    def hidden(part):
        cols = slice(D + part * D, D + (part + 1) * D)
        held["v", part] = dot(held["h2"], w_ref[:, cols])

    def hidden_back(part):
        held["dg", part] = dot_nt(held["dy"], down_ref[lanes_of[part], :])

    def gelu(part, at):
        own = slice(at, at + count)
        v = held["v", part][own] + biases[part]
        g, slope = gelu_parts(v)
        keep(("g", part), at, g.astype(BF))
        du = held["dg", part][own] * slope
        keep(("du", part), at, du.astype(BF))

    def gelus(part):
        return [functools.partial(gelu, part, at) for at in rows]

    def grad_up(part):
        both = dot(held["hat_t"], held["du", part])
        gup_scr[:, lanes_of[part]] += both[:D]
        bup_ref[:, lanes_of[part]] += both[D : D + 8]

    def grad_down(part):
        gdn_scr[:, lanes_of[part]] += dot(held["dy_t"], held["g", part])

    def joined(key, *parts):
        return jnp.concatenate([held[key, part] for part in parts], axis=1)

    half = FF // 2

    def out_first():
        held["out"] = dot(joined("g", 0, 1), down_ref[:half, :])

    def out_last():
        held["out"] += dot(joined("g", 2, 3), down_ref[half:, :])

    def out_store(at):
        own = slice(at, at + count)
        out = x1_scr[own, :] + held["out"][own] * ROOT + s_ref[22:23, :]
        store_rows(out_ref, at, at + count, out)

    def back_first():
        held["dh"] = dot_nt(joined("du", 0, 1), w_ref[:, D : D + half])

    def back_last():
        held["dh"] += dot_nt(joined("du", 2, 3), w_ref[:, D + half : D + FF])

    def norm_grad(at):
        own = slice(at, at + count)
        hat = held["hat"][own].astype(F32)
        dx = masked(at) + norm_back(held["dh"][own] * (gain * 0.5), hat, rs_scr[own, :])
        store_rows(dx_ref, at, at + count, dx)
        keep("dz", at, dx.astype(BF))
        add_sum("dz", dx, at, sums_ref, 1)

    def attention():
        datt = dot_nt(held["dz"], w_ref[:, :D])
        datt_ref[0] = datt.astype(BF)

    def grad_out():
        gout_scr[...] += dot_tn(att_ref[0], held["dz"])

    def each(step, *parts):
        return [functools.partial(step, part) for part in parts]

    def turn(key):
        held[key + "_t"] = held[key].T

    beside(each(cot, *rows), [project])
    turn("dy")
    beside(each(norm, *rows), each(hidden_back, 0, 1, 2, 3))
    turn("hat")
    held["hat_t"] = with_ones(held["hat_t"])
    hidden(0)
    beside(each(hidden, 1, 2, 3), gelus(0))
    beside(each(grad_up, 0) + each(grad_down, 0), gelus(1))
    beside([back_first] + each(grad_up, 1) + each(grad_down, 1), gelus(2))
    beside([out_first] + each(grad_up, 2) + each(grad_down, 2), gelus(3))
    back_last()
    beside([out_last] + each(grad_up, 3) + each(grad_down, 3), each(norm_grad, *rows))
    beside([attention, grad_out], each(out_store, *rows))

    @pl.when(image == pl.num_programs(0) - 1)
    def _():
        turn_scr[...] = gdn_scr[...].T * ROOT
        for owner in range(D // shard):
            for part in range(FF // D):
                low = (owner * (FF // D) + part) * shard
                pack_scr[owner * shard : (owner + 1) * shard, part * D : (part + 1) * D] = turn_scr[
                    low : low + shard, :
                ]
        bup_ref[...] *= 0.5
        bias = bup_ref[0:1, :]
        grad = gup_scr[...] * 0.5
        terms = weight_terms(grad, w_ref[:, D : D + FF].astype(F32), bias)
        out_bias = jnp.sum(sums_ref[1], axis=0, keepdims=True)
        terms += weight_terms(None, w_ref[:, :D].astype(F32), out_bias)
        for at, term in enumerate(terms):
            sums_ref[2 + at, 0:1, :] = term
        columns = s_ref[15:23, :].T
        grad = columns[:, 1:2] * grad + columns[:, 2:3] * bias
        pack_ref[:, :D] = gout_scr[...].astype(BF)
        pack_ref[:, D : D + FF] = grad.astype(BF)
        pack_ref[:, D + FF :] = pack_scr[...].astype(BF)


def small_spans(shard, narrow):
    count = D // shard
    own = shard * narrow
    rows = max((own * (i + 1) - 1) // HALF - own * i // HALF + 1 for i in range(count))
    return [(own * i // HALF, rows) for i in range(count)]


def back_kernel(
    spans,
    places,
    datt_ref,
    win_ref,
    e_ref,
    il_ref,
    o_ref,
    hat_ref,
    w_ref,
    s_ref,
    k_ref,
    feed_ref,
    bup_ref,
    tap_ref,
    edge_ref,
    dqkv_ref,
    pack_ref,
    g_scr,
    kern_scr,
    bias_scr,
    datt_scr,
    turn_scr,
    pad_scr,
    back_scr,
    dqkv_scr,
    small_scr,
    pack_scr,
):
    image = pl.program_id(0)

    @pl.when(image == 0)
    def _():
        for ref in (g_scr, kern_scr, bias_scr, turn_scr, pad_scr, small_scr, pack_scr):
            ref[...] = jnp.zeros_like(ref)
        datt_scr[ROWS:, :] = jnp.zeros((LONG - ROWS, D), F32)
        dqkv_scr[TOK_IMG:, :] = jnp.zeros((ROWS - TOK_IMG, 3 * D), F32)

    for low, high in CHUNKS:
        datt_scr[low:high, :] = datt_ref[0, low:high, :].astype(F32)
    minus = two_heads(jnp.full((HALF, WIN), -1.0, BF), 0)
    none = jnp.zeros((WIN - QROWS, HALF), BF)

    def weigh(pair, state):
        for member in range(2):
            at = 2 * pair + member
            branch = branch_of(pair, member)
            lanes = slice(branch * HALF, (branch + 1) * HALF)
            if kind_of(pair) == 1:
                for source, target in pieces_of(pair, member):
                    turn_scr[at - 4, target : target + STRIPE, :] = datt_scr[
                        source : source + STRIPE, lanes
                    ]
                grad = turn_scr[at - 4]
            else:
                low = first_of(pair, member)
                grad = first_rows(datt_scr[low : low + QROWS, lanes], tokens_of(pair))
            v = win_ref[0, at, :, 2 * HALF :]
            pad_scr[at, EDGE : EDGE + QROWS, :] = first_rows(v.astype(F32), tokens_of(pair))
            dn = grad * il_ref[0, at]
            z = pltpu.roll(dn * o_ref[0, at].astype(F32), HALF // 2, 1).astype(BF)
            dn = dn.astype(BF)
            rows = z * lane_half(True), z * lane_half(False)
            v = jnp.concatenate([v, none], axis=0).T
            state[member] = grad, dn, by_two_heads(dn, rows, v, minus)
            yield

    def score(pair, state):
        for member in range(2):
            grad, dn, weighed = state[member]
            e = e_ref[0, 2 * pair + member]
            ds = jnp.concatenate(weighed, axis=1).astype(BF) * e
            state[member] = grad, dn, ds, e
            yield

    def spread(pair, state):
        kind = kind_of(pair)
        taps = []
        for member in range(2):
            grad, dn, ds, e = state[member]
            at = 2 * pair + member
            kernel = k_ref[branch_of(pair, member)].astype(BF)
            q = win_ref[0, at, :, 0:HALF]
            k = jnp.concatenate([win_ref[0, at, :, HALF : 2 * HALF], none], axis=0)
            dq = dot(ds, by_head(k))
            q_t, dn_t = q.T, dn.T
            dk, dv = [], []
            for half in range(2):
                lanes = slice(2 * half * WIN, 2 * (half + 1) * WIN)
                own = slice(2 * half * HEAD, 2 * (half + 1) * HEAD)
                for parts, left, right in ((dk, q_t, ds), (dv, dn_t, e)):
                    both = dot(left[own], right[:, lanes])
                    parts += [both[:HEAD, :WIN], both[HEAD:, WIN:]]
            state[member] = dq, dk, dv, grad
            low = grad.astype(BF)
            taps.append(
                jnp.concatenate([low * kernel[8 - tap : 9 - tap] for tap in range(9)], axis=0)
            )
            yield
        state[2] = dot(tap_ref[kind], jnp.concatenate(taps, axis=1))
        yield

    def kernels(pair, state):
        kind = kind_of(pair)
        broad = shape_of(kind)[1]
        for member in range(2):
            at = 2 * pair + member
            grad = state[member][3]
            sides = {0: grad}
            if kind < 2:
                for dx in (-1, 1):
                    sides[dx] = grad * edge_ref[places[kind, 0, dx]]
            for tap, (dy, dx) in enumerate(TAPS):
                if kind < 2 or tap == 4:
                    side = sides[dx]
                else:
                    side = grad * edge_ref[places[kind, dy, dx]]
                start = EDGE + dy * broad + dx
                kern_scr[branch_of(pair, member), tap] += fold(
                    side * pad_scr[at, start : start + QROWS, :]
                )
            yield

    def put(pair, state):
        for member in range(2):
            at = 2 * pair + member
            branch = branch_of(pair, member)
            dq, dk, dv, _ = state[member]
            dk = jnp.concatenate(dk, axis=0).T[:QROWS] * LN2
            dv = jnp.concatenate(dv, axis=0).T[:QROWS]
            dv = dv + state[2][:, member * HALF : (member + 1) * HALF]
            for part, piece in enumerate((dq * SCALE, dk, dv)):
                lanes = slice(part * D + branch * HALF, part * D + (branch + 1) * HALF)
                if kind_of(pair) == 1:
                    back_scr[at - 4, part] = piece
                    for source, target in pieces_of(pair, member):
                        dqkv_scr[source : source + STRIPE, lanes] = back_scr[
                            at - 4, part, target : target + STRIPE, :
                        ]
                else:
                    low, count = first_of(pair, member), tokens_of(pair)
                    dqkv_scr[low : low + count, lanes] = piece[:count]
            yield

    pipelined((weigh, score, spread, put, kernels), ORDER)
    dqkv = dqkv_scr[...].astype(BF)
    dqkv_ref[0] = dqkv
    both = dot(with_ones(hat_ref[0].T), dqkv)
    g_scr[...] += both[:D]
    bias_scr[...] += both[D : D + 8]

    @pl.when(image == pl.num_programs(0) - 1)
    def _():
        def put(row, terms):
            for at in range(0, terms.shape[1], HALF):
                small_scr[row : row + 1, :] = terms[:, at : at + HALF]
                row += 1

        total = lambda terms: jnp.sum(terms, axis=0, keepdims=True)
        bias = bias_scr[0:1, :]
        gain, shift = weight_terms(g_scr[...], w_ref[:, : 3 * D].astype(F32), bias)
        put(0, gain)
        put(2, shift)
        put(4, bias)
        for tap in range(9):
            for branch in range(2):
                put(10 + 2 * tap + branch, total(kern_scr[branch, tap]))
        for row, entry in ((30, 1), (44, 0)):
            put(row, total(feed_ref[entry]))
        for row, entry in ((32, 2), (34, 3), (28, 4)):
            put(row, feed_ref[entry, 0:1, :])
        put(36, bup_ref[0:1, :])
        for owner, (row, rows) in enumerate(spans):
            shard = D // len(spans)
            pack_scr[owner * shard : owner * shard + rows, :] = small_scr[row : row + rows, :]
        columns = s_ref[0:8, :].T
        grad = columns[:, 0:1] * g_scr[...] + columns[:, 1:2] * bias
        pack_ref[:, : 3 * D] = grad.astype(BF)
        pack_ref[:, 3 * D :] = pack_scr[...].astype(BF)


def input_kernel(x_ref, dqkv_ref, dx_ref, w_ref, s_ref, *out_refs):
    out_ref = out_refs[-1]
    for low, high in CHUNKS:
        dh = dot_nt(dqkv_ref[0, low:high, :], w_ref[:, : 3 * D])
        hat, scale = normalise(rows_of(x_ref, low, high))
        grad = rows_of(dx_ref, low, high) + norm_back(dh * s_ref[0:1, :], hat, scale)
        store_rows(out_ref, low, high, grad)


def whole(shape):
    return pl.BlockSpec(shape, lambda i, *_: (0,) * len(shape))


def image_of(shape):
    return pl.BlockSpec((1,) + shape, lambda i, *_: (i,) + (0,) * len(shape))


def tokens():
    return pl.BlockSpec((TOK_IMG, D), lambda i, *_: (i, 0))


def params():
    return pltpu.CompilerParams(
        vmem_limit_bytes=VMEM, dimension_semantics=("arbitrary",)
    )


def sds(shape, dtype):
    return jax.ShapeDtypeStruct(shape, dtype)


def small_tables(small):
    rows = small.reshape(-1, D)
    taps = rows[5:15].reshape(10, 2, HALF).transpose(1, 0, 2)
    return rows, taps


def run_norm(tokens_in):
    rows = TOK_IMG * 2
    block = pl.BlockSpec((rows, D), lambda i: (i, 0))
    return pl.pallas_call(
        norm_kernel,
        grid=(tokens_in.shape[0] // rows,),
        in_specs=[block],
        out_specs=block,
        out_shape=sds(tokens_in.shape, F32),
        compiler_params=params(),
        name="norm",
    )(tokens_in)


def run_attend(tokens_in, w_qkv, table, kernels, side):
    images = tokens_in.shape[0] // TOK_IMG
    mrow, mkey = mask_operands()
    consts = [table, kernels, side, bf(mrow), bf(mkey)]
    outs = [
        ((ROWS, D), BF),
        ((ROWS, D), BF),
        ((2 * PAIRS, QROWS, 3 * HALF), BF),
        ((2 * PAIRS, QROWS, HEADS * WIN), BF),
        ((2 * PAIRS, QROWS, HALF), F32),
        ((2 * PAIRS, QROWS, HALF), BF),
    ]
    return pl.pallas_call(
        attend_kernel,
        grid=(images,),
        in_specs=[tokens(), whole(w_qkv.shape)] + [whole(c.shape) for c in consts],
        out_specs=[image_of(shape) for shape, _ in outs],
        out_shape=[sds((images,) + shape, dtype) for shape, dtype in outs],
        scratch_shapes=[
            pltpu.VMEM((2, LONG, 3 * HALF), F32),
            pltpu.VMEM((4, QROWS, 3 * HALF), F32),
            pltpu.VMEM((4, QROWS, HALF), F32),
            pltpu.VMEM((ROWS, D), F32),
        ],
        compiler_params=params(),
        name="attend",
    )(tokens_in, w_qkv, *consts)


def run_feed(shard, counts, tokens_in, cotangent, att, wide, down, table):
    images = tokens_in.shape[0] // TOK_IMG
    return pl.pallas_call(
        functools.partial(feed_kernel, shard),
        grid_spec=pltpu.PrefetchScalarGridSpec(
            num_scalar_prefetch=1,
            grid=(images,),
            in_specs=[
                tokens(),
                tokens(),
                image_of((ROWS, D)),
                whole(wide.shape),
                whole(down.shape),
                whole(table.shape),
            ],
            out_specs=[
                tokens(),
                tokens(),
                image_of((ROWS, D)),
                whole((D, D + 2 * FF)),
                whole((5, 8, D)),
                whole((8, FF)),
            ],
            scratch_shapes=[
                pltpu.VMEM((ROWS, 1), F32),
                pltpu.VMEM((ROWS, D), F32),
                pltpu.VMEM((D, FF), F32),
                pltpu.VMEM((D, FF), F32),
                pltpu.VMEM((D, D), F32),
                pltpu.VMEM((FF, D), F32),
                pltpu.VMEM((D, FF), F32),
            ],
        ),
        out_shape=[
            sds(tokens_in.shape, F32),
            sds(tokens_in.shape, F32),
            sds((images, ROWS, D), BF),
            sds((D, D + 2 * FF), BF),
            sds((5, 8, D), F32),
            sds((8, FF), F32),
        ],
        compiler_params=params(),
        name="feed",
    )(counts, tokens_in, cotangent, att, wide, down, table)


def run_back(spans, blocks, w_qkv, table, kernels, sums, b_up, side):
    images = blocks[0].shape[0]
    masks, places = edge_masks()
    consts = [w_qkv, table, kernels, sums, b_up, side, jnp.asarray(masks)]
    return pl.pallas_call(
        functools.partial(back_kernel, spans, places),
        grid=(images,),
        in_specs=[image_of(b.shape[1:]) for b in blocks] + [whole(c.shape) for c in consts],
        out_specs=[image_of((ROWS, 3 * D)), whole((D, 3 * D + HALF))],
        out_shape=[sds((images, ROWS, 3 * D), BF), sds((D, 3 * D + HALF), BF)],
        scratch_shapes=[
            pltpu.VMEM((D, 3 * D), F32),
            pltpu.VMEM((2, 9, 8, HALF), F32),
            pltpu.VMEM((8, 3 * D), F32),
            pltpu.VMEM((LONG, D), F32),
            pltpu.VMEM((4, QROWS, HALF), F32),
            pltpu.VMEM((2 * PAIRS, QROWS + 2 * EDGE, HALF), F32),
            pltpu.VMEM((4, 3, QROWS, HALF), F32),
            pltpu.VMEM((ROWS, 3 * D), F32),
            pltpu.VMEM((56, HALF), F32),
            pltpu.VMEM((D, HALF), F32),
        ],
        compiler_params=params(),
        name="back",
    )(*blocks, *consts)


def run_input(tokens_in, dqkv, dx, w_qkv, table, low, high, out=None):
    own = pl.BlockSpec((TOK_IMG, D), lambda i: (low + i, 0))
    rows = pl.BlockSpec((1, ROWS, 3 * D), lambda i: (low + i, 0, 0))
    ends = [] if out is None else [out]
    return pl.pallas_call(
        input_kernel,
        grid=(high - low,),
        in_specs=[own, rows, own, whole(w_qkv.shape), whole(table.shape)]
        + [pl.BlockSpec(memory_space=pl.ANY) for _ in ends],
        out_specs=own,
        out_shape=sds(tokens_in.shape, F32),
        input_output_aliases={5: 0} if ends else {},
        compiler_params=params(),
        cost_estimate=pl.CostEstimate(
            flops=(high - low) * 2 * ROWS * 3 * D * D,
            bytes_accessed=(high - low) * ROWS * D * 18,
            transcendentals=0,
        ),
        name="input_grad",
    )(tokens_in, dqkv, dx, w_qkv, table, *ends)


def moments(grad, first, second):
    first_new = BETA_ONE * first + (1.0 - BETA_ONE) * grad
    second_new = BETA_TWO * second + (1.0 - BETA_TWO) * grad * grad
    direction = (
        first_new
        / (1.0 - BETA_ONE**STEP)
        / (jnp.sqrt(second_new / (1.0 - BETA_TWO**STEP)) + ADAM_EPS)
    )
    return (first_new, second_new, direction)


MATRICES = (slice(0, 3 * D), slice(3 * D, 4 * D), slice(4 * D, 4 * D + FF))


def lane_sums(values):
    column = jnp.sum(values * values, axis=0, keepdims=True)
    parts = [column[:, at : at + HALF] for at in range(0, column.shape[1], HALF)]
    return functools.reduce(jnp.add, parts)


def moment_kernel(
    gq_ref,
    gq_other_ref,
    gl_ref,
    gl_other_ref,
    ww_ref,
    wm_ref,
    wv_ref,
    dw_ref,
    dm_ref,
    dv_ref,
    wf_ref,
    ws_ref,
    wu_ref,
    df_ref,
    ds_ref,
    du_ref,
    sq_ref,
):
    for lanes, own, other in (
        (slice(0, 3 * D), gq_ref[:, : 3 * D], gq_other_ref[:, : 3 * D]),
        (slice(3 * D, 4 * D + FF), gl_ref[:, : D + FF], gl_other_ref[:, : D + FF]),
    ):
        first, second, way = moments(own + other, wm_ref[:, lanes], wv_ref[:, lanes])
        wf_ref[:, lanes] = first
        ws_ref[:, lanes] = second
        wu_ref[:, lanes] = way + DECAY * ww_ref[:, lanes]
    count = ww_ref.shape[0]
    for part in range(FF // D):
        lanes = slice(D + FF + part * D, D + FF + (part + 1) * D)
        own = slice(part * count, (part + 1) * count)
        grad = gl_ref[:, lanes] + gl_other_ref[:, lanes]
        first, second, way = moments(grad, dm_ref[own, :], dv_ref[own, :])
        df_ref[own, :] = first
        ds_ref[own, :] = second
        du_ref[own, :] = way + DECAY * dw_ref[own, :]
    for base, wide, down in ((0, ww_ref, dw_ref), (4, wu_ref, du_ref)):
        for at, lanes in enumerate(MATRICES):
            sq_ref[base + at : base + at + 1, :] = lane_sums(wide[:, lanes])
        sq_ref[base + 3 : base + 4, :] = lane_sums(down[...])


def update_kernel(
    sq_ref,
    ww_ref,
    wu_ref,
    we_ref,
    dw_ref,
    du_ref,
    de_ref,
    wn_ref,
    wa_ref,
    dn_ref,
    da_ref,
    norm_ref,
):
    total = jnp.sum(jnp.sum(sq_ref[...], axis=0), axis=1, keepdims=True)
    norm = jnp.sqrt(total)
    row = lax.broadcasted_iota(jnp.int32, (8, HALF), 0)
    lane = lax.broadcasted_iota(jnp.int32, (8, HALF), 1)
    for half in range(2):
        own = jnp.where(row == lane + 4 * half, norm, 0.0)
        norm_ref[half : half + 1, :] = jnp.sum(own, axis=0, keepdims=True)[:, 0:4]
    ratio = norm[0:4] / norm[4:8]
    keep = min(EMA_CEILING, (1.0 + STEP) / (10.0 + STEP))
    for at, lanes in enumerate(MATRICES):
        new = ww_ref[:, lanes] - (RATE * ratio[at : at + 1]) * wu_ref[:, lanes]
        wn_ref[:, lanes] = new
        wa_ref[:, lanes] = keep * we_ref[:, lanes] + (1.0 - keep) * new
    new = dw_ref[...] - (RATE * ratio[3:4]) * du_ref[...]
    dn_ref[...] = new
    da_ref[...] = keep * de_ref[...] + (1.0 - keep) * new


def plain(kernel, name, out_shape, *operands):
    return pl.pallas_call(kernel, out_shape=out_shape, compiler_params=pltpu.CompilerParams(
        vmem_limit_bytes=VMEM), name=name)(*operands)


def to_other(values):
    return lax.ppermute(values, "dp", [(0, 1), (1, 0)])


def side_by_side(wide, down):
    rows = wide.shape[0]
    blocks = [down[at : at + rows] for at in range(0, down.shape[0], rows)]
    return jnp.concatenate([wide] + blocks, axis=1)


def copies(values, count):
    return jnp.broadcast_to(values[None], (count,) + values.shape)


def send_terms(values, count):
    return lax.all_to_all(values.reshape(count, -1, values.shape[-1]), "fsdp", 0, 0)


def add_terms(terms):
    return jnp.sum(terms.astype(F32), axis=0)


def on_device(
    count,
    tokens_in,
    cotangent,
    crop_count,
    wide_w,
    wide_m,
    wide_v,
    wide_ema,
    down_w,
    down_m,
    down_v,
    down_ema,
    small_p,
    small_m,
    small_v,
    small_ema,
):
    rows = wide_w.shape[0]
    narrow = small_p.shape[0] // rows
    wide_low = wide_w.astype(BF)
    small_low = jnp.pad(small_p.astype(BF).reshape(rows, narrow), ((0, 0), (0, HALF - narrow)))
    first = jnp.concatenate([wide_low[:, : 3 * D], small_low], axis=1)
    first = send_terms(copies(first, count), count)
    late_all = copies(side_by_side(wide_low[:, 3 * D :], down_w.astype(BF)), count)
    hat = run_norm(tokens_in)
    first, late_all, hat = lax.optimization_barrier((first, late_all, hat))
    first = first.reshape(D, -1)
    late_all = send_terms(late_all, count).reshape(D, -1)
    down_all = late_all[:, D + FF :].reshape(count, rows, FF // D, D)
    down_all = down_all.transpose(0, 2, 1, 3).reshape(FF, D)
    table, kernels = small_tables(first[:, 3 * D : 3 * D + narrow].astype(F32).reshape(-1))
    side = np.stack([tap_matrix(kind) for kind in range(3)])
    side = bf(side.transpose(0, 2, 1, 3).reshape(3, QROWS, 9 * QROWS))
    hat, att, win, e, il, o = run_attend(hat, first, table, kernels, side)
    block_out, dx, datt, g_late, sums, b_up = run_feed(
        rows, crop_count, tokens_in, cotangent, att, late_all, down_all, table
    )
    late = send_terms(g_late, count)
    spans = small_spans(rows, narrow)
    dqkv, g_last = run_back(
        spans, [datt, win, e, il, o, hat], first, table, kernels, sums, b_up, side
    )
    late, g_last = lax.optimization_barrier((late, g_last))
    late = add_terms(late)
    last = send_terms(g_last, count)
    images = dqkv.shape[0]
    begin = images * 3 // 4
    grad_in = run_input(tokens_in, dqkv, dx, first, table, 0, begin)
    last, grad_in = lax.optimization_barrier((last, grad_in))
    last = add_terms(last)
    last_other = to_other(last)
    late_other = to_other(late)
    wide_like, down_like = sds(wide_w.shape, F32), sds(down_w.shape, F32)
    wide_first, wide_second, wide_upd, down_first, down_second, down_upd, squares = plain(
        moment_kernel,
        "moment",
        [wide_like] * 3 + [down_like] * 3 + [sds((8, HALF), F32)],
        *(last, last_other, late, late_other),
        *(wide_w, wide_m, wide_v, down_w, down_m, down_v),
    )
    squares, grad_in = lax.optimization_barrier((copies(squares, count), grad_in))
    squares = send_terms(squares, count)
    grad_in = run_input(tokens_in, dqkv, dx, first, table, begin, images, grad_in)
    squares, grad_in = lax.optimization_barrier((squares, grad_in))
    wide_new, wide_avg, down_new, down_avg, norms = plain(
        update_kernel,
        "update",
        [wide_like] * 2 + [down_like] * 2 + [sds((2, 4), F32)],
        *(squares, wide_w, wide_upd, wide_ema, down_w, down_upd, down_ema),
    )
    shard_small = (last + last_other)[: spans[0][1], 3 * D :].reshape(-1)
    offset = lax.axis_index("fsdp") * (rows * narrow) % HALF
    shard_small = lax.dynamic_slice(shard_small, (offset,), (rows * narrow,))
    small_first, small_second, small_dir = moments(shard_small, small_m, small_v)
    small_new = small_p - RATE * small_dir
    ema_keep = min(EMA_CEILING, (1.0 + STEP) / (10.0 + STEP))
    small_avg = ema_keep * small_ema + (1.0 - ema_keep) * small_new
    return (
        block_out,
        grad_in,
        wide_new,
        wide_first,
        wide_second,
        wide_avg,
        down_new,
        down_first,
        down_second,
        down_avg,
        small_new,
        small_first,
        small_second,
        small_avg,
        norms,
    )


def solution(mesh):
    tok, row, vec = P(("dp", "fsdp"), None), P("fsdp", None), P("fsdp")
    in_specs = (tok, tok, P(("dp", "fsdp"))) + (row,) * 8 + (vec,) * 4
    out_specs = (tok, tok) + (row,) * 8 + (vec,) * 4 + (P(),)
    return jax.shard_map(
        functools.partial(on_device, mesh.shape["fsdp"]),
        mesh=mesh,
        in_specs=in_specs,
        out_specs=out_specs,
        check_vma=False,
    )
```

```python
import functools

import jax
import jax.numpy as jnp
import numpy as np
from jax import lax
from jax.experimental import pallas as pl
from jax.experimental.pallas import tpu as pltpu
from jax.sharding import PartitionSpec as P

D = 256
FF = 1024
HEAD = 32
STRIPE = 7
GRID_L = 14
GRID_S = 6
SMALL = 8
STEP = 10
TOK_IMG = 680

EPSILON = 1e-05
BETA_ONE = 0.9
BETA_TWO = 0.999
ADAM_EPS = 1e-06
DECAY = 0.05
RATE = 0.25
EMA_CEILING = 0.9999

ROWS = 688
BIG = 2 * GRID_L * GRID_L
PAIRS = 7
WIN = 128
QROWS = 112
HALF = 128
HEADS = 4
SCALE = HEAD**-0.5
LOG2E = 1.4426950408889634
LN2 = 0.6931471805599453
ROOT = 2**-0.5
CHUNKS = ((0, 240), (240, 464), (464, 688))
LONG = 744
EDGE = 16
COPIES = (3, 3, 2)
TAPS = tuple((dy, dx) for dy in (-1, 0, 1) for dx in (-1, 0, 1))
ORDER = (0, 2, 1, 3, 4, 5, 6)
VMEM = 60 * 1024 * 1024

BF = jnp.bfloat16
F32 = jnp.float32


def kind_of(pair):
    return 0 if pair < 2 else 1 if pair < 4 else 2


def branch_of(pair, member):
    return 0 if pair < 2 else 1 if pair < 4 else member


def first_of(pair, member):
    if pair < 2:
        return pair * GRID_L * GRID_L + member * STRIPE * GRID_L
    if pair < 4:
        return (pair - 2) * GRID_L * GRID_L + member * STRIPE
    return BIG + (pair - 4) * COPIES[0] * GRID_S * GRID_S


def tokens_of(pair):
    return STRIPE * GRID_L if pair < 4 else COPIES[pair - 4] * GRID_S * GRID_S


def shape_of(kind):
    return ((STRIPE, GRID_L), (GRID_L, STRIPE), (GRID_S, GRID_S))[kind]


def edge_masks():
    masks, places = [], {}
    for kind in range(3):
        high, broad = shape_of(kind)
        size = high * broad
        for dy, dx in TAPS:
            if (dy, dx) == (0, 0) or (kind < 2 and (dy != 0 or dx == 0)):
                continue
            mask = np.zeros((QROWS, HALF), np.float32)
            for at in range(size * (1 if kind < 2 else COPIES[0])):
                r, c = divmod(at % size, broad)
                mask[at] = 0 <= r + dy < high and 0 <= c + dx < broad
            places[kind, dy, dx] = len(masks)
            masks.append(mask)
    return np.stack(masks), places


def tap_matrix(kind):
    shape = shape_of(kind)
    copies = 1 if kind < 2 else COPIES[0]
    size = shape[0] * shape[1]
    out = np.zeros((9, QROWS, QROWS), np.float32)
    for copy in range(copies):
        for r in range(shape[0]):
            for c in range(shape[1]):
                for tap in range(9):
                    rr, cc = r + tap // 3 - 1, c + tap % 3 - 1
                    if 0 <= rr < shape[0] and 0 <= cc < shape[1]:
                        out[tap, copy * size + r * shape[1] + c, copy * size + rr * shape[1] + cc] = 1
    return out


def mask_operands():
    size = GRID_S * GRID_S
    rows = np.zeros((3, 2, QROWS, HALF), np.float32)
    keys = np.zeros((3, HALF // 2, WIN), np.float32)
    for kind, crops in ((0, 1), (1, 3), (2, 2)):
        count = STRIPE * GRID_L if kind == 0 else crops * size
        each = count // crops
        for at in range(QROWS):
            rows[kind, 0, at, HALF // 2 + (at // each if at < count else 0)] = 1
        for at in range(WIN):
            for crop in range(crops):
                if at >= count or at // each != crop:
                    keys[kind, crop, at] = -1e30
    rows[:, 1, :, : HALF // 2] = rows[:, 0, :, HALF // 2 :]
    return rows, np.tile(keys, (1, 1, 2))


def bf(array):
    return jnp.asarray(array, BF)


def dot(left, right):
    return jnp.dot(left, right, preferred_element_type=F32)


def dot_nt(left, right):
    return lax.dot_general(left, right, (((1,), (1,)), ((), ())), preferred_element_type=F32)


def dot_tn(left, right):
    return lax.dot_general(left, right, (((0,), (0,)), ((), ())), preferred_element_type=F32)


def normalise(values):
    center = values - jnp.mean(values, axis=-1, keepdims=True)
    spread = jnp.mean(center * center, axis=-1, keepdims=True)
    scale = lax.rsqrt(spread + EPSILON)
    return center * scale, scale


def norm_back(grad_hat, hat, scale):
    mean_grad = jnp.mean(grad_hat, axis=-1, keepdims=True)
    mean_dot = jnp.mean(grad_hat * hat, axis=-1, keepdims=True)
    return scale * (grad_hat - mean_grad - hat * mean_dot)


def rows_of(ref, low, high):
    if high <= TOK_IMG:
        return ref[low:high, :]
    tail = jnp.zeros((high - TOK_IMG, ref.shape[1]), F32)
    return jnp.concatenate([ref[low:TOK_IMG, :], tail], axis=0)


def store_rows(ref, low, high, values):
    last = min(high, TOK_IMG)
    ref[low:last, :] = values[: last - low]


def with_ones(turned):
    return jnp.concatenate([turned, jnp.ones((16, turned.shape[1]), turned.dtype)], axis=0)


def fold(values):
    return jnp.sum(values.reshape(values.shape[0] // 8, 8, values.shape[1]), axis=0)


def head_lanes(head):
    lanes = lax.broadcasted_iota(jnp.int32, (1, HALF), 1)
    return jnp.where(lanes // HEAD == head, 1.0, 0.0).astype(BF)


def by_head(values):
    return jnp.concatenate([values * head_lanes(h) for h in range(HEADS)], axis=0)


def lane_half(upper):
    lanes = lax.broadcasted_iota(jnp.int32, (1, HALF), 1)
    return jnp.where((lanes >= HALF // 2) == upper, 1.0, 0.0).astype(BF)


def two_heads(turned, pair):
    low = pair * 2 * HEAD
    none = jnp.zeros((HEAD, WIN), turned.dtype)
    first = jnp.concatenate([turned[low : low + HEAD], none], axis=1)
    second = jnp.concatenate([none, turned[low + HEAD : low + 2 * HEAD]], axis=1)
    return jnp.concatenate([first, second], axis=0)


def by_two_heads(left, other, turned, added):
    low, high = lane_half(False), lane_half(True)
    first = dot(
        left * low + other[0], jnp.concatenate([two_heads(turned, 0), added], axis=0)
    )
    second = dot(
        left * high + other[1], jnp.concatenate([added, two_heads(turned, 1)], axis=0)
    )
    return [first[:, :WIN], first[:, WIN:], second[:, :WIN], second[:, WIN:]]


def head_block(rows):
    return jnp.concatenate(
        [jnp.broadcast_to(head_lanes(h), (rows, HALF)) for h in range(HEADS)], axis=0
    )


def first_rows(values, count):
    low = count // 16 * 16
    if low >= values.shape[0]:
        return values
    row = lax.broadcasted_iota(jnp.int32, (values.shape[0] - low, 1), 0)
    tail = jnp.where(row < count - low, values[low:], 0.0)
    return jnp.concatenate([values[:low], tail], axis=0)


def pieces_of(pair, member):
    low = first_of(pair, member)
    return [(low + r * GRID_L, r * STRIPE) for r in range(GRID_L)]


def pipelined(stages, order, extra=()):
    extra = dict(extra)
    state = {item: {} for item in order}
    for turn in range(len(order) + max(lag for lag, _ in stages)):
        if turn in extra:
            extra[turn]()
        running = []
        for lag, stage in stages:
            if 0 <= turn - lag < len(order):
                item = order[turn - lag]
                running.append(stage(item, state[item]))
        while running:
            running = [stage for stage in running if next(stage, True) is None]


def norm_kernel(x_ref, wide_ref, down_ref, hat_ref, late_ref):
    for low in range(0, x_ref.shape[0], TOK_IMG // 5):
        hat_ref[low : low + TOK_IMG // 5, :] = normalise(x_ref[low : low + TOK_IMG // 5, :])[0]

    @pl.when(pl.program_id(0) == 0)
    def _():
        rows = wide_ref.shape[0]
        pieces = [wide_ref[:, 3 * D :]]
        pieces += [down_ref[at : at + rows, :] for at in range(0, down_ref.shape[0], rows)]
        late = jnp.concatenate(pieces, axis=1).astype(BF)
        for owner in range(late_ref.shape[0]):
            late_ref[owner] = late


def attend_kernel(
    x_ref,
    w_ref,
    s_ref,
    k_ref,
    tap_ref,
    mrow_ref,
    mkey_ref,
    hat_ref,
    att_ref,
    win_ref,
    e_ref,
    il_ref,
    o_ref,
    qkv_scr,
    turn_scr,
    back_scr,
    att_scr,
):
    @pl.when(pl.program_id(0) == 0)
    def _():
        for branch in range(2):
            qkv_scr[branch, ROWS:, :] = jnp.zeros((LONG - ROWS, 3 * HALF), F32)
        turn_scr[...] = jnp.zeros_like(turn_scr)
        att_scr[TOK_IMG:, :] = jnp.zeros((ROWS - TOK_IMG, D), F32)

    gain, shift = s_ref[0:1, :], s_ref[1:2, :]
    ones = head_block(WIN)

    def project(chunk):
        low, high = CHUNKS[chunk]
        hat = rows_of(x_ref, low, high)
        hat_ref[0, low:high, :] = hat.astype(BF)
        a = (hat * gain + shift).astype(BF)
        for part in range(3):
            lanes = slice(part * D, (part + 1) * D)
            piece = dot(a, w_ref[:, lanes]) + s_ref[2 + part : 3 + part, :]
            if part == 0:
                piece = piece * (SCALE * LOG2E)
            for branch in range(2):
                qkv_scr[branch, low:high, part * HALF : (part + 1) * HALF] = piece[
                    :, branch * HALF : (branch + 1) * HALF
                ]

    none = jnp.zeros((WIN - QROWS, HALF), BF)

    def cut(pair, state):
        for member in range(2):
            at = 2 * pair + member
            if kind_of(pair) == 1:
                for source, target in pieces_of(pair, member):
                    turn_scr[at - 4, target : target + STRIPE, :] = qkv_scr[
                        1, source : source + STRIPE, :
                    ]
                window = turn_scr[at - 4, :QROWS, :]
            else:
                low = first_of(pair, member)
                window = qkv_scr[branch_of(pair, member), low : low + QROWS, :]
            window = window.astype(BF)
            win_ref[0, at] = window
            state[member] = [window[:, part * HALF : (part + 1) * HALF] for part in range(3)]
            yield

    def score(pair, state):
        mask = 0 if pair < 4 else 1 if pair < 6 else 2
        for member in range(2):
            q, k, v = state[member]
            k = jnp.concatenate([k, none], axis=0).T
            rows = mrow_ref[mask, 0], mrow_ref[mask, 1]
            state[member] = v, by_two_heads(q, rows, k, mkey_ref[mask])
            yield

    def soften(pair, state):
        for member in range(2):
            v, scores = state[member]
            exps = []
            for part in scores:
                peak = jnp.max(part, axis=-1, keepdims=True)
                exps.append(jnp.exp2(part - peak).astype(BF))
            e = jnp.concatenate(exps, axis=1)
            e_ref[0, 2 * pair + member] = e
            state[member] = v, e
            yield

    def mix(pair, state):
        taps = []
        for member in range(2):
            v, e = state[member]
            low = k_ref[branch_of(pair, member)].astype(BF)
            keys = jnp.concatenate([v, none], axis=0)
            state[member] = dot(e, jnp.concatenate([by_head(keys), ones], axis=1))
            taps.append(jnp.concatenate([v * low[tap : tap + 1] for tap in range(9)], axis=0))
            yield
        state[2] = dot(tap_ref[kind_of(pair)], jnp.concatenate(taps, axis=1))
        yield

    def put(pair, state):
        for member in range(2):
            at = 2 * pair + member
            branch = branch_of(pair, member)
            lanes = slice(branch * HALF, (branch + 1) * HALF)
            both = state[member]
            inv = 1.0 / both[:, HALF:]
            o = both[:, :HALF] * inv
            il_ref[0, at] = inv
            o_ref[0, at] = o.astype(BF)
            conv = state[2][:, member * HALF : (member + 1) * HALF]
            piece = o + k_ref[branch, 9:10, :] + conv
            if kind_of(pair) == 1:
                back_scr[at - 4] = piece
                for source, target in pieces_of(pair, member):
                    att_scr[source : source + STRIPE, lanes] = back_scr[
                        at - 4, target : target + STRIPE, :
                    ]
            else:
                low, count = first_of(pair, member), tokens_of(pair)
                att_scr[low : low + count, lanes] = piece[:count]
            yield

    project(0)
    extra = {1: functools.partial(project, 1), 3: functools.partial(project, 2)}
    stages = enumerate((cut, score, soften, mix, put))
    pipelined(tuple(stages), ORDER, extra)
    att_ref[0] = att_scr[...].astype(BF)


def gelu_parts(v):
    above = lax.erf(v) + 1.0
    decay = jnp.exp2((v * v) * -LOG2E)
    return v * above, above + (v * decay) * (2 / np.sqrt(np.pi))


def beside(*streams):
    left = [[list(stream), 0] for stream in streams]
    total = max((len(steps) for steps, _ in left), default=0)
    for at in range(total):
        for entry in left:
            steps, done = entry
            goal = -(-len(steps) * (at + 1) // total)
            for step in steps[done:goal]:
                step()
            entry[1] = goal


def weight_terms(grad, weight, bias):
    terms = []
    for value in (weight * bias,) if grad is None else (weight * grad, weight * bias):
        column = jnp.sum(value, axis=1, keepdims=True)
        terms.append(jnp.broadcast_to(column, (D, HALF)).T[0:1, :])
    return terms


def down_blocks(shard):
    parts = FF // D
    return [(i, part, (i * parts + part) * shard) for i in range(D // shard) for part in range(parts)]


def feed_kernel(
    shard,
    cnt_ref,
    x_ref,
    c_ref,
    att_ref,
    w_ref,
    s_ref,
    out_ref,
    dx_ref,
    datt_ref,
    pack_ref,
    sums_ref,
    bup_ref,
    rs_scr,
    x1_scr,
    gup_scr,
    gdn_scr,
    gout_scr,
    turn_scr,
    pack_scr,
    down_scr,
):
    image = pl.program_id(0)

    @pl.when(image == 0)
    def _():
        for ref in (gup_scr, gdn_scr, gout_scr, sums_ref, bup_ref):
            ref[...] = jnp.zeros_like(ref)
        pack_scr[...] = w_ref[:, D + FF :].astype(F32)
        for owner, part, low in down_blocks(shard):
            turn_scr[low : low + shard, :] = pack_scr[
                owner * shard : (owner + 1) * shard, part * D : (part + 1) * D
            ]
        down_scr[...] = turn_scr[...].astype(BF)

    bound = BIG + GRID_S * GRID_S * cnt_ref[image]
    bias_out, gain, shift = s_ref[15:16, :], s_ref[16:17, :], s_ref[17:18, :]
    lanes_of = [slice(part * D, (part + 1) * D) for part in range(FF // D)]
    count = 16
    rows = range(0, ROWS, count)
    biases = [s_ref[18 + part : 19 + part, :] * ROOT for part in range(FF // D)]
    sums = {}
    held = {}

    def add_sum(key, values, at, ref, *index):
        sums[key] = sums[key] + fold(values) if key in sums else fold(values)
        if at + count >= ROWS:
            ref[index] += sums[key]

    def keep(key, at, values):
        held.setdefault(key, []).append(values)
        if at + count >= ROWS:
            held[key] = jnp.concatenate(held[key], axis=0)

    def masked(at):
        row = at + lax.broadcasted_iota(jnp.int32, (count, 1), 0)
        return jnp.where(row < bound, rows_of(c_ref, at, at + count), 0.0)

    def cot(at):
        dy = masked(at)
        keep("dy", at, dy.astype(BF))
        add_sum("dy", dy, at, sums_ref, 0)

    def project():
        held["x1"] = dot(att_ref[0], w_ref[:, :D])

    def norm(at):
        own = slice(at, at + count)
        x1 = rows_of(x_ref, at, at + count) + held["x1"][own] + bias_out
        x1_scr[own, :] = x1
        hat, scale = normalise(x1)
        rs_scr[own, :] = scale
        keep("hat", at, hat.astype(BF))
        keep("h2", at, (hat * (gain * ROOT) + shift * ROOT).astype(BF))

    def hidden(part):
        cols = slice(D + part * D, D + (part + 1) * D)
        held["v", part] = dot(held["h2"], w_ref[:, cols])

    def hidden_back(part):
        held["dg", part] = dot_nt(held["dy"], down_scr[lanes_of[part], :])

    def gelu(part, at):
        own = slice(at, at + count)
        v = held["v", part][own] + biases[part]
        g, slope = gelu_parts(v)
        keep(("g", part), at, g.astype(BF))
        du = held["dg", part][own] * slope
        keep(("du", part), at, du.astype(BF))

    def gelus(part):
        return [functools.partial(gelu, part, at) for at in rows]

    def grad_up(part):
        both = dot(held["hat_t"], held["du", part])
        gup_scr[:, lanes_of[part]] += both[:D]
        bup_ref[:, lanes_of[part]] += both[D : D + 8]

    def grad_down(part):
        gdn_scr[:, lanes_of[part]] += dot(held["dy_t"], held["g", part])

    def joined(key, *parts):
        return jnp.concatenate([held[key, part] for part in parts], axis=1)

    half = FF // 2

    def out_first():
        held["out"] = dot(joined("g", 0, 1), down_scr[:half, :])

    def out_last():
        held["out"] += dot(joined("g", 2, 3), down_scr[half:, :])

    def out_store(at):
        own = slice(at, at + count)
        out = x1_scr[own, :] + held["out"][own] * ROOT + s_ref[22:23, :]
        store_rows(out_ref, at, at + count, out)

    def back_first():
        held["dh"] = dot_nt(joined("du", 0, 1), w_ref[:, D : D + half])

    def back_last():
        held["dh"] += dot_nt(joined("du", 2, 3), w_ref[:, D + half : D + FF])

    def norm_grad(at):
        own = slice(at, at + count)
        hat = held["hat"][own].astype(F32)
        dx = masked(at) + norm_back(held["dh"][own] * (gain * 0.5), hat, rs_scr[own, :])
        store_rows(dx_ref, at, at + count, dx)
        keep("dz", at, dx.astype(BF))
        add_sum("dz", dx, at, sums_ref, 1)

    def attention():
        datt = dot_nt(held["dz"], w_ref[:, :D])
        datt_ref[0] = datt.astype(BF)

    def grad_out():
        gout_scr[...] += dot_tn(att_ref[0], held["dz"])

    def each(step, *parts):
        return [functools.partial(step, part) for part in parts]

    def turn(key):
        held[key + "_t"] = held[key].T

    beside(each(cot, *rows), [project])
    turn("dy")
    beside(each(norm, *rows), each(hidden_back, 0, 1, 2, 3))
    turn("hat")
    held["hat_t"] = with_ones(held["hat_t"])
    hidden(0)
    beside(each(hidden, 1, 2, 3), gelus(0))
    beside(each(grad_up, 0) + each(grad_down, 0), gelus(1))
    beside([back_first] + each(grad_up, 1) + each(grad_down, 1), gelus(2))
    beside([out_first] + each(grad_up, 2) + each(grad_down, 2), gelus(3))
    back_last()
    beside([out_last] + each(grad_up, 3) + each(grad_down, 3), each(norm_grad, *rows))
    beside([attention, grad_out], each(out_store, *rows))

    @pl.when(image == pl.num_programs(0) - 1)
    def _():
        turn_scr[...] = gdn_scr[...].T * ROOT
        for owner, part, low in down_blocks(shard):
            pack_scr[owner * shard : (owner + 1) * shard, part * D : (part + 1) * D] = turn_scr[
                low : low + shard, :
            ]
        bup_ref[...] *= 0.5
        bias = bup_ref[0:1, :]
        grad = gup_scr[...] * 0.5
        terms = weight_terms(grad, w_ref[:, D : D + FF].astype(F32), bias)
        out_bias = jnp.sum(sums_ref[1], axis=0, keepdims=True)
        terms += weight_terms(None, w_ref[:, :D].astype(F32), out_bias)
        for at, term in enumerate(terms):
            sums_ref[2 + at, 0:1, :] = term
        columns = s_ref[15:23, :].T
        grad = columns[:, 1:2] * grad + columns[:, 2:3] * bias
        pack_ref[:, :D] = gout_scr[...].astype(BF)
        pack_ref[:, D : D + FF] = grad.astype(BF)
        pack_ref[:, D + FF :] = pack_scr[...].astype(BF)


def small_spans(shard, narrow):
    count = D // shard
    own = shard * narrow
    rows = max((own * (i + 1) - 1) // HALF - own * i // HALF + 1 for i in range(count))
    return [(own * i // HALF, rows) for i in range(count)]


def back_kernel(
    spans,
    places,
    datt_ref,
    win_ref,
    e_ref,
    il_ref,
    o_ref,
    hat_ref,
    w_ref,
    s_ref,
    k_ref,
    feed_ref,
    bup_ref,
    tap_ref,
    edge_ref,
    dqkv_ref,
    pack_ref,
    g_scr,
    kern_scr,
    bias_scr,
    datt_scr,
    grad_scr,
    turn_scr,
    pad_scr,
    back_scr,
    dqkv_scr,
    small_scr,
    pack_scr,
):
    image = pl.program_id(0)

    @pl.when(image == 0)
    def _():
        for ref in (g_scr, kern_scr, bias_scr, turn_scr, pad_scr, small_scr, pack_scr):
            ref[...] = jnp.zeros_like(ref)
        datt_scr[ROWS:, :] = jnp.zeros((LONG - ROWS, D), F32)
        dqkv_scr[TOK_IMG:, :] = jnp.zeros((ROWS - TOK_IMG, 3 * D), F32)

    for low, high in CHUNKS:
        datt_scr[low:high, :] = datt_ref[0, low:high, :].astype(F32)
    minus = two_heads(jnp.full((HALF, WIN), -1.0, BF), 0)
    none = jnp.zeros((WIN - QROWS, HALF), BF)

    def weigh(pair, state):
        for member in range(2):
            at = 2 * pair + member
            branch = branch_of(pair, member)
            lanes = slice(branch * HALF, (branch + 1) * HALF)
            if kind_of(pair) == 1:
                for source, target in pieces_of(pair, member):
                    turn_scr[at - 4, target : target + STRIPE, :] = datt_scr[
                        source : source + STRIPE, lanes
                    ]
                grad = turn_scr[at - 4]
            else:
                low = first_of(pair, member)
                grad = first_rows(datt_scr[low : low + QROWS, lanes], tokens_of(pair))
            grad_scr[at * QROWS : (at + 1) * QROWS, :] = grad
            v = win_ref[0, at, :, 2 * HALF :]
            pad_scr[at, EDGE : EDGE + QROWS, :] = first_rows(v.astype(F32), tokens_of(pair))
            dn = grad * il_ref[0, at]
            z = pltpu.roll(dn * o_ref[0, at].astype(F32), HALF // 2, 1).astype(BF)
            dn = dn.astype(BF)
            rows = z * lane_half(True), z * lane_half(False)
            v = jnp.concatenate([v, none], axis=0).T
            state[member] = grad, dn, by_two_heads(dn, rows, v, minus)
            yield

    def score(pair, state):
        for member in range(2):
            grad, dn, weighed = state[member]
            e = e_ref[0, 2 * pair + member]
            ds = jnp.concatenate(weighed, axis=1).astype(BF) * e
            state[member] = grad, dn, ds, e
            yield

    def spread(pair, state):
        kind = kind_of(pair)
        taps = []
        for member in range(2):
            grad, dn, ds, e = state[member]
            at = 2 * pair + member
            kernel = k_ref[branch_of(pair, member)].astype(BF)
            q = win_ref[0, at, :, 0:HALF]
            k = jnp.concatenate([win_ref[0, at, :, HALF : 2 * HALF], none], axis=0)
            dq = dot(ds, by_head(k))
            row = 2 * PAIRS * QROWS + 8 * at
            grad_scr[row : row + 8, :] = dq[:8]
            q_t, dn_t = q.T, dn.T
            dk, dv = [], []
            for half in range(2):
                lanes = slice(2 * half * WIN, 2 * (half + 1) * WIN)
                own = slice(2 * half * HEAD, 2 * (half + 1) * HEAD)
                for parts, left, right in ((dk, q_t, ds), (dv, dn_t, e)):
                    both = dot(left[own], right[:, lanes])
                    parts += [both[:HEAD, :WIN], both[HEAD:, WIN:]]
            state[member] = dq, dk, dv
            low = grad.astype(BF)
            taps.append(
                jnp.concatenate([low * kernel[8 - tap : 9 - tap] for tap in range(9)], axis=0)
            )
            yield
        state[2] = dot(tap_ref[kind], jnp.concatenate(taps, axis=1))
        yield

    def kernels(pair, state):
        kind = kind_of(pair)
        broad = shape_of(kind)[1]
        for member in range(2):
            at = 2 * pair + member
            base = pl.multiple_of(at * QROWS + image // 4096 * 8, 8)
            totals = [jnp.zeros((8, HALF), F32)] * 9
            for low in range(0, tokens_of(pair), 8):
                own = slice(low, low + 8)
                grad = grad_scr[pl.ds(pl.multiple_of(base + low, 8), 8), :]
                sides = {}
                for tap, (dy, dx) in enumerate(TAPS):
                    place = places.get((kind, 0 if kind < 2 else dy, dx))
                    if place not in sides:
                        mask = 1.0 if place is None else edge_ref[place, own, :]
                        sides[place] = grad * mask
                    start = EDGE + low + dy * broad + dx
                    totals[tap] = totals[tap] + sides[place] * pad_scr[at, start : start + 8, :]
            for tap in range(9):
                kern_scr[branch_of(pair, member), tap] += totals[tap]
            yield

    def put(pair, state):
        for member in range(2):
            at = 2 * pair + member
            branch = branch_of(pair, member)
            dq, dk, dv = state[member]
            dk = jnp.concatenate(dk, axis=0).T[:QROWS] * LN2
            dv = jnp.concatenate(dv, axis=0).T[:QROWS]
            dv = dv + state[2][:, member * HALF : (member + 1) * HALF]
            for part, piece in enumerate((dq * SCALE, dk, dv)):
                lanes = slice(part * D + branch * HALF, part * D + (branch + 1) * HALF)
                if kind_of(pair) == 1:
                    back_scr[at - 4, part] = piece
                    for source, target in pieces_of(pair, member):
                        dqkv_scr[source : source + STRIPE, lanes] = back_scr[
                            at - 4, part, target : target + STRIPE, :
                        ]
                else:
                    low, count = first_of(pair, member), tokens_of(pair)
                    dqkv_scr[low : low + count, lanes] = piece[:count]
            yield

    pipelined(((3, kernels), (0, weigh), (1, score), (2, spread), (3, put)), ORDER)
    dqkv = dqkv_scr[...].astype(BF)
    dqkv_ref[0] = dqkv
    both = dot(with_ones(hat_ref[0].T), dqkv)
    g_scr[...] += both[:D]
    bias_scr[...] += both[D : D + 8]

    @pl.when(image == pl.num_programs(0) - 1)
    def _():
        def put(row, terms):
            for at in range(0, terms.shape[1], HALF):
                small_scr[row : row + 1, :] = terms[:, at : at + HALF]
                row += 1

        total = lambda terms: jnp.sum(terms, axis=0, keepdims=True)
        bias = bias_scr[0:1, :]
        gain, shift = weight_terms(g_scr[...], w_ref[:, : 3 * D].astype(F32), bias)
        put(0, gain)
        put(2, shift)
        put(4, bias)
        for tap in range(9):
            for branch in range(2):
                put(10 + 2 * tap + branch, total(kern_scr[branch, tap]))
        for row, entry in ((30, 1), (44, 0)):
            put(row, total(feed_ref[entry]))
        for row, entry in ((32, 2), (34, 3), (28, 4)):
            put(row, feed_ref[entry, 0:1, :])
        put(36, bup_ref[0:1, :])
        for owner, (row, rows) in enumerate(spans):
            shard = D // len(spans)
            pack_scr[owner * shard : owner * shard + rows, :] = small_scr[row : row + rows, :]
        columns = s_ref[0:8, :].T
        grad = columns[:, 0:1] * g_scr[...] + columns[:, 1:2] * bias
        pack_ref[:, : 3 * D] = grad.astype(BF)
        pack_ref[:, 3 * D :] = pack_scr[...].astype(BF)


def input_kernel(x_ref, dqkv_ref, dx_ref, w_ref, s_ref, *out_refs):
    out_ref = out_refs[-1]
    for low, high in CHUNKS:
        dh = dot_nt(dqkv_ref[0, low:high, :], w_ref[:, : 3 * D])
        hat, scale = normalise(rows_of(x_ref, low, high))
        grad = rows_of(dx_ref, low, high) + norm_back(dh * s_ref[0:1, :], hat, scale)
        store_rows(out_ref, low, high, grad)


def whole(shape):
    return pl.BlockSpec(shape, lambda i, *_: (0,) * len(shape))


def image_of(shape):
    return pl.BlockSpec((1,) + shape, lambda i, *_: (i,) + (0,) * len(shape))


def tokens():
    return pl.BlockSpec((TOK_IMG, D), lambda i, *_: (i, 0))


def params(room=0):
    return pltpu.CompilerParams(
        vmem_limit_bytes=VMEM - room * 1024 * 1024, dimension_semantics=("arbitrary",)
    )


def sds(shape, dtype):
    return jax.ShapeDtypeStruct(shape, dtype)


def small_tables(small):
    rows = small.reshape(-1, D)
    taps = rows[5:15].reshape(10, 2, HALF).transpose(1, 0, 2)
    return rows, taps


def run_norm(tokens_in, wide, down, count):
    rows = TOK_IMG * 2
    block = pl.BlockSpec((rows, D), lambda i: (i, 0))
    late = (count, wide.shape[0], D + 2 * FF)
    return pl.pallas_call(
        norm_kernel,
        grid=(tokens_in.shape[0] // rows,),
        in_specs=[block, whole(wide.shape), whole(down.shape)],
        out_specs=[block, whole(late)],
        out_shape=[sds(tokens_in.shape, F32), sds(late, BF)],
        compiler_params=params(),
        name="norm",
    )(tokens_in, wide, down)


def run_attend(tokens_in, w_qkv, table, kernels, side):
    images = tokens_in.shape[0] // TOK_IMG
    mrow, mkey = mask_operands()
    consts = [table, kernels, side, bf(mrow), bf(mkey)]
    outs = [
        ((ROWS, D), BF),
        ((ROWS, D), BF),
        ((2 * PAIRS, QROWS, 3 * HALF), BF),
        ((2 * PAIRS, QROWS, HEADS * WIN), BF),
        ((2 * PAIRS, QROWS, HALF), F32),
        ((2 * PAIRS, QROWS, HALF), BF),
    ]
    return pl.pallas_call(
        attend_kernel,
        grid=(images,),
        in_specs=[tokens(), whole(w_qkv.shape)] + [whole(c.shape) for c in consts],
        out_specs=[image_of(shape) for shape, _ in outs],
        out_shape=[sds((images,) + shape, dtype) for shape, dtype in outs],
        scratch_shapes=[
            pltpu.VMEM((2, LONG, 3 * HALF), F32),
            pltpu.VMEM((4, QROWS, 3 * HALF), F32),
            pltpu.VMEM((4, QROWS, HALF), F32),
            pltpu.VMEM((ROWS, D), F32),
        ],
        compiler_params=params(),
        name="attend",
    )(tokens_in, w_qkv, *consts)


def run_feed(shard, counts, tokens_in, cotangent, att, wide, table):
    images = tokens_in.shape[0] // TOK_IMG
    return pl.pallas_call(
        functools.partial(feed_kernel, shard),
        grid_spec=pltpu.PrefetchScalarGridSpec(
            num_scalar_prefetch=1,
            grid=(images,),
            in_specs=[
                tokens(),
                tokens(),
                image_of((ROWS, D)),
                whole(wide.shape),
                whole(table.shape),
            ],
            out_specs=[
                tokens(),
                tokens(),
                image_of((ROWS, D)),
                whole((D, D + 2 * FF)),
                whole((5, 8, D)),
                whole((8, FF)),
            ],
            scratch_shapes=[
                pltpu.VMEM((ROWS, 1), F32),
                pltpu.VMEM((ROWS, D), F32),
                pltpu.VMEM((D, FF), F32),
                pltpu.VMEM((D, FF), F32),
                pltpu.VMEM((D, D), F32),
                pltpu.VMEM((FF, D), F32),
                pltpu.VMEM((D, FF), F32),
                pltpu.VMEM((FF, D), BF),
            ],
        ),
        out_shape=[
            sds(tokens_in.shape, F32),
            sds(tokens_in.shape, F32),
            sds((images, ROWS, D), BF),
            sds((D, D + 2 * FF), BF),
            sds((5, 8, D), F32),
            sds((8, FF), F32),
        ],
        compiler_params=params(),
        name="feed",
    )(counts, tokens_in, cotangent, att, wide, table)


def run_back(spans, blocks, w_qkv, table, kernels, sums, b_up, side):
    images = blocks[0].shape[0]
    masks, places = edge_masks()
    consts = [w_qkv, table, kernels, sums, b_up, side, jnp.asarray(masks)]
    return pl.pallas_call(
        functools.partial(back_kernel, spans, places),
        grid=(images,),
        in_specs=[image_of(b.shape[1:]) for b in blocks] + [whole(c.shape) for c in consts],
        out_specs=[image_of((ROWS, 3 * D)), whole((D, 3 * D + HALF))],
        out_shape=[sds((images, ROWS, 3 * D), BF), sds((D, 3 * D + HALF), BF)],
        scratch_shapes=[
            pltpu.VMEM((D, 3 * D), F32),
            pltpu.VMEM((2, 9, 8, HALF), F32),
            pltpu.VMEM((8, 3 * D), F32),
            pltpu.VMEM((LONG, D), F32),
            pltpu.VMEM((2 * PAIRS * (QROWS + 8), HALF), F32),
            pltpu.VMEM((4, QROWS, HALF), F32),
            pltpu.VMEM((2 * PAIRS, QROWS + 2 * EDGE, HALF), F32),
            pltpu.VMEM((4, 3, QROWS, HALF), F32),
            pltpu.VMEM((ROWS, 3 * D), F32),
            pltpu.VMEM((56, HALF), F32),
            pltpu.VMEM((D, HALF), F32),
        ],
        compiler_params=params(),
        name="back",
    )(*blocks, *consts)


def run_input(tokens_in, dqkv, dx, w_qkv, table, low, high, out=None):
    own = pl.BlockSpec((TOK_IMG, D), lambda i: (low + i, 0))
    rows = pl.BlockSpec((1, ROWS, 3 * D), lambda i: (low + i, 0, 0))
    ends = [] if out is None else [out]
    return pl.pallas_call(
        input_kernel,
        grid=(high - low,),
        in_specs=[own, rows, own, whole(w_qkv.shape), whole(table.shape)]
        + [pl.BlockSpec(memory_space=pl.ANY) for _ in ends],
        out_specs=own,
        out_shape=sds(tokens_in.shape, F32),
        input_output_aliases={5: 0} if ends else {},
        compiler_params=params(),
        cost_estimate=pl.CostEstimate(
            flops=(high - low) * 2 * ROWS * 3 * D * D,
            bytes_accessed=(high - low) * ROWS * D * 18,
            transcendentals=0,
        ),
        name="input_grad",
    )(tokens_in, dqkv, dx, w_qkv, table, *ends)


def moments(grad, first, second):
    first_new = BETA_ONE * first + (1.0 - BETA_ONE) * grad
    second_new = BETA_TWO * second + (1.0 - BETA_TWO) * grad * grad
    direction = (
        first_new
        / (1.0 - BETA_ONE**STEP)
        / (jnp.sqrt(second_new / (1.0 - BETA_TWO**STEP)) + ADAM_EPS)
    )
    return (first_new, second_new, direction)


MATRICES = (slice(0, 3 * D), slice(3 * D, 4 * D), slice(4 * D, 4 * D + FF))


def lane_sums(values):
    column = jnp.sum(values * values, axis=0, keepdims=True)
    parts = [column[:, at : at + HALF] for at in range(0, column.shape[1], HALF)]
    return functools.reduce(jnp.add, parts)


def moment_kernel(
    gq_ref,
    gq_other_ref,
    gl_ref,
    gl_other_ref,
    ww_ref,
    wm_ref,
    wv_ref,
    dw_ref,
    dm_ref,
    dv_ref,
    wf_ref,
    ws_ref,
    wu_ref,
    df_ref,
    ds_ref,
    du_ref,
    sq_ref,
):
    for lanes, own, other in (
        (slice(0, 3 * D), gq_ref[:, : 3 * D], gq_other_ref[:, : 3 * D]),
        (slice(3 * D, 4 * D + FF), gl_ref[:, : D + FF], gl_other_ref[:, : D + FF]),
    ):
        first, second, way = moments(own + other, wm_ref[:, lanes], wv_ref[:, lanes])
        wf_ref[:, lanes] = first
        ws_ref[:, lanes] = second
        wu_ref[:, lanes] = way + DECAY * ww_ref[:, lanes]
    count = ww_ref.shape[0]
    for part in range(FF // D):
        lanes = slice(D + FF + part * D, D + FF + (part + 1) * D)
        own = slice(part * count, (part + 1) * count)
        grad = gl_ref[:, lanes] + gl_other_ref[:, lanes]
        first, second, way = moments(grad, dm_ref[own, :], dv_ref[own, :])
        df_ref[own, :] = first
        ds_ref[own, :] = second
        du_ref[own, :] = way + DECAY * dw_ref[own, :]
    for base, wide, down in ((0, ww_ref, dw_ref), (4, wu_ref, du_ref)):
        for at, lanes in enumerate(MATRICES):
            sq_ref[base + at : base + at + 1, :] = lane_sums(wide[:, lanes])
        sq_ref[base + 3 : base + 4, :] = lane_sums(down[...])


def update_kernel(
    sq_ref,
    ww_ref,
    wu_ref,
    we_ref,
    dw_ref,
    du_ref,
    de_ref,
    wn_ref,
    wa_ref,
    dn_ref,
    da_ref,
    norm_ref,
):
    total = jnp.sum(jnp.sum(sq_ref[...], axis=0), axis=1, keepdims=True)
    norm = jnp.sqrt(total)
    row = lax.broadcasted_iota(jnp.int32, (8, HALF), 0)
    lane = lax.broadcasted_iota(jnp.int32, (8, HALF), 1)
    for half in range(2):
        own = jnp.where(row == lane + 4 * half, norm, 0.0)
        norm_ref[half : half + 1, :] = jnp.sum(own, axis=0, keepdims=True)[:, 0:4]
    ratio = norm[0:4] / norm[4:8]
    keep = min(EMA_CEILING, (1.0 + STEP) / (10.0 + STEP))
    for at, lanes in enumerate(MATRICES):
        new = ww_ref[:, lanes] - (RATE * ratio[at : at + 1]) * wu_ref[:, lanes]
        wn_ref[:, lanes] = new
        wa_ref[:, lanes] = keep * we_ref[:, lanes] + (1.0 - keep) * new
    new = dw_ref[...] - (RATE * ratio[3:4]) * du_ref[...]
    dn_ref[...] = new
    da_ref[...] = keep * de_ref[...] + (1.0 - keep) * new


def plain(kernel, name, out_shape, *operands):
    small = pltpu.CompilerParams(vmem_limit_bytes=8 * 1024 * 1024)
    return pl.pallas_call(kernel, out_shape=out_shape, compiler_params=small, name=name)(*operands)


def to_other(values):
    return lax.ppermute(values, "dp", [(0, 1), (1, 0)])


def copies(values, count):
    return jnp.broadcast_to(values[None], (count,) + values.shape)


def send_terms(values, count):
    return lax.all_to_all(values.reshape(count, -1, values.shape[-1]), "fsdp", 0, 0)


def add_terms(terms):
    return jnp.sum(terms.astype(F32), axis=0)


def on_device(
    count,
    tokens_in,
    cotangent,
    crop_count,
    wide_w,
    wide_m,
    wide_v,
    wide_ema,
    down_w,
    down_m,
    down_v,
    down_ema,
    small_p,
    small_m,
    small_v,
    small_ema,
):
    rows = wide_w.shape[0]
    narrow = small_p.shape[0] // rows
    small_low = jnp.pad(small_p.astype(BF).reshape(rows, narrow), ((0, 0), (0, HALF - narrow)))
    first = jnp.concatenate([wide_w[:, : 3 * D].astype(BF), small_low], axis=1)
    first = send_terms(copies(first, count), count)
    hat, late_all = run_norm(tokens_in, wide_w, down_w, count)
    first, late_all, hat = lax.optimization_barrier((first, late_all, hat))
    first = first.reshape(D, -1)
    late_all = send_terms(late_all, count).reshape(D, -1)
    table, kernels = small_tables(first[:, 3 * D : 3 * D + narrow].astype(F32).reshape(-1))
    side = np.stack([tap_matrix(kind) for kind in range(3)])
    side = bf(side.transpose(0, 2, 1, 3).reshape(3, QROWS, 9 * QROWS))
    hat, att, win, e, il, o = run_attend(hat, first, table, kernels, side)
    block_out, dx, datt, g_late, sums, b_up = run_feed(
        rows, crop_count, tokens_in, cotangent, att, late_all, table
    )
    late = send_terms(g_late, count)
    spans = small_spans(rows, narrow)
    dqkv, g_last = run_back(
        spans, [datt, win, e, il, o, hat], first, table, kernels, sums, b_up, side
    )
    late, g_last = lax.optimization_barrier((late, g_last))
    late = add_terms(late)
    last = send_terms(g_last, count)
    images = dqkv.shape[0]
    begin = images * 3 // 4
    grad_in = run_input(tokens_in, dqkv, dx, first, table, 0, begin)
    last, grad_in = lax.optimization_barrier((last, grad_in))
    last = add_terms(last)
    last_other = to_other(last)
    late_other = to_other(late)
    wide_like, down_like = sds(wide_w.shape, F32), sds(down_w.shape, F32)
    wide_first, wide_second, wide_upd, down_first, down_second, down_upd, squares = plain(
        moment_kernel,
        "moment",
        [wide_like] * 3 + [down_like] * 3 + [sds((8, HALF), F32)],
        *(last, last_other, late, late_other),
        *(wide_w, wide_m, wide_v, down_w, down_m, down_v),
    )
    squares, grad_in = lax.optimization_barrier((copies(squares, count), grad_in))
    squares = send_terms(squares, count)
    grad_in = run_input(tokens_in, dqkv, dx, first, table, begin, images, grad_in)
    squares, grad_in = lax.optimization_barrier((squares, grad_in))
    wide_new, wide_avg, down_new, down_avg, norms = plain(
        update_kernel,
        "update",
        [wide_like] * 2 + [down_like] * 2 + [sds((2, 4), F32)],
        *(squares, wide_w, wide_upd, wide_ema, down_w, down_upd, down_ema),
    )
    shard_small = (last + last_other)[: spans[0][1], 3 * D :].reshape(-1)
    offset = lax.axis_index("fsdp") * (rows * narrow) % HALF
    shard_small = lax.dynamic_slice(shard_small, (offset,), (rows * narrow,))
    small_first, small_second, small_dir = moments(shard_small, small_m, small_v)
    small_new = small_p - RATE * small_dir
    ema_keep = min(EMA_CEILING, (1.0 + STEP) / (10.0 + STEP))
    small_avg = ema_keep * small_ema + (1.0 - ema_keep) * small_new
    return (
        block_out,
        grad_in,
        wide_new,
        wide_first,
        wide_second,
        wide_avg,
        down_new,
        down_first,
        down_second,
        down_avg,
        small_new,
        small_first,
        small_second,
        small_avg,
        norms,
    )


def solution(mesh):
    tok, row, vec = P(("dp", "fsdp"), None), P("fsdp", None), P("fsdp")
    in_specs = (tok, tok, P(("dp", "fsdp"))) + (row,) * 8 + (vec,) * 4
    out_specs = (tok, tok) + (row,) * 8 + (vec,) * 4 + (P(),)
    return jax.shard_map(
        functools.partial(on_device, mesh.shape["fsdp"]),
        mesh=mesh,
        in_specs=in_specs,
        out_specs=out_specs,
        check_vma=False,
    )
```

```python
import functools

import jax
import jax.numpy as jnp
import numpy as np
from jax import lax
from jax.experimental import pallas as pl
from jax.experimental.pallas import tpu as pltpu
from jax.sharding import PartitionSpec as P

D = 256
FF = 1024
HEAD = 32
STRIPE = 7
GRID_L = 14
GRID_S = 6
SMALL = 8
STEP = 10
TOK_IMG = 680

EPSILON = 1e-05
BETA_ONE = 0.9
BETA_TWO = 0.999
ADAM_EPS = 1e-06
DECAY = 0.05
RATE = 0.25
EMA_CEILING = 0.9999

ROWS = 688
BIG = 2 * GRID_L * GRID_L
PAIRS = 7
WIN = 128
QROWS = 112
HALF = 128
HEADS = 4
SCALE = HEAD**-0.5
LOG2E = 1.4426950408889634
LN2 = 0.6931471805599453
ROOT = 2**-0.5
CHUNKS = ((0, 240), (240, 464), (464, 688))
LONG = 744
EDGE = 16
COPIES = (3, 3, 2)
TAPS = tuple((dy, dx) for dy in (-1, 0, 1) for dx in (-1, 0, 1))
ORDER = (0, 2, 1, 3, 4, 5, 6)
VMEM = 60 * 1024 * 1024

BF = jnp.bfloat16
F32 = jnp.float32


def kind_of(pair):
    return 0 if pair < 2 else 1 if pair < 4 else 2


def branch_of(pair, member):
    return 0 if pair < 2 else 1 if pair < 4 else member


def first_of(pair, member):
    if pair < 2:
        return pair * GRID_L * GRID_L + member * STRIPE * GRID_L
    if pair < 4:
        return (pair - 2) * GRID_L * GRID_L + member * STRIPE
    return BIG + (pair - 4) * COPIES[0] * GRID_S * GRID_S


def tokens_of(pair):
    return STRIPE * GRID_L if pair < 4 else COPIES[pair - 4] * GRID_S * GRID_S


def shape_of(kind):
    return ((STRIPE, GRID_L), (GRID_L, STRIPE), (GRID_S, GRID_S))[kind]


def edge_masks():
    masks, places = [], {}
    for kind in range(3):
        high, broad = shape_of(kind)
        size = high * broad
        for dy, dx in TAPS:
            if (dy, dx) == (0, 0) or (kind < 2 and (dy != 0 or dx == 0)):
                continue
            mask = np.zeros((QROWS, HALF), np.float32)
            for at in range(size * (1 if kind < 2 else COPIES[0])):
                r, c = divmod(at % size, broad)
                mask[at] = 0 <= r + dy < high and 0 <= c + dx < broad
            places[kind, dy, dx] = len(masks)
            masks.append(mask)
    return np.stack(masks), places


def tap_matrix(kind):
    shape = shape_of(kind)
    copies = 1 if kind < 2 else COPIES[0]
    size = shape[0] * shape[1]
    out = np.zeros((9, QROWS, QROWS), np.float32)
    for copy in range(copies):
        for r in range(shape[0]):
            for c in range(shape[1]):
                for tap in range(9):
                    rr, cc = r + tap // 3 - 1, c + tap % 3 - 1
                    if 0 <= rr < shape[0] and 0 <= cc < shape[1]:
                        out[tap, copy * size + r * shape[1] + c, copy * size + rr * shape[1] + cc] = 1
    return out


def mask_operands():
    size = GRID_S * GRID_S
    rows = np.zeros((3, 2, QROWS, HALF), np.float32)
    keys = np.zeros((3, HALF // 2, WIN), np.float32)
    for kind, crops in ((0, 1), (1, 3), (2, 2)):
        count = STRIPE * GRID_L if kind == 0 else crops * size
        each = count // crops
        for at in range(QROWS):
            rows[kind, 0, at, HALF // 2 + (at // each if at < count else 0)] = 1
        for at in range(WIN):
            for crop in range(crops):
                if at >= count or at // each != crop:
                    keys[kind, crop, at] = -1e30
    rows[:, 1, :, : HALF // 2] = rows[:, 0, :, HALF // 2 :]
    return rows, np.tile(keys, (1, 1, 2))


def bf(array):
    return jnp.asarray(array, BF)


def dot(left, right):
    return jnp.dot(left, right, preferred_element_type=F32)


def dot_nt(left, right):
    return lax.dot_general(left, right, (((1,), (1,)), ((), ())), preferred_element_type=F32)


def dot_tn(left, right):
    return lax.dot_general(left, right, (((0,), (0,)), ((), ())), preferred_element_type=F32)


def normalise(values):
    center = values - jnp.mean(values, axis=-1, keepdims=True)
    spread = jnp.mean(center * center, axis=-1, keepdims=True)
    scale = lax.rsqrt(spread + EPSILON)
    return center * scale, scale


def norm_back(grad_hat, hat, scale):
    mean_grad = jnp.mean(grad_hat, axis=-1, keepdims=True)
    mean_dot = jnp.mean(grad_hat * hat, axis=-1, keepdims=True)
    return scale * (grad_hat - mean_grad - hat * mean_dot)


def rows_of(ref, low, high):
    if high <= TOK_IMG:
        return ref[low:high, :]
    tail = jnp.zeros((high - TOK_IMG, ref.shape[1]), F32)
    return jnp.concatenate([ref[low:TOK_IMG, :], tail], axis=0)


def store_rows(ref, low, high, values):
    last = min(high, TOK_IMG)
    ref[low:last, :] = values[: last - low]


def with_ones(turned):
    return jnp.concatenate([turned, jnp.ones((16, turned.shape[1]), turned.dtype)], axis=0)


def fold(values):
    return jnp.sum(values.reshape(values.shape[0] // 8, 8, values.shape[1]), axis=0)


def head_lanes(head):
    lanes = lax.broadcasted_iota(jnp.int32, (1, HALF), 1)
    return jnp.where(lanes // HEAD == head, 1.0, 0.0).astype(BF)


def by_head(values):
    return jnp.concatenate([values * head_lanes(h) for h in range(HEADS)], axis=0)


def lane_half(upper):
    lanes = lax.broadcasted_iota(jnp.int32, (1, HALF), 1)
    return jnp.where((lanes >= HALF // 2) == upper, 1.0, 0.0).astype(BF)


def two_heads(turned, pair):
    low = pair * 2 * HEAD
    none = jnp.zeros((HEAD, WIN), turned.dtype)
    first = jnp.concatenate([turned[low : low + HEAD], none], axis=1)
    second = jnp.concatenate([none, turned[low + HEAD : low + 2 * HEAD]], axis=1)
    return jnp.concatenate([first, second], axis=0)


def by_two_heads(left, other, turned, added):
    low, high = lane_half(False), lane_half(True)
    first = dot(
        left * low + other[0], jnp.concatenate([two_heads(turned, 0), added], axis=0)
    )
    second = dot(
        left * high + other[1], jnp.concatenate([added, two_heads(turned, 1)], axis=0)
    )
    return [first[:, :WIN], first[:, WIN:], second[:, :WIN], second[:, WIN:]]


def head_block(rows):
    return jnp.concatenate(
        [jnp.broadcast_to(head_lanes(h), (rows, HALF)) for h in range(HEADS)], axis=0
    )


def first_rows(values, count):
    low = count // 16 * 16
    if low >= values.shape[0]:
        return values
    row = lax.broadcasted_iota(jnp.int32, (values.shape[0] - low, 1), 0)
    tail = jnp.where(row < count - low, values[low:], 0.0)
    return jnp.concatenate([values[:low], tail], axis=0)


def pieces_of(pair, member):
    low = first_of(pair, member)
    return [(low + r * GRID_L, r * STRIPE) for r in range(GRID_L)]


def pipelined(stages, order, extra=()):
    extra = dict(extra)
    state = {item: {} for item in order}
    for turn in range(len(order) + max(lag for lag, _ in stages)):
        if turn in extra:
            extra[turn]()
        running = []
        for lag, stage in stages:
            if 0 <= turn - lag < len(order):
                item = order[turn - lag]
                running.append(stage(item, state[item]))
        while running:
            running = [stage for stage in running if next(stage, True) is None]


def norm_kernel(x_ref, wide_ref, down_ref, hat_ref, late_ref):
    for low in range(0, x_ref.shape[0], TOK_IMG // 5):
        hat_ref[low : low + TOK_IMG // 5, :] = normalise(x_ref[low : low + TOK_IMG // 5, :])[0]

    @pl.when(pl.program_id(0) == 0)
    def _():
        rows = wide_ref.shape[0]
        pieces = [wide_ref[:, 3 * D :]]
        pieces += [down_ref[at : at + rows, :] for at in range(0, down_ref.shape[0], rows)]
        late = jnp.concatenate(pieces, axis=1).astype(BF)
        for owner in range(late_ref.shape[0]):
            late_ref[owner] = late


def attend_kernel(
    x_ref,
    w_ref,
    s_ref,
    k_ref,
    tap_ref,
    mrow_ref,
    mkey_ref,
    hat_ref,
    att_ref,
    win_ref,
    e_ref,
    il_ref,
    o_ref,
    qkv_scr,
    turn_scr,
    back_scr,
    att_scr,
):
    @pl.when(pl.program_id(0) == 0)
    def _():
        for branch in range(2):
            qkv_scr[branch, ROWS:, :] = jnp.zeros((LONG - ROWS, 3 * HALF), F32)
        turn_scr[...] = jnp.zeros_like(turn_scr)
        att_scr[TOK_IMG:, :] = jnp.zeros((ROWS - TOK_IMG, D), F32)

    gain, shift = s_ref[0:1, :], s_ref[1:2, :]
    ones = head_block(WIN)

    def project(chunk):
        low, high = CHUNKS[chunk]
        hat = rows_of(x_ref, low, high)
        hat_ref[0, low:high, :] = hat.astype(BF)
        a = (hat * gain + shift).astype(BF)
        for part in range(3):
            lanes = slice(part * D, (part + 1) * D)
            piece = dot(a, w_ref[:, lanes]) + s_ref[2 + part : 3 + part, :]
            if part == 0:
                piece = piece * (SCALE * LOG2E)
            for branch in range(2):
                qkv_scr[branch, low:high, part * HALF : (part + 1) * HALF] = piece[
                    :, branch * HALF : (branch + 1) * HALF
                ]

    none = jnp.zeros((WIN - QROWS, HALF), BF)

    def cut(pair, state):
        for member in range(2):
            at = 2 * pair + member
            if kind_of(pair) == 1:
                for source, target in pieces_of(pair, member):
                    turn_scr[at - 4, target : target + STRIPE, :] = qkv_scr[
                        1, source : source + STRIPE, :
                    ]
                window = turn_scr[at - 4, :QROWS, :]
            else:
                low = first_of(pair, member)
                window = qkv_scr[branch_of(pair, member), low : low + QROWS, :]
            window = window.astype(BF)
            win_ref[0, at] = window
            state[member] = [window[:, part * HALF : (part + 1) * HALF] for part in range(3)]
            yield

    def score(pair, state):
        mask = 0 if pair < 4 else 1 if pair < 6 else 2
        for member in range(2):
            q, k, v = state[member]
            k = jnp.concatenate([k, none], axis=0).T
            rows = mrow_ref[mask, 0], mrow_ref[mask, 1]
            state[member] = v, by_two_heads(q, rows, k, mkey_ref[mask])
            yield

    def soften(pair, state):
        for member in range(2):
            v, scores = state[member]
            exps = []
            for part in scores:
                peak = jnp.max(part, axis=-1, keepdims=True)
                exps.append(jnp.exp2(part - peak).astype(BF))
            e = jnp.concatenate(exps, axis=1)
            e_ref[0, 2 * pair + member] = e
            state[member] = v, e
            yield

    def mix(pair, state):
        taps = []
        for member in range(2):
            v, e = state[member]
            low = k_ref[branch_of(pair, member)].astype(BF)
            keys = jnp.concatenate([v, none], axis=0)
            state[member] = dot(e, jnp.concatenate([by_head(keys), ones], axis=1))
            taps.append(jnp.concatenate([v * low[tap : tap + 1] for tap in range(9)], axis=0))
            yield
        state[2] = dot(tap_ref[kind_of(pair)], jnp.concatenate(taps, axis=1))
        yield

    def put(pair, state):
        for member in range(2):
            at = 2 * pair + member
            branch = branch_of(pair, member)
            lanes = slice(branch * HALF, (branch + 1) * HALF)
            both = state[member]
            inv = 1.0 / both[:, HALF:]
            o = both[:, :HALF] * inv
            il_ref[0, at] = inv
            o_ref[0, at] = o.astype(BF)
            conv = state[2][:, member * HALF : (member + 1) * HALF]
            piece = o + k_ref[branch, 9:10, :] + conv
            if kind_of(pair) == 1:
                back_scr[at - 4] = piece
                for source, target in pieces_of(pair, member):
                    att_scr[source : source + STRIPE, lanes] = back_scr[
                        at - 4, target : target + STRIPE, :
                    ]
            else:
                low, count = first_of(pair, member), tokens_of(pair)
                att_scr[low : low + count, lanes] = piece[:count]
            yield

    project(0)
    extra = {1: functools.partial(project, 1), 3: functools.partial(project, 2)}
    stages = enumerate((cut, score, soften, mix, put))
    pipelined(tuple(stages), ORDER, extra)
    att_ref[0] = att_scr[...].astype(BF)


def gelu_parts(v):
    above = lax.erf(v) + 1.0
    decay = jnp.exp2((v * v) * -LOG2E)
    return v * above, above + (v * decay) * (2 / np.sqrt(np.pi))


def beside(*streams):
    left = [[list(stream), 0] for stream in streams]
    total = max((len(steps) for steps, _ in left), default=0)
    for at in range(total):
        for entry in left:
            steps, done = entry
            goal = -(-len(steps) * (at + 1) // total)
            for step in steps[done:goal]:
                step()
            entry[1] = goal


def weight_terms(grad, weight, bias):
    terms = []
    for value in (weight * bias,) if grad is None else (weight * grad, weight * bias):
        column = jnp.sum(value, axis=1, keepdims=True)
        terms.append(jnp.broadcast_to(column, (D, HALF)).T[0:1, :])
    return terms


def down_blocks(shard):
    parts = FF // D
    return [(i, part, (i * parts + part) * shard) for i in range(D // shard) for part in range(parts)]


def feed_kernel(
    shard,
    cnt_ref,
    x_ref,
    c_ref,
    att_ref,
    w_ref,
    s_ref,
    out_ref,
    dx_ref,
    datt_ref,
    pack_ref,
    sums_ref,
    bup_ref,
    rs_scr,
    x1_scr,
    gup_scr,
    gdn_scr,
    gout_scr,
    turn_scr,
    pack_scr,
    down_scr,
):
    image = pl.program_id(0)

    @pl.when(image == 0)
    def _():
        for ref in (gup_scr, gdn_scr, gout_scr, sums_ref, bup_ref):
            ref[...] = jnp.zeros_like(ref)
        pack_scr[...] = w_ref[:, D + FF :].astype(F32)
        for owner, part, low in down_blocks(shard):
            turn_scr[low : low + shard, :] = pack_scr[
                owner * shard : (owner + 1) * shard, part * D : (part + 1) * D
            ]
        down_scr[...] = turn_scr[...].astype(BF)

    bound = BIG + GRID_S * GRID_S * cnt_ref[image]
    bias_out, gain, shift = s_ref[15:16, :], s_ref[16:17, :], s_ref[17:18, :]
    lanes_of = [slice(part * D, (part + 1) * D) for part in range(FF // D)]
    count = 16
    rows = range(0, ROWS, count)
    biases = [s_ref[18 + part : 19 + part, :] * ROOT for part in range(FF // D)]
    sums = {}
    held = {}

    def add_sum(key, values, at, ref, *index):
        sums[key] = sums[key] + fold(values) if key in sums else fold(values)
        if at + count >= ROWS:
            ref[index] += sums[key]

    def keep(key, at, values):
        held.setdefault(key, []).append(values)
        if at + count >= ROWS:
            held[key] = jnp.concatenate(held[key], axis=0)

    def masked(at):
        row = at + lax.broadcasted_iota(jnp.int32, (count, 1), 0)
        return jnp.where(row < bound, rows_of(c_ref, at, at + count), 0.0)

    def cot(at):
        dy = masked(at)
        keep("dy", at, dy.astype(BF))
        add_sum("dy", dy, at, sums_ref, 0)

    def project():
        held["x1"] = dot(att_ref[0], w_ref[:, :D])

    def norm(at):
        own = slice(at, at + count)
        x1 = rows_of(x_ref, at, at + count) + held["x1"][own] + bias_out
        x1_scr[own, :] = x1
        hat, scale = normalise(x1)
        rs_scr[own, :] = scale
        keep("hat", at, hat.astype(BF))
        keep("h2", at, (hat * (gain * ROOT) + shift * ROOT).astype(BF))

    def hidden(part):
        cols = slice(D + part * D, D + (part + 1) * D)
        held["v", part] = dot(held["h2"], w_ref[:, cols])

    def hidden_back(part):
        held["dg", part] = dot_nt(held["dy"], down_scr[lanes_of[part], :])

    def gelu(part, at):
        own = slice(at, at + count)
        v = held["v", part][own] + biases[part]
        g, slope = gelu_parts(v)
        keep(("g", part), at, g.astype(BF))
        du = held["dg", part][own] * slope
        keep(("du", part), at, du.astype(BF))

    def gelus(part):
        return [functools.partial(gelu, part, at) for at in rows]

    def grad_up(part):
        both = dot(held["hat_t"], held["du", part])
        gup_scr[:, lanes_of[part]] += both[:D]
        bup_ref[:, lanes_of[part]] += both[D : D + 8]

    def grad_down(part):
        gdn_scr[:, lanes_of[part]] += dot(held["dy_t"], held["g", part])

    def joined(key, *parts):
        return jnp.concatenate([held[key, part] for part in parts], axis=1)

    half = FF // 2

    def out_first():
        held["out"] = dot(joined("g", 0, 1), down_scr[:half, :])

    def out_last():
        held["out"] += dot(joined("g", 2, 3), down_scr[half:, :])

    def out_store(at):
        own = slice(at, at + count)
        out = x1_scr[own, :] + held["out"][own] * ROOT + s_ref[22:23, :]
        store_rows(out_ref, at, at + count, out)

    def back_first():
        held["dh"] = dot_nt(joined("du", 0, 1), w_ref[:, D : D + half])

    def back_last():
        held["dh"] += dot_nt(joined("du", 2, 3), w_ref[:, D + half : D + FF])

    def norm_grad(at):
        own = slice(at, at + count)
        hat = held["hat"][own].astype(F32)
        dx = masked(at) + norm_back(held["dh"][own] * (gain * 0.5), hat, rs_scr[own, :])
        store_rows(dx_ref, at, at + count, dx)
        keep("dz", at, dx.astype(BF))
        add_sum("dz", dx, at, sums_ref, 1)

    def attention():
        datt = dot_nt(held["dz"], w_ref[:, :D])
        datt_ref[0] = datt.astype(BF)

    def grad_out():
        gout_scr[...] += dot_tn(att_ref[0], held["dz"])

    def each(step, *parts):
        return [functools.partial(step, part) for part in parts]

    def turn(key):
        held[key + "_t"] = held[key].T

    beside(each(cot, *rows), [project])
    turn("dy")
    beside(each(norm, *rows), each(hidden_back, 0, 1, 2, 3))
    turn("hat")
    held["hat_t"] = with_ones(held["hat_t"])
    hidden(0)
    beside(each(hidden, 1, 2, 3), gelus(0))
    beside(each(grad_up, 0) + each(grad_down, 0), gelus(1))
    beside([back_first] + each(grad_up, 1) + each(grad_down, 1), gelus(2))
    beside([out_first] + each(grad_up, 2) + each(grad_down, 2), gelus(3))
    back_last()
    beside([out_last] + each(grad_up, 3) + each(grad_down, 3), each(norm_grad, *rows))
    beside([attention, grad_out], each(out_store, *rows))

    @pl.when(image == pl.num_programs(0) - 1)
    def _():
        turn_scr[...] = gdn_scr[...].T * ROOT
        for owner, part, low in down_blocks(shard):
            pack_scr[owner * shard : (owner + 1) * shard, part * D : (part + 1) * D] = turn_scr[
                low : low + shard, :
            ]
        bup_ref[...] *= 0.5
        bias = bup_ref[0:1, :]
        grad = gup_scr[...] * 0.5
        terms = weight_terms(grad, w_ref[:, D : D + FF].astype(F32), bias)
        out_bias = jnp.sum(sums_ref[1], axis=0, keepdims=True)
        terms += weight_terms(None, w_ref[:, :D].astype(F32), out_bias)
        for at, term in enumerate(terms):
            sums_ref[2 + at, 0:1, :] = term
        columns = s_ref[15:23, :].T
        grad = columns[:, 1:2] * grad + columns[:, 2:3] * bias
        pack_ref[:, :D] = gout_scr[...].astype(BF)
        pack_ref[:, D : D + FF] = grad.astype(BF)
        pack_ref[:, D + FF :] = pack_scr[...].astype(BF)


def small_spans(shard, narrow):
    count = D // shard
    own = shard * narrow
    rows = max((own * (i + 1) - 1) // HALF - own * i // HALF + 1 for i in range(count))
    return [(own * i // HALF, rows) for i in range(count)]


def back_kernel(
    spans,
    places,
    datt_ref,
    win_ref,
    e_ref,
    il_ref,
    o_ref,
    hat_ref,
    w_ref,
    s_ref,
    k_ref,
    feed_ref,
    bup_ref,
    tap_ref,
    edge_ref,
    dqkv_ref,
    pack_ref,
    g_scr,
    kern_scr,
    bias_scr,
    datt_scr,
    grad_scr,
    turn_scr,
    pad_scr,
    back_scr,
    dqkv_scr,
    small_scr,
    pack_scr,
):
    image = pl.program_id(0)

    @pl.when(image == 0)
    def _():
        for ref in (g_scr, kern_scr, bias_scr, turn_scr, pad_scr, small_scr, pack_scr):
            ref[...] = jnp.zeros_like(ref)
        datt_scr[ROWS:, :] = jnp.zeros((LONG - ROWS, D), F32)
        dqkv_scr[TOK_IMG:, :] = jnp.zeros((ROWS - TOK_IMG, 3 * D), F32)

    for low, high in CHUNKS:
        datt_scr[low:high, :] = datt_ref[0, low:high, :].astype(F32)
    minus = two_heads(jnp.full((HALF, WIN), -1.0, BF), 0)
    none = jnp.zeros((WIN - QROWS, HALF), BF)

    def weigh(pair, state):
        for member in range(2):
            at = 2 * pair + member
            branch = branch_of(pair, member)
            lanes = slice(branch * HALF, (branch + 1) * HALF)
            if kind_of(pair) == 1:
                for source, target in pieces_of(pair, member):
                    turn_scr[at - 4, target : target + STRIPE, :] = datt_scr[
                        source : source + STRIPE, lanes
                    ]
                grad = turn_scr[at - 4]
            else:
                low = first_of(pair, member)
                grad = first_rows(datt_scr[low : low + QROWS, lanes], tokens_of(pair))
            grad_scr[at * QROWS : (at + 1) * QROWS, :] = grad
            v = win_ref[0, at, :, 2 * HALF :]
            pad_scr[at, EDGE : EDGE + QROWS, :] = first_rows(v.astype(F32), tokens_of(pair))
            dn = grad * il_ref[0, at]
            z = pltpu.roll(dn * o_ref[0, at].astype(F32), HALF // 2, 1).astype(BF)
            dn = dn.astype(BF)
            rows = z * lane_half(True), z * lane_half(False)
            v = jnp.concatenate([v, none], axis=0).T
            state[member] = grad, dn, by_two_heads(dn, rows, v, minus)
            yield

    def score(pair, state):
        for member in range(2):
            grad, dn, weighed = state[member]
            e = e_ref[0, 2 * pair + member]
            ds = jnp.concatenate(weighed, axis=1).astype(BF) * e
            state[member] = grad, dn, ds, e
            yield

    def spread(pair, state):
        kind = kind_of(pair)
        taps = []
        for member in range(2):
            grad, dn, ds, e = state[member]
            at = 2 * pair + member
            kernel = k_ref[branch_of(pair, member)].astype(BF)
            q = win_ref[0, at, :, 0:HALF]
            k = jnp.concatenate([win_ref[0, at, :, HALF : 2 * HALF], none], axis=0)
            dq = dot(ds, by_head(k))
            row = 2 * PAIRS * QROWS + 8 * at
            grad_scr[row : row + 8, :] = dq[:8]
            q_t, dn_t = q.T, dn.T
            dk, dv = [], []
            for half in range(2):
                lanes = slice(2 * half * WIN, 2 * (half + 1) * WIN)
                own = slice(2 * half * HEAD, 2 * (half + 1) * HEAD)
                for parts, left, right in ((dk, q_t, ds), (dv, dn_t, e)):
                    both = dot(left[own], right[:, lanes])
                    parts += [both[:HEAD, :WIN], both[HEAD:, WIN:]]
            state[member] = dq, dk, dv
            low = grad.astype(BF)
            taps.append(
                jnp.concatenate([low * kernel[8 - tap : 9 - tap] for tap in range(9)], axis=0)
            )
            yield
        state[2] = dot(tap_ref[kind], jnp.concatenate(taps, axis=1))
        yield

    def kernels(pair, state):
        kind = kind_of(pair)
        broad = shape_of(kind)[1]
        for member in range(2):
            at = 2 * pair + member
            base = pl.multiple_of(at * QROWS + image // 4096 * 8, 8)
            totals = [jnp.zeros((8, HALF), F32)] * 9
            for low in range(0, tokens_of(pair), 8):
                own = slice(low, low + 8)
                grad = grad_scr[pl.ds(pl.multiple_of(base + low, 8), 8), :]
                sides = {}
                for tap, (dy, dx) in enumerate(TAPS):
                    place = places.get((kind, 0 if kind < 2 else dy, dx))
                    if place not in sides:
                        mask = 1.0 if place is None else edge_ref[place, own, :]
                        sides[place] = grad * mask
                    start = EDGE + low + dy * broad + dx
                    totals[tap] = totals[tap] + sides[place] * pad_scr[at, start : start + 8, :]
            for tap in range(9):
                kern_scr[branch_of(pair, member), tap] += totals[tap]
            yield

    def put(pair, state):
        for member in range(2):
            at = 2 * pair + member
            branch = branch_of(pair, member)
            dq, dk, dv = state[member]
            dk = jnp.concatenate(dk, axis=0).T[:QROWS] * LN2
            dv = jnp.concatenate(dv, axis=0).T[:QROWS]
            dv = dv + state[2][:, member * HALF : (member + 1) * HALF]
            for part, piece in enumerate((dq * SCALE, dk, dv)):
                lanes = slice(part * D + branch * HALF, part * D + (branch + 1) * HALF)
                if kind_of(pair) == 1:
                    back_scr[at - 4, part] = piece
                    for source, target in pieces_of(pair, member):
                        dqkv_scr[source : source + STRIPE, lanes] = back_scr[
                            at - 4, part, target : target + STRIPE, :
                        ]
                else:
                    low, count = first_of(pair, member), tokens_of(pair)
                    dqkv_scr[low : low + count, lanes] = piece[:count]
            yield

    pipelined(((3, kernels), (0, weigh), (1, score), (2, spread), (3, put)), ORDER)
    dqkv = dqkv_scr[...].astype(BF)
    dqkv_ref[0] = dqkv
    both = dot(with_ones(hat_ref[0].T), dqkv)
    g_scr[...] += both[:D]
    bias_scr[...] += both[D : D + 8]

    @pl.when(image == pl.num_programs(0) - 1)
    def _():
        def put(row, terms):
            for at in range(0, terms.shape[1], HALF):
                small_scr[row : row + 1, :] = terms[:, at : at + HALF]
                row += 1

        total = lambda terms: jnp.sum(terms, axis=0, keepdims=True)
        bias = bias_scr[0:1, :]
        gain, shift = weight_terms(g_scr[...], w_ref[:, : 3 * D].astype(F32), bias)
        put(0, gain)
        put(2, shift)
        put(4, bias)
        for tap in range(9):
            for branch in range(2):
                put(10 + 2 * tap + branch, total(kern_scr[branch, tap]))
        for row, entry in ((30, 1), (44, 0)):
            put(row, total(feed_ref[entry]))
        for row, entry in ((32, 2), (34, 3), (28, 4)):
            put(row, feed_ref[entry, 0:1, :])
        put(36, bup_ref[0:1, :])
        for owner, (row, rows) in enumerate(spans):
            shard = D // len(spans)
            pack_scr[owner * shard : owner * shard + rows, :] = small_scr[row : row + rows, :]
        columns = s_ref[0:8, :].T
        grad = columns[:, 0:1] * g_scr[...] + columns[:, 1:2] * bias
        pack_ref[:, : 3 * D] = grad.astype(BF)
        pack_ref[:, 3 * D :] = pack_scr[...].astype(BF)


def input_kernel(x_ref, dqkv_ref, dx_ref, w_ref, s_ref, *out_refs):
    out_ref = out_refs[-1]
    for low, high in CHUNKS:
        dh = dot_nt(dqkv_ref[0, low:high, :], w_ref[:, : 3 * D])
        hat, scale = normalise(rows_of(x_ref, low, high))
        grad = rows_of(dx_ref, low, high) + norm_back(dh * s_ref[0:1, :], hat, scale)
        store_rows(out_ref, low, high, grad)


def whole(shape):
    return pl.BlockSpec(shape, lambda i, *_: (0,) * len(shape))


def image_of(shape):
    return pl.BlockSpec((1,) + shape, lambda i, *_: (i,) + (0,) * len(shape))


def tokens():
    return pl.BlockSpec((TOK_IMG, D), lambda i, *_: (i, 0))


def params(room=0):
    return pltpu.CompilerParams(
        vmem_limit_bytes=VMEM - room * 1024 * 1024, dimension_semantics=("arbitrary",)
    )


def sds(shape, dtype):
    return jax.ShapeDtypeStruct(shape, dtype)


def small_tables(small):
    rows = small.reshape(-1, D)
    taps = rows[5:15].reshape(10, 2, HALF).transpose(1, 0, 2)
    return rows, taps


def run_norm(tokens_in, wide, down, count):
    rows = TOK_IMG * 2
    block = pl.BlockSpec((rows, D), lambda i: (i, 0))
    late = (count, wide.shape[0], D + 2 * FF)
    return pl.pallas_call(
        norm_kernel,
        grid=(tokens_in.shape[0] // rows,),
        in_specs=[block, whole(wide.shape), whole(down.shape)],
        out_specs=[block, whole(late)],
        out_shape=[sds(tokens_in.shape, F32), sds(late, BF)],
        compiler_params=params(),
        name="norm",
    )(tokens_in, wide, down)


def run_attend(tokens_in, w_qkv, table, kernels, side):
    images = tokens_in.shape[0] // TOK_IMG
    mrow, mkey = mask_operands()
    consts = [table, kernels, side, bf(mrow), bf(mkey)]
    outs = [
        ((ROWS, D), BF),
        ((ROWS, D), BF),
        ((2 * PAIRS, QROWS, 3 * HALF), BF),
        ((2 * PAIRS, QROWS, HEADS * WIN), BF),
        ((2 * PAIRS, QROWS, HALF), F32),
        ((2 * PAIRS, QROWS, HALF), BF),
    ]
    return pl.pallas_call(
        attend_kernel,
        grid=(images,),
        in_specs=[tokens(), whole(w_qkv.shape)] + [whole(c.shape) for c in consts],
        out_specs=[image_of(shape) for shape, _ in outs],
        out_shape=[sds((images,) + shape, dtype) for shape, dtype in outs],
        scratch_shapes=[
            pltpu.VMEM((2, LONG, 3 * HALF), F32),
            pltpu.VMEM((4, QROWS, 3 * HALF), F32),
            pltpu.VMEM((4, QROWS, HALF), F32),
            pltpu.VMEM((ROWS, D), F32),
        ],
        compiler_params=params(-3),
        name="attend",
    )(tokens_in, w_qkv, *consts)


def run_feed(shard, counts, tokens_in, cotangent, att, wide, table):
    images = tokens_in.shape[0] // TOK_IMG
    return pl.pallas_call(
        functools.partial(feed_kernel, shard),
        grid_spec=pltpu.PrefetchScalarGridSpec(
            num_scalar_prefetch=1,
            grid=(images,),
            in_specs=[
                tokens(),
                tokens(),
                image_of((ROWS, D)),
                whole(wide.shape),
                whole(table.shape),
            ],
            out_specs=[
                tokens(),
                tokens(),
                image_of((ROWS, D)),
                whole((D, D + 2 * FF)),
                whole((5, 8, D)),
                whole((8, FF)),
            ],
            scratch_shapes=[
                pltpu.VMEM((ROWS, 1), F32),
                pltpu.VMEM((ROWS, D), F32),
                pltpu.VMEM((D, FF), F32),
                pltpu.VMEM((D, FF), F32),
                pltpu.VMEM((D, D), F32),
                pltpu.VMEM((FF, D), F32),
                pltpu.VMEM((D, FF), F32),
                pltpu.VMEM((FF, D), BF),
            ],
        ),
        out_shape=[
            sds(tokens_in.shape, F32),
            sds(tokens_in.shape, F32),
            sds((images, ROWS, D), BF),
            sds((D, D + 2 * FF), BF),
            sds((5, 8, D), F32),
            sds((8, FF), F32),
        ],
        compiler_params=params(),
        name="feed",
    )(counts, tokens_in, cotangent, att, wide, table)


def run_back(spans, blocks, w_qkv, table, kernels, sums, b_up, side):
    images = blocks[0].shape[0]
    masks, places = edge_masks()
    consts = [w_qkv, table, kernels, sums, b_up, side, jnp.asarray(masks)]
    return pl.pallas_call(
        functools.partial(back_kernel, spans, places),
        grid=(images,),
        in_specs=[image_of(b.shape[1:]) for b in blocks] + [whole(c.shape) for c in consts],
        out_specs=[image_of((ROWS, 3 * D)), whole((D, 3 * D + HALF))],
        out_shape=[sds((images, ROWS, 3 * D), BF), sds((D, 3 * D + HALF), BF)],
        scratch_shapes=[
            pltpu.VMEM((D, 3 * D), F32),
            pltpu.VMEM((2, 9, 8, HALF), F32),
            pltpu.VMEM((8, 3 * D), F32),
            pltpu.VMEM((LONG, D), F32),
            pltpu.VMEM((2 * PAIRS * (QROWS + 8), HALF), F32),
            pltpu.VMEM((4, QROWS, HALF), F32),
            pltpu.VMEM((2 * PAIRS, QROWS + 2 * EDGE, HALF), F32),
            pltpu.VMEM((4, 3, QROWS, HALF), F32),
            pltpu.VMEM((ROWS, 3 * D), F32),
            pltpu.VMEM((56, HALF), F32),
            pltpu.VMEM((D, HALF), F32),
        ],
        compiler_params=params(),
        name="back",
    )(*blocks, *consts)


def run_input(tokens_in, dqkv, dx, w_qkv, table, low, high, out=None):
    own = pl.BlockSpec((TOK_IMG, D), lambda i: (low + i, 0))
    rows = pl.BlockSpec((1, ROWS, 3 * D), lambda i: (low + i, 0, 0))
    ends = [] if out is None else [out]
    return pl.pallas_call(
        input_kernel,
        grid=(high - low,),
        in_specs=[own, rows, own, whole(w_qkv.shape), whole(table.shape)]
        + [pl.BlockSpec(memory_space=pl.ANY) for _ in ends],
        out_specs=own,
        out_shape=sds(tokens_in.shape, F32),
        input_output_aliases={5: 0} if ends else {},
        compiler_params=params(),
        cost_estimate=pl.CostEstimate(
            flops=(high - low) * 2 * ROWS * 3 * D * D,
            bytes_accessed=(high - low) * ROWS * D * 18,
            transcendentals=0,
        ),
        name="input_grad",
    )(tokens_in, dqkv, dx, w_qkv, table, *ends)


def moments(grad, first, second):
    first_new = BETA_ONE * first + (1.0 - BETA_ONE) * grad
    second_new = BETA_TWO * second + (1.0 - BETA_TWO) * grad * grad
    direction = (
        first_new
        / (1.0 - BETA_ONE**STEP)
        / (jnp.sqrt(second_new / (1.0 - BETA_TWO**STEP)) + ADAM_EPS)
    )
    return (first_new, second_new, direction)


MATRICES = (slice(0, 3 * D), slice(3 * D, 4 * D), slice(4 * D, 4 * D + FF))


def lane_sums(values):
    column = jnp.sum(values * values, axis=0, keepdims=True)
    parts = [column[:, at : at + HALF] for at in range(0, column.shape[1], HALF)]
    return functools.reduce(jnp.add, parts)


def moment_kernel(
    gq_ref,
    gq_other_ref,
    gl_ref,
    gl_other_ref,
    ww_ref,
    wm_ref,
    wv_ref,
    dw_ref,
    dm_ref,
    dv_ref,
    wf_ref,
    ws_ref,
    wu_ref,
    df_ref,
    ds_ref,
    du_ref,
    sq_ref,
):
    for lanes, own, other in (
        (slice(0, 3 * D), gq_ref[:, : 3 * D], gq_other_ref[:, : 3 * D]),
        (slice(3 * D, 4 * D + FF), gl_ref[:, : D + FF], gl_other_ref[:, : D + FF]),
    ):
        first, second, way = moments(own + other, wm_ref[:, lanes], wv_ref[:, lanes])
        wf_ref[:, lanes] = first
        ws_ref[:, lanes] = second
        wu_ref[:, lanes] = way + DECAY * ww_ref[:, lanes]
    count = ww_ref.shape[0]
    for part in range(FF // D):
        lanes = slice(D + FF + part * D, D + FF + (part + 1) * D)
        own = slice(part * count, (part + 1) * count)
        grad = gl_ref[:, lanes] + gl_other_ref[:, lanes]
        first, second, way = moments(grad, dm_ref[own, :], dv_ref[own, :])
        df_ref[own, :] = first
        ds_ref[own, :] = second
        du_ref[own, :] = way + DECAY * dw_ref[own, :]
    for base, wide, down in ((0, ww_ref, dw_ref), (4, wu_ref, du_ref)):
        for at, lanes in enumerate(MATRICES):
            sq_ref[base + at : base + at + 1, :] = lane_sums(wide[:, lanes])
        sq_ref[base + 3 : base + 4, :] = lane_sums(down[...])


def update_kernel(
    sq_ref,
    ww_ref,
    wu_ref,
    we_ref,
    dw_ref,
    du_ref,
    de_ref,
    wn_ref,
    wa_ref,
    dn_ref,
    da_ref,
    norm_ref,
):
    total = jnp.sum(jnp.sum(sq_ref[...], axis=0), axis=1, keepdims=True)
    norm = jnp.sqrt(total)
    row = lax.broadcasted_iota(jnp.int32, (8, HALF), 0)
    lane = lax.broadcasted_iota(jnp.int32, (8, HALF), 1)
    for half in range(2):
        own = jnp.where(row == lane + 4 * half, norm, 0.0)
        norm_ref[half : half + 1, :] = jnp.sum(own, axis=0, keepdims=True)[:, 0:4]
    ratio = norm[0:4] / norm[4:8]
    keep = min(EMA_CEILING, (1.0 + STEP) / (10.0 + STEP))
    for at, lanes in enumerate(MATRICES):
        new = ww_ref[:, lanes] - (RATE * ratio[at : at + 1]) * wu_ref[:, lanes]
        wn_ref[:, lanes] = new
        wa_ref[:, lanes] = keep * we_ref[:, lanes] + (1.0 - keep) * new
    new = dw_ref[...] - (RATE * ratio[3:4]) * du_ref[...]
    dn_ref[...] = new
    da_ref[...] = keep * de_ref[...] + (1.0 - keep) * new


def plain(kernel, name, out_shape, *operands):
    small = pltpu.CompilerParams(vmem_limit_bytes=8 * 1024 * 1024)
    return pl.pallas_call(kernel, out_shape=out_shape, compiler_params=small, name=name)(*operands)


def to_other(values):
    return lax.ppermute(values, "dp", [(0, 1), (1, 0)])


def copies(values, count):
    return jnp.broadcast_to(values[None], (count,) + values.shape)


def send_terms(values, count):
    return lax.all_to_all(values.reshape(count, -1, values.shape[-1]), "fsdp", 0, 0)


def add_terms(terms):
    return jnp.sum(terms.astype(F32), axis=0)


def on_device(
    count,
    tokens_in,
    cotangent,
    crop_count,
    wide_w,
    wide_m,
    wide_v,
    wide_ema,
    down_w,
    down_m,
    down_v,
    down_ema,
    small_p,
    small_m,
    small_v,
    small_ema,
):
    rows = wide_w.shape[0]
    narrow = small_p.shape[0] // rows
    small_low = jnp.pad(small_p.astype(BF).reshape(rows, narrow), ((0, 0), (0, HALF - narrow)))
    first = jnp.concatenate([wide_w[:, : 3 * D].astype(BF), small_low], axis=1)
    core = lax.axis_index("dp")
    half = lax.dynamic_slice_in_dim(first, core * (rows // 2), rows // 2, axis=0)
    half = send_terms(copies(half, count), count)
    hat, late_all = run_norm(tokens_in, wide_w, down_w, count)
    half, late_all, hat = lax.optimization_barrier((half, late_all, hat))
    late_all = send_terms(late_all, count).reshape(D, -1)
    other = to_other(half)
    first = [jnp.where(core == at, half, other) for at in range(2)]
    first = jnp.stack(first, axis=1).reshape(D, -1)
    table, kernels = small_tables(first[:, 3 * D : 3 * D + narrow].astype(F32).reshape(-1))
    side = np.stack([tap_matrix(kind) for kind in range(3)])
    side = bf(side.transpose(0, 2, 1, 3).reshape(3, QROWS, 9 * QROWS))
    hat, att, win, e, il, o = run_attend(hat, first, table, kernels, side)
    block_out, dx, datt, g_late, sums, b_up = run_feed(
        rows, crop_count, tokens_in, cotangent, att, late_all, table
    )
    late = send_terms(g_late, count)
    spans = small_spans(rows, narrow)
    dqkv, g_last = run_back(
        spans, [datt, win, e, il, o, hat], first, table, kernels, sums, b_up, side
    )
    late, g_last = lax.optimization_barrier((late, g_last))
    late = add_terms(late)
    last = send_terms(g_last, count)
    images = dqkv.shape[0]
    begin = images * 3 // 4
    grad_in = run_input(tokens_in, dqkv, dx, first, table, 0, begin)
    last, grad_in = lax.optimization_barrier((last, grad_in))
    last = add_terms(last)
    last_other = to_other(last)
    late_other = to_other(late)
    wide_like, down_like = sds(wide_w.shape, F32), sds(down_w.shape, F32)
    wide_first, wide_second, wide_upd, down_first, down_second, down_upd, squares = plain(
        moment_kernel,
        "moment",
        [wide_like] * 3 + [down_like] * 3 + [sds((8, HALF), F32)],
        *(last, last_other, late, late_other),
        *(wide_w, wide_m, wide_v, down_w, down_m, down_v),
    )
    squares, grad_in = lax.optimization_barrier((copies(squares, count), grad_in))
    squares = send_terms(squares, count)
    grad_in = run_input(tokens_in, dqkv, dx, first, table, begin, images, grad_in)
    squares, grad_in = lax.optimization_barrier((squares, grad_in))
    wide_new, wide_avg, down_new, down_avg, norms = plain(
        update_kernel,
        "update",
        [wide_like] * 2 + [down_like] * 2 + [sds((2, 4), F32)],
        *(squares, wide_w, wide_upd, wide_ema, down_w, down_upd, down_ema),
    )
    shard_small = (last + last_other)[: spans[0][1], 3 * D :].reshape(-1)
    offset = lax.axis_index("fsdp") * (rows * narrow) % HALF
    shard_small = lax.dynamic_slice(shard_small, (offset,), (rows * narrow,))
    small_first, small_second, small_dir = moments(shard_small, small_m, small_v)
    small_new = small_p - RATE * small_dir
    ema_keep = min(EMA_CEILING, (1.0 + STEP) / (10.0 + STEP))
    small_avg = ema_keep * small_ema + (1.0 - ema_keep) * small_new
    return (
        block_out,
        grad_in,
        wide_new,
        wide_first,
        wide_second,
        wide_avg,
        down_new,
        down_first,
        down_second,
        down_avg,
        small_new,
        small_first,
        small_second,
        small_avg,
        norms,
    )


def solution(mesh):
    tok, row, vec = P(("dp", "fsdp"), None), P("fsdp", None), P("fsdp")
    in_specs = (tok, tok, P(("dp", "fsdp"))) + (row,) * 8 + (vec,) * 4
    out_specs = (tok, tok) + (row,) * 8 + (vec,) * 4 + (P(),)
    return jax.shard_map(
        functools.partial(on_device, mesh.shape["fsdp"]),
        mesh=mesh,
        in_specs=in_specs,
        out_specs=out_specs,
        check_vma=False,
    )
```

```python
import functools

import jax
import jax.numpy as jnp
import numpy as np
from jax import lax
from jax.experimental import pallas as pl
from jax.experimental.pallas import tpu as pltpu
from jax.sharding import PartitionSpec as P

D = 256
FF = 1024
HEAD = 32
STRIPE = 7
GRID_L = 14
GRID_S = 6
SMALL = 8
STEP = 10
TOK_IMG = 680

EPSILON = 1e-05
BETA_ONE = 0.9
BETA_TWO = 0.999
ADAM_EPS = 1e-06
DECAY = 0.05
RATE = 0.25
EMA_CEILING = 0.9999

ROWS = 688
BIG = 2 * GRID_L * GRID_L
PAIRS = 7
WIN = 128
QROWS = 112
HALF = 128
HEADS = 4
SCALE = HEAD**-0.5
LOG2E = 1.4426950408889634
LN2 = 0.6931471805599453
ROOT = 2**-0.5
CHUNKS = ((0, 240), (240, 464), (464, 688))
LONG = 744
EDGE = 16
COPIES = (3, 3, 2)
TAPS = tuple((dy, dx) for dy in (-1, 0, 1) for dx in (-1, 0, 1))
ORDER = (0, 2, 1, 3, 4, 5, 6)
VMEM = 60 * 1024 * 1024

BF = jnp.bfloat16
F32 = jnp.float32


def kind_of(pair):
    return 0 if pair < 2 else 1 if pair < 4 else 2


def branch_of(pair, member):
    return 0 if pair < 2 else 1 if pair < 4 else member


def first_of(pair, member):
    if pair < 2:
        return pair * GRID_L * GRID_L + member * STRIPE * GRID_L
    if pair < 4:
        return (pair - 2) * GRID_L * GRID_L + member * STRIPE
    return BIG + (pair - 4) * COPIES[0] * GRID_S * GRID_S


def tokens_of(pair):
    return STRIPE * GRID_L if pair < 4 else COPIES[pair - 4] * GRID_S * GRID_S


def shape_of(kind):
    return ((STRIPE, GRID_L), (GRID_L, STRIPE), (GRID_S, GRID_S))[kind]


def edge_masks():
    masks, places = [], {}
    for kind in range(3):
        high, broad = shape_of(kind)
        size = high * broad
        for dy, dx in TAPS:
            if (dy, dx) == (0, 0) or (kind < 2 and (dy != 0 or dx == 0)):
                continue
            mask = np.zeros((QROWS, HALF), np.float32)
            for at in range(size * (1 if kind < 2 else COPIES[0])):
                r, c = divmod(at % size, broad)
                mask[at] = 0 <= r + dy < high and 0 <= c + dx < broad
            places[kind, dy, dx] = len(masks)
            masks.append(mask)
    return np.stack(masks), places


def tap_matrix(kind):
    shape = shape_of(kind)
    copies = 1 if kind < 2 else COPIES[0]
    size = shape[0] * shape[1]
    out = np.zeros((9, QROWS, QROWS), np.float32)
    for copy in range(copies):
        for r in range(shape[0]):
            for c in range(shape[1]):
                for tap in range(9):
                    rr, cc = r + tap // 3 - 1, c + tap % 3 - 1
                    if 0 <= rr < shape[0] and 0 <= cc < shape[1]:
                        out[tap, copy * size + r * shape[1] + c, copy * size + rr * shape[1] + cc] = 1
    return out


def mask_operands():
    size = GRID_S * GRID_S
    rows = np.zeros((3, 2, QROWS, HALF), np.float32)
    keys = np.zeros((3, HALF // 2, WIN), np.float32)
    for kind, crops in ((0, 1), (1, 3), (2, 2)):
        count = STRIPE * GRID_L if kind == 0 else crops * size
        each = count // crops
        for at in range(QROWS):
            rows[kind, 0, at, HALF // 2 + (at // each if at < count else 0)] = 1
        for at in range(WIN):
            for crop in range(crops):
                if at >= count or at // each != crop:
                    keys[kind, crop, at] = -1e30
    rows[:, 1, :, : HALF // 2] = rows[:, 0, :, HALF // 2 :]
    return rows, np.tile(keys, (1, 1, 2))


def bf(array):
    return jnp.asarray(array, BF)


def dot(left, right):
    return jnp.dot(left, right, preferred_element_type=F32)


def dot_nt(left, right):
    return lax.dot_general(left, right, (((1,), (1,)), ((), ())), preferred_element_type=F32)


def dot_tn(left, right):
    return lax.dot_general(left, right, (((0,), (0,)), ((), ())), preferred_element_type=F32)


def normalise(values):
    center = values - jnp.mean(values, axis=-1, keepdims=True)
    spread = jnp.mean(center * center, axis=-1, keepdims=True)
    scale = lax.rsqrt(spread + EPSILON)
    return center * scale, scale


def norm_back(grad_hat, hat, scale):
    mean_grad = jnp.mean(grad_hat, axis=-1, keepdims=True)
    mean_dot = jnp.mean(grad_hat * hat, axis=-1, keepdims=True)
    return scale * (grad_hat - mean_grad - hat * mean_dot)


def rows_of(ref, low, high):
    if high <= TOK_IMG:
        return ref[low:high, :]
    tail = jnp.zeros((high - TOK_IMG, ref.shape[1]), F32)
    return jnp.concatenate([ref[low:TOK_IMG, :], tail], axis=0)


def store_rows(ref, low, high, values):
    last = min(high, TOK_IMG)
    ref[low:last, :] = values[: last - low]


def with_ones(turned):
    return jnp.concatenate([turned, jnp.ones((16, turned.shape[1]), turned.dtype)], axis=0)


def fold(values):
    return jnp.sum(values.reshape(values.shape[0] // 8, 8, values.shape[1]), axis=0)


def head_lanes(head):
    lanes = lax.broadcasted_iota(jnp.int32, (1, HALF), 1)
    return jnp.where(lanes // HEAD == head, 1.0, 0.0).astype(BF)


def by_head(values):
    return jnp.concatenate([values * head_lanes(h) for h in range(HEADS)], axis=0)


def lane_half(upper):
    lanes = lax.broadcasted_iota(jnp.int32, (1, HALF), 1)
    return jnp.where((lanes >= HALF // 2) == upper, 1.0, 0.0).astype(BF)


def two_heads(turned, pair):
    low = pair * 2 * HEAD
    none = jnp.zeros((HEAD, WIN), turned.dtype)
    first = jnp.concatenate([turned[low : low + HEAD], none], axis=1)
    second = jnp.concatenate([none, turned[low + HEAD : low + 2 * HEAD]], axis=1)
    return jnp.concatenate([first, second], axis=0)


def by_two_heads(left, other, turned, added):
    low, high = lane_half(False), lane_half(True)
    first = dot(
        left * low + other[0], jnp.concatenate([two_heads(turned, 0), added], axis=0)
    )
    second = dot(
        left * high + other[1], jnp.concatenate([added, two_heads(turned, 1)], axis=0)
    )
    return [first[:, :WIN], first[:, WIN:], second[:, :WIN], second[:, WIN:]]


def head_block(rows):
    return jnp.concatenate(
        [jnp.broadcast_to(head_lanes(h), (rows, HALF)) for h in range(HEADS)], axis=0
    )


def taps_of(table, branch):
    return table[5:14, branch * HALF : (branch + 1) * HALF]


def first_rows(values, count):
    low = count // 16 * 16
    if low >= values.shape[0]:
        return values
    row = lax.broadcasted_iota(jnp.int32, (values.shape[0] - low, 1), 0)
    tail = jnp.where(row < count - low, values[low:], 0.0)
    return jnp.concatenate([values[:low], tail], axis=0)


def pieces_of(pair, member):
    low = first_of(pair, member)
    return [(low + r * GRID_L, r * STRIPE) for r in range(GRID_L)]


def pipelined(stages, order, extra=()):
    extra = dict(extra)
    state = {item: {} for item in order}
    for turn in range(len(order) + max(lag for lag, _ in stages)):
        if turn in extra:
            extra[turn]()
        running = []
        for lag, stage in stages:
            if 0 <= turn - lag < len(order):
                item = order[turn - lag]
                running.append(stage(item, state[item]))
        while running:
            running = [stage for stage in running if next(stage, True) is None]


def norm_kernel(x_ref, wide_ref, down_ref, hat_ref, late_ref):
    for low in range(0, x_ref.shape[0], TOK_IMG // 5):
        hat_ref[low : low + TOK_IMG // 5, :] = normalise(x_ref[low : low + TOK_IMG // 5, :])[0]

    @pl.when(pl.program_id(0) == 0)
    def _():
        rows = wide_ref.shape[0]
        pieces = [wide_ref[:, 3 * D :]]
        pieces += [down_ref[at : at + rows, :] for at in range(0, down_ref.shape[0], rows)]
        late = jnp.concatenate(pieces, axis=1).astype(BF)
        for owner in range(late_ref.shape[0]):
            late_ref[owner] = late


def attend_kernel(
    x_ref,
    w_ref,
    s_ref,
    tap_ref,
    mrow_ref,
    mkey_ref,
    hat_ref,
    att_ref,
    win_ref,
    e_ref,
    il_ref,
    o_ref,
    qkv_scr,
    turn_scr,
    back_scr,
    att_scr,
):
    @pl.when(pl.program_id(0) == 0)
    def _():
        for branch in range(2):
            qkv_scr[branch, ROWS:, :] = jnp.zeros((LONG - ROWS, 3 * HALF), F32)
        turn_scr[...] = jnp.zeros_like(turn_scr)
        att_scr[TOK_IMG:, :] = jnp.zeros((ROWS - TOK_IMG, D), F32)

    gain, shift = s_ref[0:1, :], s_ref[1:2, :]
    ones = head_block(WIN)

    def project(chunk):
        low, high = CHUNKS[chunk]
        hat = rows_of(x_ref, low, high)
        hat_ref[0, low:high, :] = hat.astype(BF)
        a = (hat * gain + shift).astype(BF)
        for part in range(3):
            lanes = slice(part * D, (part + 1) * D)
            piece = dot(a, w_ref[:, lanes]) + s_ref[2 + part : 3 + part, :]
            if part == 0:
                piece = piece * (SCALE * LOG2E)
            for branch in range(2):
                qkv_scr[branch, low:high, part * HALF : (part + 1) * HALF] = piece[
                    :, branch * HALF : (branch + 1) * HALF
                ]

    none = jnp.zeros((WIN - QROWS, HALF), BF)

    def cut(pair, state):
        for member in range(2):
            at = 2 * pair + member
            if kind_of(pair) == 1:
                for source, target in pieces_of(pair, member):
                    turn_scr[at - 4, target : target + STRIPE, :] = qkv_scr[
                        1, source : source + STRIPE, :
                    ]
                window = turn_scr[at - 4, :QROWS, :]
            else:
                low = first_of(pair, member)
                window = qkv_scr[branch_of(pair, member), low : low + QROWS, :]
            window = window.astype(BF)
            win_ref[0, at] = window
            state[member] = [window[:, part * HALF : (part + 1) * HALF] for part in range(3)]
            yield

    def score(pair, state):
        mask = 0 if pair < 4 else 1 if pair < 6 else 2
        for member in range(2):
            q, k, v = state[member]
            k = jnp.concatenate([k, none], axis=0).T
            rows = mrow_ref[mask, 0], mrow_ref[mask, 1]
            state[member] = v, by_two_heads(q, rows, k, mkey_ref[mask])
            yield

    def soften(pair, state):
        for member in range(2):
            v, scores = state[member]
            exps = []
            for part in scores:
                peak = jnp.max(part, axis=-1, keepdims=True)
                exps.append(jnp.exp2(part - peak).astype(BF))
            e = jnp.concatenate(exps, axis=1)
            e_ref[0, 2 * pair + member] = e
            state[member] = v, e
            yield

    def mix(pair, state):
        taps = []
        for member in range(2):
            v, e = state[member]
            low = taps_of(s_ref, branch_of(pair, member)).astype(BF)
            keys = jnp.concatenate([v, none], axis=0)
            state[member] = dot(e, jnp.concatenate([by_head(keys), ones], axis=1))
            taps.append(jnp.concatenate([v * low[tap : tap + 1] for tap in range(9)], axis=0))
            yield
        state[2] = dot(tap_ref[kind_of(pair)], jnp.concatenate(taps, axis=1))
        yield

    def put(pair, state):
        for member in range(2):
            at = 2 * pair + member
            branch = branch_of(pair, member)
            lanes = slice(branch * HALF, (branch + 1) * HALF)
            both = state[member]
            inv = 1.0 / both[:, HALF:]
            o = both[:, :HALF] * inv
            il_ref[0, at] = inv
            o_ref[0, at] = o.astype(BF)
            conv = state[2][:, member * HALF : (member + 1) * HALF]
            piece = o + s_ref[14:15, lanes] + conv
            if kind_of(pair) == 1:
                back_scr[at - 4] = piece
                for source, target in pieces_of(pair, member):
                    att_scr[source : source + STRIPE, lanes] = back_scr[
                        at - 4, target : target + STRIPE, :
                    ]
            else:
                low, count = first_of(pair, member), tokens_of(pair)
                att_scr[low : low + count, lanes] = piece[:count]
            yield

    project(0)
    extra = {1: functools.partial(project, 1), 3: functools.partial(project, 2)}
    stages = enumerate((cut, score, soften, mix, put))
    pipelined(tuple(stages), ORDER, extra)
    att_ref[0] = att_scr[...].astype(BF)


def gelu_parts(v):
    above = lax.erf(v) + 1.0
    decay = jnp.exp2((v * v) * -LOG2E)
    return v * above, above + (v * decay) * (2 / np.sqrt(np.pi))


def beside(*streams):
    left = [[list(stream), 0] for stream in streams]
    total = max((len(steps) for steps, _ in left), default=0)
    for at in range(total):
        for entry in left:
            steps, done = entry
            goal = -(-len(steps) * (at + 1) // total)
            for step in steps[done:goal]:
                step()
            entry[1] = goal


def weight_terms(grad, weight, bias):
    terms = []
    for value in (weight * bias,) if grad is None else (weight * grad, weight * bias):
        column = jnp.sum(value, axis=1, keepdims=True)
        terms.append(jnp.broadcast_to(column, (D, HALF)).T[0:1, :])
    return terms


def down_blocks(shard):
    parts = FF // D
    return [(i, part, (i * parts + part) * shard) for i in range(D // shard) for part in range(parts)]


def feed_kernel(
    shard,
    cnt_ref,
    x_ref,
    c_ref,
    att_ref,
    w_ref,
    s_ref,
    out_ref,
    dx_ref,
    datt_ref,
    pack_ref,
    sums_ref,
    bup_ref,
    rs_scr,
    x1_scr,
    gup_scr,
    gdn_scr,
    gout_scr,
    turn_scr,
    pack_scr,
    down_scr,
):
    image = pl.program_id(0)

    @pl.when(image == 0)
    def _():
        for ref in (gup_scr, gdn_scr, gout_scr, sums_ref, bup_ref):
            ref[...] = jnp.zeros_like(ref)
        pack_scr[...] = w_ref[:, D + FF :].astype(F32)
        for owner, part, low in down_blocks(shard):
            turn_scr[low : low + shard, :] = pack_scr[
                owner * shard : (owner + 1) * shard, part * D : (part + 1) * D
            ]
        down_scr[...] = turn_scr[...].astype(BF)

    bound = BIG + GRID_S * GRID_S * cnt_ref[image]
    bias_out, gain, shift = s_ref[15:16, :], s_ref[16:17, :], s_ref[17:18, :]
    lanes_of = [slice(part * D, (part + 1) * D) for part in range(FF // D)]
    count = 16
    rows = range(0, ROWS, count)
    biases = [s_ref[18 + part : 19 + part, :] * ROOT for part in range(FF // D)]
    sums = {}
    held = {}

    def add_sum(key, values, at, ref, *index):
        sums[key] = sums[key] + fold(values) if key in sums else fold(values)
        if at + count >= ROWS:
            ref[index] += sums[key]

    def keep(key, at, values):
        held.setdefault(key, []).append(values)
        if at + count >= ROWS:
            held[key] = jnp.concatenate(held[key], axis=0)

    def masked(at):
        row = at + lax.broadcasted_iota(jnp.int32, (count, 1), 0)
        return jnp.where(row < bound, rows_of(c_ref, at, at + count), 0.0)

    def cot(at):
        dy = masked(at)
        keep("dy", at, dy.astype(BF))
        add_sum("dy", dy, at, sums_ref, 0)

    def project():
        held["x1"] = dot(att_ref[0], w_ref[:, :D])

    def norm(at):
        own = slice(at, at + count)
        x1 = rows_of(x_ref, at, at + count) + held["x1"][own] + bias_out
        x1_scr[own, :] = x1
        hat, scale = normalise(x1)
        rs_scr[own, :] = scale
        keep("hat", at, hat.astype(BF))
        keep("h2", at, (hat * (gain * ROOT) + shift * ROOT).astype(BF))

    def hidden(part):
        cols = slice(D + part * D, D + (part + 1) * D)
        held["v", part] = dot(held["h2"], w_ref[:, cols])

    def hidden_back(part):
        held["dg", part] = dot_nt(held["dy"], down_scr[lanes_of[part], :])

    def gelu(part, at):
        own = slice(at, at + count)
        v = held["v", part][own] + biases[part]
        g, slope = gelu_parts(v)
        keep(("g", part), at, g.astype(BF))
        du = held["dg", part][own] * slope
        keep(("du", part), at, du.astype(BF))

    def gelus(part):
        return [functools.partial(gelu, part, at) for at in rows]

    def grad_up(part):
        both = dot(held["hat_t"], held["du", part])
        gup_scr[:, lanes_of[part]] += both[:D]
        bup_ref[:, lanes_of[part]] += both[D : D + 8]

    def grad_down(part):
        gdn_scr[:, lanes_of[part]] += dot(held["dy_t"], held["g", part])

    def joined(key, *parts):
        return jnp.concatenate([held[key, part] for part in parts], axis=1)

    half = FF // 2

    def out_first():
        held["out"] = dot(joined("g", 0, 1), down_scr[:half, :])

    def out_last():
        held["out"] += dot(joined("g", 2, 3), down_scr[half:, :])

    def out_store(at):
        own = slice(at, at + count)
        out = x1_scr[own, :] + held["out"][own] * ROOT + s_ref[22:23, :]
        store_rows(out_ref, at, at + count, out)

    def back_first():
        held["dh"] = dot_nt(joined("du", 0, 1), w_ref[:, D : D + half])

    def back_last():
        held["dh"] += dot_nt(joined("du", 2, 3), w_ref[:, D + half : D + FF])

    def norm_grad(at):
        own = slice(at, at + count)
        hat = held["hat"][own].astype(F32)
        dx = masked(at) + norm_back(held["dh"][own] * (gain * 0.5), hat, rs_scr[own, :])
        store_rows(dx_ref, at, at + count, dx)
        keep("dz", at, dx.astype(BF))
        add_sum("dz", dx, at, sums_ref, 1)

    def attention():
        datt = dot_nt(held["dz"], w_ref[:, :D])
        datt_ref[0] = datt.astype(BF)

    def grad_out():
        gout_scr[...] += dot_tn(att_ref[0], held["dz"])

    def each(step, *parts):
        return [functools.partial(step, part) for part in parts]

    def turn(key):
        held[key + "_t"] = held[key].T

    beside(each(cot, *rows), [project])
    turn("dy")
    beside(each(norm, *rows), each(hidden_back, 0, 1, 2, 3))
    turn("hat")
    held["hat_t"] = with_ones(held["hat_t"])
    hidden(0)
    beside(each(hidden, 1, 2, 3), gelus(0))
    beside(each(grad_up, 0) + each(grad_down, 0), gelus(1))
    beside([back_first] + each(grad_up, 1) + each(grad_down, 1), gelus(2))
    beside([out_first] + each(grad_up, 2) + each(grad_down, 2), gelus(3))
    back_last()
    beside([out_last] + each(grad_up, 3) + each(grad_down, 3), each(norm_grad, *rows))
    beside([attention, grad_out], each(out_store, *rows))

    @pl.when(image == pl.num_programs(0) - 1)
    def _():
        turn_scr[...] = gdn_scr[...].T * ROOT
        for owner, part, low in down_blocks(shard):
            pack_scr[owner * shard : (owner + 1) * shard, part * D : (part + 1) * D] = turn_scr[
                low : low + shard, :
            ]
        bup_ref[...] *= 0.5
        bias = bup_ref[0:1, :]
        grad = gup_scr[...] * 0.5
        terms = weight_terms(grad, w_ref[:, D : D + FF].astype(F32), bias)
        out_bias = jnp.sum(sums_ref[1], axis=0, keepdims=True)
        terms += weight_terms(None, w_ref[:, :D].astype(F32), out_bias)
        for at, term in enumerate(terms):
            sums_ref[2 + at, 0:1, :] = term
        columns = s_ref[15:23, :].T
        grad = columns[:, 1:2] * grad + columns[:, 2:3] * bias
        pack_ref[:, :D] = gout_scr[...].astype(BF)
        pack_ref[:, D : D + FF] = grad.astype(BF)
        pack_ref[:, D + FF :] = pack_scr[...].astype(BF)


def small_spans(shard, narrow):
    count = D // shard
    own = shard * narrow
    rows = max((own * (i + 1) - 1) // HALF - own * i // HALF + 1 for i in range(count))
    return [(own * i // HALF, rows) for i in range(count)]


def back_kernel(
    spans,
    places,
    datt_ref,
    win_ref,
    e_ref,
    il_ref,
    o_ref,
    hat_ref,
    w_ref,
    s_ref,
    feed_ref,
    bup_ref,
    tap_ref,
    edge_ref,
    dqkv_ref,
    pack_ref,
    g_scr,
    kern_scr,
    bias_scr,
    datt_scr,
    grad_scr,
    turn_scr,
    pad_scr,
    back_scr,
    dqkv_scr,
    small_scr,
    pack_scr,
):
    image = pl.program_id(0)

    @pl.when(image == 0)
    def _():
        for ref in (g_scr, kern_scr, bias_scr, turn_scr, pad_scr, small_scr, pack_scr):
            ref[...] = jnp.zeros_like(ref)
        datt_scr[ROWS:, :] = jnp.zeros((LONG - ROWS, D), F32)
        dqkv_scr[TOK_IMG:, :] = jnp.zeros((ROWS - TOK_IMG, 3 * D), F32)

    for low, high in CHUNKS:
        datt_scr[low:high, :] = datt_ref[0, low:high, :].astype(F32)
    minus = two_heads(jnp.full((HALF, WIN), -1.0, BF), 0)
    none = jnp.zeros((WIN - QROWS, HALF), BF)

    def weigh(pair, state):
        for member in range(2):
            at = 2 * pair + member
            branch = branch_of(pair, member)
            lanes = slice(branch * HALF, (branch + 1) * HALF)
            if kind_of(pair) == 1:
                for source, target in pieces_of(pair, member):
                    turn_scr[at - 4, target : target + STRIPE, :] = datt_scr[
                        source : source + STRIPE, lanes
                    ]
                grad = turn_scr[at - 4]
            else:
                low = first_of(pair, member)
                grad = first_rows(datt_scr[low : low + QROWS, lanes], tokens_of(pair))
            grad_scr[at * QROWS : (at + 1) * QROWS, :] = grad
            v = win_ref[0, at, :, 2 * HALF :]
            pad_scr[at, EDGE : EDGE + QROWS, :] = first_rows(v.astype(F32), tokens_of(pair))
            dn = grad * il_ref[0, at]
            z = pltpu.roll(dn * o_ref[0, at].astype(F32), HALF // 2, 1).astype(BF)
            dn = dn.astype(BF)
            rows = z * lane_half(True), z * lane_half(False)
            v = jnp.concatenate([v, none], axis=0).T
            state[member] = grad, dn, by_two_heads(dn, rows, v, minus)
            yield

    def score(pair, state):
        for member in range(2):
            grad, dn, weighed = state[member]
            e = e_ref[0, 2 * pair + member]
            ds = jnp.concatenate(weighed, axis=1).astype(BF) * e
            state[member] = grad, dn, ds, e
            yield

    def spread(pair, state):
        kind = kind_of(pair)
        taps = []
        for member in range(2):
            grad, dn, ds, e = state[member]
            at = 2 * pair + member
            kernel = taps_of(s_ref, branch_of(pair, member)).astype(BF)
            q = win_ref[0, at, :, 0:HALF]
            k = jnp.concatenate([win_ref[0, at, :, HALF : 2 * HALF], none], axis=0)
            dq = dot(ds, by_head(k))
            row = 2 * PAIRS * QROWS + 8 * at
            grad_scr[row : row + 8, :] = dq[:8]
            q_t, dn_t = q.T, dn.T
            dk, dv = [], []
            for half in range(2):
                lanes = slice(2 * half * WIN, 2 * (half + 1) * WIN)
                own = slice(2 * half * HEAD, 2 * (half + 1) * HEAD)
                for parts, left, right in ((dk, q_t, ds), (dv, dn_t, e)):
                    both = dot(left[own], right[:, lanes])
                    parts += [both[:HEAD, :WIN], both[HEAD:, WIN:]]
            state[member] = dq, dk, dv
            low = grad.astype(BF)
            taps.append(
                jnp.concatenate([low * kernel[8 - tap : 9 - tap] for tap in range(9)], axis=0)
            )
            yield
        state[2] = dot(tap_ref[kind], jnp.concatenate(taps, axis=1))
        yield

    def kernels(pair, state):
        kind = kind_of(pair)
        broad = shape_of(kind)[1]
        for member in range(2):
            at = 2 * pair + member
            base = pl.multiple_of(at * QROWS + image // 4096 * 8, 8)
            totals = [jnp.zeros((8, HALF), F32)] * 9
            for low in range(0, tokens_of(pair), 8):
                own = slice(low, low + 8)
                grad = grad_scr[pl.ds(pl.multiple_of(base + low, 8), 8), :]
                sides = {}
                for tap, (dy, dx) in enumerate(TAPS):
                    place = places.get((kind, 0 if kind < 2 else dy, dx))
                    if place not in sides:
                        mask = 1.0 if place is None else edge_ref[place, own, :]
                        sides[place] = grad * mask
                    start = EDGE + low + dy * broad + dx
                    totals[tap] = totals[tap] + sides[place] * pad_scr[at, start : start + 8, :]
            for tap in range(9):
                kern_scr[branch_of(pair, member), tap] += totals[tap]
            yield

    def put(pair, state):
        for member in range(2):
            at = 2 * pair + member
            branch = branch_of(pair, member)
            dq, dk, dv = state[member]
            dk = jnp.concatenate(dk, axis=0).T[:QROWS] * LN2
            dv = jnp.concatenate(dv, axis=0).T[:QROWS]
            dv = dv + state[2][:, member * HALF : (member + 1) * HALF]
            for part, piece in enumerate((dq * SCALE, dk, dv)):
                lanes = slice(part * D + branch * HALF, part * D + (branch + 1) * HALF)
                if kind_of(pair) == 1:
                    back_scr[at - 4, part] = piece
                    for source, target in pieces_of(pair, member):
                        dqkv_scr[source : source + STRIPE, lanes] = back_scr[
                            at - 4, part, target : target + STRIPE, :
                        ]
                else:
                    low, count = first_of(pair, member), tokens_of(pair)
                    dqkv_scr[low : low + count, lanes] = piece[:count]
            yield

    pipelined(((3, kernels), (0, weigh), (1, score), (2, spread), (3, put)), ORDER)
    dqkv = dqkv_scr[...].astype(BF)
    dqkv_ref[0] = dqkv
    both = dot(with_ones(hat_ref[0].T), dqkv)
    g_scr[...] += both[:D]
    bias_scr[...] += both[D : D + 8]

    @pl.when(image == pl.num_programs(0) - 1)
    def _():
        def put(row, terms):
            for at in range(0, terms.shape[1], HALF):
                small_scr[row : row + 1, :] = terms[:, at : at + HALF]
                row += 1

        total = lambda terms: jnp.sum(terms, axis=0, keepdims=True)
        bias = bias_scr[0:1, :]
        gain, shift = weight_terms(g_scr[...], w_ref[:, : 3 * D].astype(F32), bias)
        put(0, gain)
        put(2, shift)
        put(4, bias)
        for tap in range(9):
            for branch in range(2):
                put(10 + 2 * tap + branch, total(kern_scr[branch, tap]))
        for row, entry in ((30, 1), (44, 0)):
            put(row, total(feed_ref[entry]))
        for row, entry in ((32, 2), (34, 3), (28, 4)):
            put(row, feed_ref[entry, 0:1, :])
        put(36, bup_ref[0:1, :])
        for owner, (row, rows) in enumerate(spans):
            shard = D // len(spans)
            pack_scr[owner * shard : owner * shard + rows, :] = small_scr[row : row + rows, :]
        columns = s_ref[0:8, :].T
        grad = columns[:, 0:1] * g_scr[...] + columns[:, 1:2] * bias
        pack_ref[:, : 3 * D] = grad.astype(BF)
        pack_ref[:, 3 * D :] = pack_scr[...].astype(BF)


def input_kernel(x_ref, dqkv_ref, dx_ref, w_ref, s_ref, *out_refs):
    out_ref = out_refs[-1]
    for low, high in CHUNKS:
        dh = dot_nt(dqkv_ref[0, low:high, :], w_ref[:, : 3 * D])
        hat, scale = normalise(rows_of(x_ref, low, high))
        grad = rows_of(dx_ref, low, high) + norm_back(dh * s_ref[0:1, :], hat, scale)
        store_rows(out_ref, low, high, grad)


def whole(shape):
    return pl.BlockSpec(shape, lambda i, *_: (0,) * len(shape))


def image_of(shape):
    return pl.BlockSpec((1,) + shape, lambda i, *_: (i,) + (0,) * len(shape))


def tokens():
    return pl.BlockSpec((TOK_IMG, D), lambda i, *_: (i, 0))


def params(room=0):
    return pltpu.CompilerParams(
        vmem_limit_bytes=VMEM - room * 1024 * 1024, dimension_semantics=("arbitrary",)
    )


def sds(shape, dtype):
    return jax.ShapeDtypeStruct(shape, dtype)


def run_norm(tokens_in, wide, down, count):
    rows = TOK_IMG * 2
    block = pl.BlockSpec((rows, D), lambda i: (i, 0))
    late = (count, wide.shape[0], D + 2 * FF)
    return pl.pallas_call(
        norm_kernel,
        grid=(tokens_in.shape[0] // rows,),
        in_specs=[block, whole(wide.shape), whole(down.shape)],
        out_specs=[block, whole(late)],
        out_shape=[sds(tokens_in.shape, F32), sds(late, BF)],
        compiler_params=params(),
        name="norm",
    )(tokens_in, wide, down)


def run_attend(tokens_in, w_qkv, table, side):
    images = tokens_in.shape[0] // TOK_IMG
    mrow, mkey = mask_operands()
    consts = [table, side, bf(mrow), bf(mkey)]
    outs = [
        ((ROWS, D), BF),
        ((ROWS, D), BF),
        ((2 * PAIRS, QROWS, 3 * HALF), BF),
        ((2 * PAIRS, QROWS, HEADS * WIN), BF),
        ((2 * PAIRS, QROWS, HALF), F32),
        ((2 * PAIRS, QROWS, HALF), BF),
    ]
    return pl.pallas_call(
        attend_kernel,
        grid=(images,),
        in_specs=[tokens(), whole(w_qkv.shape)] + [whole(c.shape) for c in consts],
        out_specs=[image_of(shape) for shape, _ in outs],
        out_shape=[sds((images,) + shape, dtype) for shape, dtype in outs],
        scratch_shapes=[
            pltpu.VMEM((2, LONG, 3 * HALF), F32),
            pltpu.VMEM((4, QROWS, 3 * HALF), F32),
            pltpu.VMEM((4, QROWS, HALF), F32),
            pltpu.VMEM((ROWS, D), F32),
        ],
        compiler_params=params(-3),
        name="attend",
    )(tokens_in, w_qkv, *consts)


def run_feed(shard, counts, tokens_in, cotangent, att, wide, table):
    images = tokens_in.shape[0] // TOK_IMG
    return pl.pallas_call(
        functools.partial(feed_kernel, shard),
        grid_spec=pltpu.PrefetchScalarGridSpec(
            num_scalar_prefetch=1,
            grid=(images,),
            in_specs=[
                tokens(),
                tokens(),
                image_of((ROWS, D)),
                whole(wide.shape),
                whole(table.shape),
            ],
            out_specs=[
                tokens(),
                tokens(),
                image_of((ROWS, D)),
                whole((D, D + 2 * FF)),
                whole((5, 8, D)),
                whole((8, FF)),
            ],
            scratch_shapes=[
                pltpu.VMEM((ROWS, 1), F32),
                pltpu.VMEM((ROWS, D), F32),
                pltpu.VMEM((D, FF), F32),
                pltpu.VMEM((D, FF), F32),
                pltpu.VMEM((D, D), F32),
                pltpu.VMEM((FF, D), F32),
                pltpu.VMEM((D, FF), F32),
                pltpu.VMEM((FF, D), BF),
            ],
        ),
        out_shape=[
            sds(tokens_in.shape, F32),
            sds(tokens_in.shape, F32),
            sds((images, ROWS, D), BF),
            sds((D, D + 2 * FF), BF),
            sds((5, 8, D), F32),
            sds((8, FF), F32),
        ],
        compiler_params=params(),
        name="feed",
    )(counts, tokens_in, cotangent, att, wide, table)


def run_back(spans, blocks, w_qkv, table, sums, b_up, side):
    images = blocks[0].shape[0]
    masks, places = edge_masks()
    consts = [w_qkv, table, sums, b_up, side, jnp.asarray(masks)]
    return pl.pallas_call(
        functools.partial(back_kernel, spans, places),
        grid=(images,),
        in_specs=[image_of(b.shape[1:]) for b in blocks] + [whole(c.shape) for c in consts],
        out_specs=[image_of((ROWS, 3 * D)), whole((D, 3 * D + HALF))],
        out_shape=[sds((images, ROWS, 3 * D), BF), sds((D, 3 * D + HALF), BF)],
        scratch_shapes=[
            pltpu.VMEM((D, 3 * D), F32),
            pltpu.VMEM((2, 9, 8, HALF), F32),
            pltpu.VMEM((8, 3 * D), F32),
            pltpu.VMEM((LONG, D), F32),
            pltpu.VMEM((2 * PAIRS * (QROWS + 8), HALF), F32),
            pltpu.VMEM((4, QROWS, HALF), F32),
            pltpu.VMEM((2 * PAIRS, QROWS + 2 * EDGE, HALF), F32),
            pltpu.VMEM((4, 3, QROWS, HALF), F32),
            pltpu.VMEM((ROWS, 3 * D), F32),
            pltpu.VMEM((56, HALF), F32),
            pltpu.VMEM((D, HALF), F32),
        ],
        compiler_params=params(),
        name="back",
    )(*blocks, *consts)


def run_input(tokens_in, dqkv, dx, w_qkv, table, low, high, out=None):
    own = pl.BlockSpec((TOK_IMG, D), lambda i: (low + i, 0))
    rows = pl.BlockSpec((1, ROWS, 3 * D), lambda i: (low + i, 0, 0))
    ends = [] if out is None else [out]
    return pl.pallas_call(
        input_kernel,
        grid=(high - low,),
        in_specs=[own, rows, own, whole(w_qkv.shape), whole(table.shape)]
        + [pl.BlockSpec(memory_space=pl.ANY) for _ in ends],
        out_specs=own,
        out_shape=sds(tokens_in.shape, F32),
        input_output_aliases={5: 0} if ends else {},
        compiler_params=params(),
        cost_estimate=pl.CostEstimate(
            flops=(high - low) * 2 * ROWS * 3 * D * D,
            bytes_accessed=(high - low) * ROWS * D * 18,
            transcendentals=0,
        ),
        name="input_grad",
    )(tokens_in, dqkv, dx, w_qkv, table, *ends)


def moments(grad, first, second):
    first_new = BETA_ONE * first + (1.0 - BETA_ONE) * grad
    second_new = BETA_TWO * second + (1.0 - BETA_TWO) * grad * grad
    direction = (
        first_new
        / (1.0 - BETA_ONE**STEP)
        / (jnp.sqrt(second_new / (1.0 - BETA_TWO**STEP)) + ADAM_EPS)
    )
    return (first_new, second_new, direction)


MATRICES = (slice(0, 3 * D), slice(3 * D, 4 * D), slice(4 * D, 4 * D + FF))


def lane_sums(values):
    column = jnp.sum(values * values, axis=0, keepdims=True)
    parts = [column[:, at : at + HALF] for at in range(0, column.shape[1], HALF)]
    return functools.reduce(jnp.add, parts)


def moment_kernel(
    gq_ref,
    gq_other_ref,
    gl_ref,
    gl_other_ref,
    ww_ref,
    wm_ref,
    wv_ref,
    dw_ref,
    dm_ref,
    dv_ref,
    wf_ref,
    ws_ref,
    wu_ref,
    df_ref,
    ds_ref,
    du_ref,
    copies_ref,
    sq_ref,
):
    for lanes, own, other in (
        (slice(0, 3 * D), gq_ref[:, : 3 * D], gq_other_ref[:, : 3 * D]),
        (slice(3 * D, 4 * D + FF), gl_ref[:, : D + FF], gl_other_ref[:, : D + FF]),
    ):
        first, second, way = moments(own + other, wm_ref[:, lanes], wv_ref[:, lanes])
        wf_ref[:, lanes] = first
        ws_ref[:, lanes] = second
        wu_ref[:, lanes] = way + DECAY * ww_ref[:, lanes]
    count = ww_ref.shape[0]
    for part in range(FF // D):
        lanes = slice(D + FF + part * D, D + FF + (part + 1) * D)
        own = slice(part * count, (part + 1) * count)
        grad = gl_ref[:, lanes] + gl_other_ref[:, lanes]
        first, second, way = moments(grad, dm_ref[own, :], dv_ref[own, :])
        df_ref[own, :] = first
        ds_ref[own, :] = second
        du_ref[own, :] = way + DECAY * dw_ref[own, :]
    for base, wide, down in ((0, ww_ref, dw_ref), (4, wu_ref, du_ref)):
        for at, lanes in enumerate(MATRICES):
            sq_ref[base + at : base + at + 1, :] = lane_sums(wide[:, lanes])
        sq_ref[base + 3 : base + 4, :] = lane_sums(down[...])
    copies_ref[...] = jnp.broadcast_to(sq_ref[...][None], copies_ref.shape)


def update_kernel(
    sq_ref,
    ww_ref,
    wu_ref,
    we_ref,
    dw_ref,
    du_ref,
    de_ref,
    wn_ref,
    wa_ref,
    dn_ref,
    da_ref,
    norm_ref,
):
    total = jnp.sum(jnp.sum(sq_ref[...], axis=0), axis=1, keepdims=True)
    norm = jnp.sqrt(total)
    row = lax.broadcasted_iota(jnp.int32, (8, HALF), 0)
    lane = lax.broadcasted_iota(jnp.int32, (8, HALF), 1)
    for half in range(2):
        own = jnp.where(row == lane + 4 * half, norm, 0.0)
        norm_ref[half : half + 1, :] = jnp.sum(own, axis=0, keepdims=True)[:, 0:4]
    ratio = norm[0:4] / norm[4:8]
    keep = min(EMA_CEILING, (1.0 + STEP) / (10.0 + STEP))
    for at, lanes in enumerate(MATRICES):
        new = ww_ref[:, lanes] - (RATE * ratio[at : at + 1]) * wu_ref[:, lanes]
        wn_ref[:, lanes] = new
        wa_ref[:, lanes] = keep * we_ref[:, lanes] + (1.0 - keep) * new
    new = dw_ref[...] - (RATE * ratio[3:4]) * du_ref[...]
    dn_ref[...] = new
    da_ref[...] = keep * de_ref[...] + (1.0 - keep) * new


def plain(kernel, name, out_shape, *operands, scratch=()):
    small = pltpu.CompilerParams(vmem_limit_bytes=8 * 1024 * 1024)
    return pl.pallas_call(
        kernel,
        out_shape=out_shape,
        scratch_shapes=scratch,
        compiler_params=small,
        name=name,
    )(*operands)


def to_other(values):
    return lax.ppermute(values, "dp", [(0, 1), (1, 0)])


def copies(values, count):
    return jnp.broadcast_to(values[None], (count,) + values.shape)


def send_terms(values, count):
    return lax.all_to_all(values.reshape(count, -1, values.shape[-1]), "fsdp", 0, 0)


def add_terms(terms):
    return jnp.sum(terms.astype(F32), axis=0)


def on_device(
    count,
    tokens_in,
    cotangent,
    crop_count,
    wide_w,
    wide_m,
    wide_v,
    wide_ema,
    down_w,
    down_m,
    down_v,
    down_ema,
    small_p,
    small_m,
    small_v,
    small_ema,
):
    rows = wide_w.shape[0]
    narrow = small_p.shape[0] // rows
    small_low = jnp.pad(small_p.astype(BF).reshape(rows, narrow), ((0, 0), (0, HALF - narrow)))
    first = jnp.concatenate([wide_w[:, : 3 * D].astype(BF), small_low], axis=1)
    core = lax.axis_index("dp")
    half = lax.dynamic_slice_in_dim(first, core * (rows // 2), rows // 2, axis=0)
    half = send_terms(copies(half, count), count)
    hat, late_all = run_norm(tokens_in, wide_w, down_w, count)
    half, late_all, hat = lax.optimization_barrier((half, late_all, hat))
    late_all = send_terms(late_all, count).reshape(D, -1)
    other = to_other(half)
    first = [jnp.where(core == at, half, other) for at in range(2)]
    first = jnp.stack(first, axis=1).reshape(D, -1)
    table = first[:, 3 * D : 3 * D + narrow].astype(F32).reshape(-1, D)
    side = np.stack([tap_matrix(kind) for kind in range(3)])
    side = bf(side.transpose(0, 2, 1, 3).reshape(3, QROWS, 9 * QROWS))
    hat, att, win, e, il, o = run_attend(hat, first, table, side)
    block_out, dx, datt, g_late, sums, b_up = run_feed(
        rows, crop_count, tokens_in, cotangent, att, late_all, table
    )
    late = send_terms(g_late, count)
    spans = small_spans(rows, narrow)
    dqkv, g_last = run_back(
        spans, [datt, win, e, il, o, hat], first, table, sums, b_up, side
    )
    late, g_last = lax.optimization_barrier((late, g_last))
    late = add_terms(late)
    last = send_terms(g_last, count)
    late_other = to_other(late)
    late_other, dqkv = lax.optimization_barrier((late_other, dqkv))
    images = dqkv.shape[0]
    begin = images * 5 // 8
    grad_in = run_input(tokens_in, dqkv, dx, first, table, 0, begin)
    last, grad_in = lax.optimization_barrier((last, grad_in))
    last = add_terms(last)
    last_other = to_other(last)
    wide_like, down_like = sds(wide_w.shape, F32), sds(down_w.shape, F32)
    wide_first, wide_second, wide_upd, down_first, down_second, down_upd, squares = plain(
        moment_kernel,
        "moment",
        [wide_like] * 3 + [down_like] * 3 + [sds((count, 8, HALF), F32)],
        *(last, last_other, late, late_other),
        *(wide_w, wide_m, wide_v, down_w, down_m, down_v),
        scratch=[pltpu.VMEM((8, HALF), F32)],
    )
    squares, grad_in = lax.optimization_barrier((squares, grad_in))
    squares = send_terms(squares, count)
    grad_in = run_input(tokens_in, dqkv, dx, first, table, begin, images, grad_in)
    squares, grad_in = lax.optimization_barrier((squares, grad_in))
    wide_new, wide_avg, down_new, down_avg, norms = plain(
        update_kernel,
        "update",
        [wide_like] * 2 + [down_like] * 2 + [sds((2, 4), F32)],
        *(squares, wide_w, wide_upd, wide_ema, down_w, down_upd, down_ema),
    )
    shard_small = (last + last_other)[: spans[0][1], 3 * D :].reshape(-1)
    offset = lax.axis_index("fsdp") * (rows * narrow) % HALF
    shard_small = lax.dynamic_slice(shard_small, (offset,), (rows * narrow,))
    small_first, small_second, small_dir = moments(shard_small, small_m, small_v)
    small_new = small_p - RATE * small_dir
    ema_keep = min(EMA_CEILING, (1.0 + STEP) / (10.0 + STEP))
    small_avg = ema_keep * small_ema + (1.0 - ema_keep) * small_new
    return (
        block_out,
        grad_in,
        wide_new,
        wide_first,
        wide_second,
        wide_avg,
        down_new,
        down_first,
        down_second,
        down_avg,
        small_new,
        small_first,
        small_second,
        small_avg,
        norms,
    )


def solution(mesh):
    tok, row, vec = P(("dp", "fsdp"), None), P("fsdp", None), P("fsdp")
    in_specs = (tok, tok, P(("dp", "fsdp"))) + (row,) * 8 + (vec,) * 4
    out_specs = (tok, tok) + (row,) * 8 + (vec,) * 4 + (P(),)
    return jax.shard_map(
        functools.partial(on_device, mesh.shape["fsdp"]),
        mesh=mesh,
        in_specs=in_specs,
        out_specs=out_specs,
        check_vma=False,
    )
```

```python
import functools

import jax
import jax.numpy as jnp
import numpy as np
from jax import lax
from jax.experimental import pallas as pl
from jax.experimental.pallas import tpu as pltpu
from jax.sharding import PartitionSpec as P

D = 256
FF = 1024
HEAD = 32
STRIPE = 7
GRID_L = 14
GRID_S = 6
SMALL = 8
STEP = 10
TOK_IMG = 680

EPSILON = 1e-05
BETA_ONE = 0.9
BETA_TWO = 0.999
ADAM_EPS = 1e-06
DECAY = 0.05
RATE = 0.25
EMA_CEILING = 0.9999

ROWS = 688
BIG = 2 * GRID_L * GRID_L
PAIRS = 7
WIN = 128
QROWS = 112
HALF = 128
HEADS = 4
SCALE = HEAD**-0.5
LOG2E = 1.4426950408889634
CHUNKS = ((0, 240), (240, 464), (464, 688))
LONG = 744
EDGE = 16
COPIES = (3, 3, 2)
TAPS = tuple((dy, dx) for dy in (-1, 0, 1) for dx in (-1, 0, 1))
ORDER = (0, 2, 1, 3, 4, 5, 6)
VMEM = 60 * 1024 * 1024

BF = jnp.bfloat16
F32 = jnp.float32


def kind_of(pair):
    return 0 if pair < 2 else 1 if pair < 4 else 2


def branch_of(pair, member):
    return 0 if pair < 2 else 1 if pair < 4 else member


def first_of(pair, member):
    if pair < 2:
        return pair * GRID_L * GRID_L + member * STRIPE * GRID_L
    if pair < 4:
        return (pair - 2) * GRID_L * GRID_L + member * STRIPE
    return BIG + (pair - 4) * COPIES[0] * GRID_S * GRID_S


def tokens_of(pair):
    return STRIPE * GRID_L if pair < 4 else COPIES[pair - 4] * GRID_S * GRID_S


def shape_of(kind):
    return ((STRIPE, GRID_L), (GRID_L, STRIPE), (GRID_S, GRID_S))[kind]


def edge_masks():
    masks, places = [], {}
    for kind in range(3):
        high, broad = shape_of(kind)
        size = high * broad
        for dy, dx in TAPS:
            if (dy, dx) == (0, 0) or (kind < 2 and (dy != 0 or dx == 0)):
                continue
            mask = np.zeros((QROWS, HALF), np.float32)
            for at in range(size * (1 if kind < 2 else COPIES[0])):
                r, c = divmod(at % size, broad)
                mask[at] = 0 <= r + dy < high and 0 <= c + dx < broad
            places[kind, dy, dx] = len(masks)
            masks.append(mask)
    return np.stack(masks), places


def tap_matrix(kind):
    shape = shape_of(kind)
    copies = 1 if kind < 2 else COPIES[0]
    size = shape[0] * shape[1]
    out = np.zeros((9, QROWS, QROWS), np.float32)
    for copy in range(copies):
        for r in range(shape[0]):
            for c in range(shape[1]):
                for tap in range(9):
                    rr, cc = r + tap // 3 - 1, c + tap % 3 - 1
                    if 0 <= rr < shape[0] and 0 <= cc < shape[1]:
                        out[tap, copy * size + r * shape[1] + c, copy * size + rr * shape[1] + cc] = 1
    return out


def mask_operands():
    size = GRID_S * GRID_S
    rows = np.zeros((3, 2, QROWS, HALF), np.float32)
    keys = np.zeros((3, HALF // 2, WIN), np.float32)
    for kind, crops in ((0, 1), (1, 3), (2, 2)):
        count = STRIPE * GRID_L if kind == 0 else crops * size
        each = count // crops
        for at in range(QROWS):
            rows[kind, 0, at, HALF // 2 + (at // each if at < count else 0)] = 1
        for at in range(WIN):
            for crop in range(crops):
                if at >= count or at // each != crop:
                    keys[kind, crop, at] = -1e30
    rows[:, 1, :, : HALF // 2] = rows[:, 0, :, HALF // 2 :]
    return rows, np.tile(keys, (1, 1, 2))


def bf(array):
    return jnp.asarray(array, BF)


def dot(left, right):
    return jnp.dot(left, right, preferred_element_type=F32)


def dot_nt(left, right):
    return lax.dot_general(left, right, (((1,), (1,)), ((), ())), preferred_element_type=F32)


def dot_tn(left, right):
    return lax.dot_general(left, right, (((0,), (0,)), ((), ())), preferred_element_type=F32)


def normalise(values):
    center = values - jnp.mean(values, axis=-1, keepdims=True)
    spread = jnp.mean(center * center, axis=-1, keepdims=True)
    scale = lax.rsqrt(spread + EPSILON)
    return center * scale, scale


def norm_back(grad_hat, hat, scale):
    mean_grad = jnp.mean(grad_hat, axis=-1, keepdims=True)
    mean_dot = jnp.mean(grad_hat * hat, axis=-1, keepdims=True)
    return scale * (grad_hat - mean_grad - hat * mean_dot)


def rows_of(ref, low, high):
    if high <= TOK_IMG:
        return ref[low:high, :]
    tail = jnp.zeros((high - TOK_IMG, ref.shape[1]), F32)
    return jnp.concatenate([ref[low:TOK_IMG, :], tail], axis=0)


def store_rows(ref, low, high, values):
    last = min(high, TOK_IMG)
    ref[low:last, :] = values[: last - low]


def with_ones(turned):
    return jnp.concatenate([turned, jnp.ones((16, turned.shape[1]), turned.dtype)], axis=0)


def fold(values):
    return jnp.sum(values.reshape(values.shape[0] // 8, 8, values.shape[1]), axis=0)


def head_lanes(head):
    lanes = lax.broadcasted_iota(jnp.int32, (1, HALF), 1)
    return jnp.where(lanes // HEAD == head, 1.0, 0.0).astype(BF)


def by_head(values):
    return jnp.concatenate([values * head_lanes(h) for h in range(HEADS)], axis=0)


def lane_half(upper):
    lanes = lax.broadcasted_iota(jnp.int32, (1, HALF), 1)
    return jnp.where((lanes >= HALF // 2) == upper, 1.0, 0.0).astype(BF)


def two_heads(turned, pair):
    low = pair * 2 * HEAD
    none = jnp.zeros((HEAD, WIN), turned.dtype)
    first = jnp.concatenate([turned[low : low + HEAD], none], axis=1)
    second = jnp.concatenate([none, turned[low + HEAD : low + 2 * HEAD]], axis=1)
    return jnp.concatenate([first, second], axis=0)


def by_two_heads(left, other, turned, added, rest=None):
    low, high = lane_half(False), lane_half(True)
    none = jnp.zeros_like(added)
    first = [two_heads(turned, 0), added, none, added]
    second = [added, two_heads(turned, 1), added, none]
    lefts = [left * low + other[0], left * high + other[1]]
    if rest is None:
        first, second = first[:2], second[:2]
    else:
        lefts = [jnp.concatenate([part, rest], axis=1) for part in lefts]
    first = dot(lefts[0], jnp.concatenate(first, axis=0))
    second = dot(lefts[1], jnp.concatenate(second, axis=0))
    return [first[:, :WIN], first[:, WIN:], second[:, :WIN], second[:, WIN:]]


def taps_of(table, branch):
    return table[5:14, branch * HALF : (branch + 1) * HALF]


def first_rows(values, count):
    low = count // 16 * 16
    if low >= values.shape[0]:
        return values
    row = lax.broadcasted_iota(jnp.int32, (values.shape[0] - low, 1), 0)
    tail = jnp.where(row < count - low, values[low:], 0.0)
    return jnp.concatenate([values[:low], tail], axis=0)


def pieces_of(pair, member):
    low = first_of(pair, member)
    return [(low + r * GRID_L, r * STRIPE) for r in range(GRID_L)]


def pipelined(stages, order, extra=()):
    extra = dict(extra)
    state = {item: {} for item in order}
    for turn in range(len(order) + max(lag for lag, _ in stages)):
        if turn in extra:
            extra[turn]()
        running = []
        for lag, stage in stages:
            if 0 <= turn - lag < len(order):
                item = order[turn - lag]
                running.append(stage(item, state[item]))
        while running:
            running = [stage for stage in running if next(stage, True) is None]


def norm_kernel(x_ref, wide_ref, down_ref, hat_ref, late_ref):
    for low in range(0, x_ref.shape[0], TOK_IMG // 5):
        hat_ref[low : low + TOK_IMG // 5, :] = normalise(x_ref[low : low + TOK_IMG // 5, :])[0]

    @pl.when(pl.program_id(0) == 0)
    def _():
        rows = wide_ref.shape[0]
        pieces = [wide_ref[:, 3 * D :]]
        pieces += [down_ref[at : at + rows, :] for at in range(0, down_ref.shape[0], rows)]
        late = jnp.concatenate(pieces, axis=1).astype(BF)
        for owner in range(late_ref.shape[0]):
            late_ref[owner] = late


def attend_kernel(
    x_ref,
    w_ref,
    s_ref,
    tap_ref,
    mrow_ref,
    mkey_ref,
    hat_ref,
    att_ref,
    win_ref,
    e_ref,
    il_ref,
    o_ref,
    qkv_scr,
    turn_scr,
    back_scr,
    att_scr,
):
    @pl.when(pl.program_id(0) == 0)
    def _():
        for branch in range(2):
            qkv_scr[branch, ROWS:, :] = jnp.zeros((LONG - ROWS, 3 * HALF), F32)
        turn_scr[...] = jnp.zeros_like(turn_scr)
        att_scr[TOK_IMG:, :] = jnp.zeros((ROWS - TOK_IMG, D), F32)

    gain, shift = s_ref[0:1, :], s_ref[1:2, :]
    ones = jnp.concatenate(
        [jnp.broadcast_to(head_lanes(h), (WIN, HALF)) for h in range(HEADS)], axis=0
    )

    def project(chunk):
        low, high = CHUNKS[chunk]
        hat = rows_of(x_ref, low, high)
        hat_ref[0, low:high, :] = hat.astype(BF)
        a = (hat * gain + shift).astype(BF)
        for part in range(3):
            lanes = slice(part * D, (part + 1) * D)
            piece = dot(a, w_ref[:, lanes]) + s_ref[2 + part : 3 + part, :]
            for branch in range(2):
                qkv_scr[branch, low:high, part * HALF : (part + 1) * HALF] = piece[
                    :, branch * HALF : (branch + 1) * HALF
                ]

    none = jnp.zeros((WIN - QROWS, HALF), BF)

    def cut(pair, state):
        for member in range(2):
            at = 2 * pair + member
            if kind_of(pair) == 1:
                for source, target in pieces_of(pair, member):
                    turn_scr[at - 4, target : target + STRIPE, :] = qkv_scr[
                        1, source : source + STRIPE, :
                    ]
                window = turn_scr[at - 4, :QROWS, :]
            else:
                low = first_of(pair, member)
                window = qkv_scr[branch_of(pair, member), low : low + QROWS, :]
            window = window.astype(BF)
            win_ref[0, at] = window
            state[member] = [window[:, part * HALF : (part + 1) * HALF] for part in range(3)]
            yield

    def score(pair, state):
        mask = 0 if pair < 4 else 1 if pair < 6 else 2
        for member in range(2):
            q, k, v = state[member]
            k = jnp.concatenate([k, none], axis=0).T
            rows = mrow_ref[mask, 0], mrow_ref[mask, 1]
            state[member] = v, by_two_heads(q, rows, k, mkey_ref[mask])
            yield

    def soften(pair, state):
        for member in range(2):
            v, scores = state[member]
            exps = []
            for part in scores:
                peak = jnp.max(part, axis=-1, keepdims=True)
                exps.append(jnp.exp2((part - peak) * (SCALE * LOG2E)).astype(BF))
            e = jnp.concatenate(exps, axis=1)
            e_ref[0, 2 * pair + member] = e
            state[member] = v, e
            yield

    def mix(pair, state):
        taps = []
        for member in range(2):
            v, e = state[member]
            low = taps_of(s_ref, branch_of(pair, member)).astype(BF)
            keys = jnp.concatenate([v, none], axis=0)
            state[member] = dot(e, jnp.concatenate([by_head(keys), ones], axis=1))
            taps.append(jnp.concatenate([v * low[tap : tap + 1] for tap in range(9)], axis=0))
            yield
        state[2] = dot(tap_ref[kind_of(pair)], jnp.concatenate(taps, axis=1))
        yield

    def put(pair, state):
        for member in range(2):
            at = 2 * pair + member
            branch = branch_of(pair, member)
            lanes = slice(branch * HALF, (branch + 1) * HALF)
            both = state[member]
            inv = 1.0 / both[:, HALF:]
            o = both[:, :HALF] * inv
            il_ref[0, at] = inv
            o_ref[0, at] = o
            conv = state[2][:, member * HALF : (member + 1) * HALF]
            piece = o + s_ref[14:15, lanes] + conv
            if kind_of(pair) == 1:
                back_scr[at - 4] = piece
                for source, target in pieces_of(pair, member):
                    att_scr[source : source + STRIPE, lanes] = back_scr[
                        at - 4, target : target + STRIPE, :
                    ]
            else:
                low, count = first_of(pair, member), tokens_of(pair)
                att_scr[low : low + count, lanes] = piece[:count]
            yield

    project(0)
    extra = {1: functools.partial(project, 1), 3: functools.partial(project, 2)}
    stages = enumerate((cut, score, soften, mix, put))
    pipelined(tuple(stages), ORDER, extra)
    att_ref[0] = att_scr[...].astype(BF)


def gelu_parts(u):
    above = lax.erf(u * 2**-0.5) + 1.0
    decay = jnp.exp2((u * u) * (-0.5 * LOG2E))
    return u * above, above + (u * decay) * (2 / np.pi) ** 0.5


def beside(*streams):
    left = [[list(stream), 0] for stream in streams]
    total = max((len(steps) for steps, _ in left), default=0)
    for at in range(total):
        for entry in left:
            steps, done = entry
            goal = -(-len(steps) * (at + 1) // total)
            for step in steps[done:goal]:
                step()
            entry[1] = goal


def weight_terms(grad, weight, bias):
    terms = []
    for value in (weight * bias,) if grad is None else (weight * grad, weight * bias):
        column = jnp.sum(value, axis=1, keepdims=True)
        terms.append(jnp.broadcast_to(column, (D, HALF)).T[0:1, :])
    return terms


def down_blocks(shard):
    parts = FF // D
    return [(i, part, (i * parts + part) * shard) for i in range(D // shard) for part in range(parts)]


def feed_kernel(
    shard,
    cnt_ref,
    x_ref,
    c_ref,
    att_ref,
    w_ref,
    s_ref,
    out_ref,
    dx_ref,
    datt_ref,
    pack_ref,
    sums_ref,
    bup_ref,
    rs_scr,
    x1_scr,
    gup_scr,
    gdn_scr,
    gout_scr,
    turn_scr,
    pack_scr,
    down_scr,
):
    image = pl.program_id(0)

    @pl.when(image == 0)
    def _():
        for ref in (gup_scr, gdn_scr, gout_scr, sums_ref, bup_ref):
            ref[...] = jnp.zeros_like(ref)
        pack_scr[...] = w_ref[:, D + FF :].astype(F32)
        for owner, part, low in down_blocks(shard):
            turn_scr[low : low + shard, :] = pack_scr[
                owner * shard : (owner + 1) * shard, part * D : (part + 1) * D
            ]
        down_scr[...] = turn_scr[...].astype(BF)

    bound = BIG + GRID_S * GRID_S * cnt_ref[image]
    bias_out, gain, shift = s_ref[15:16, :], s_ref[16:17, :], s_ref[17:18, :]
    lanes_of = [slice(part * D, (part + 1) * D) for part in range(FF // D)]
    count = 16
    rows = range(0, ROWS, count)
    biases = [s_ref[18 + part : 19 + part, :] for part in range(FF // D)]
    sums = {}
    held = {}

    def add_sum(key, values, at, ref, *index):
        sums[key] = sums[key] + fold(values) if key in sums else fold(values)
        if at + count >= ROWS:
            ref[index] += sums[key]

    def keep(key, at, values):
        held.setdefault(key, []).append(values)
        if at + count >= ROWS:
            held[key] = jnp.concatenate(held[key], axis=0)

    def masked(at):
        row = at + lax.broadcasted_iota(jnp.int32, (count, 1), 0)
        return jnp.where(row < bound, rows_of(c_ref, at, at + count), 0.0)

    def cot(at):
        dy = masked(at)
        keep("dy", at, dy.astype(BF))
        add_sum("dy", dy, at, sums_ref, 0)

    def project():
        held["x1"] = dot(att_ref[0], w_ref[:, :D])

    def norm(at):
        own = slice(at, at + count)
        x1 = rows_of(x_ref, at, at + count) + held["x1"][own] + bias_out
        x1_scr[own, :] = x1
        hat, scale = normalise(x1)
        rs_scr[own, :] = scale
        keep("hat", at, hat.astype(BF))
        keep("h2", at, (hat * gain + shift).astype(BF))

    def hidden(part):
        cols = slice(D + part * D, D + (part + 1) * D)
        held["v", part] = dot(held["h2"], w_ref[:, cols])

    def hidden_back(part):
        held["dg", part] = dot_nt(held["dy"], down_scr[lanes_of[part], :])

    def gelu(part, at):
        own = slice(at, at + count)
        v = held["v", part][own] + biases[part]
        g, slope = gelu_parts(v)
        keep(("g", part), at, g.astype(BF))
        du = held["dg", part][own] * slope
        keep(("du", part), at, du.astype(BF))

    def gelus(part):
        return [functools.partial(gelu, part, at) for at in rows]

    def grad_up(part):
        both = dot(held["hat_t"], held["du", part])
        gup_scr[:, lanes_of[part]] += both[:D]
        bup_ref[:, lanes_of[part]] += both[D : D + 8]

    def grad_down(part):
        gdn_scr[:, lanes_of[part]] += dot(held["dy_t"], held["g", part])

    def joined(key, *parts):
        return jnp.concatenate([held[key, part] for part in parts], axis=1)

    half = FF // 2

    def out_first():
        held["out"] = dot(joined("g", 0, 1), down_scr[:half, :])

    def out_last():
        held["out"] += dot(joined("g", 2, 3), down_scr[half:, :])

    def out_store(at):
        own = slice(at, at + count)
        out = x1_scr[own, :] + held["out"][own] * 0.5 + s_ref[22:23, :]
        store_rows(out_ref, at, at + count, out)

    def back_first():
        held["dh"] = dot_nt(joined("du", 0, 1), w_ref[:, D : D + half])

    def back_last():
        held["dh"] += dot_nt(joined("du", 2, 3), w_ref[:, D + half : D + FF])

    def norm_grad(at):
        own = slice(at, at + count)
        hat = held["hat"][own].astype(F32)
        dx = masked(at) + norm_back(held["dh"][own] * (gain * 0.5), hat, rs_scr[own, :])
        store_rows(dx_ref, at, at + count, dx)
        keep("dz", at, dx.astype(BF))
        add_sum("dz", dx, at, sums_ref, 1)

    def attention():
        datt = dot_nt(held["dz"], w_ref[:, :D])
        datt_ref[0] = datt.astype(BF)

    def grad_out():
        gout_scr[...] += dot_tn(att_ref[0], held["dz"])

    def each(step, *parts):
        return [functools.partial(step, part) for part in parts]

    def turn(key):
        held[key + "_t"] = held[key].T

    beside(each(cot, *rows), [project])
    turn("dy")
    beside(each(norm, *rows), each(hidden_back, 0, 1, 2, 3))
    turn("hat")
    held["hat_t"] = with_ones(held["hat_t"])
    hidden(0)
    beside(each(hidden, 1, 2, 3), gelus(0))
    beside(each(grad_up, 0) + each(grad_down, 0), gelus(1))
    beside([back_first] + each(grad_up, 1) + each(grad_down, 1), gelus(2))
    beside([out_first] + each(grad_up, 2) + each(grad_down, 2), gelus(3))
    back_last()
    beside([out_last] + each(grad_up, 3) + each(grad_down, 3), each(norm_grad, *rows))
    beside([attention, grad_out], each(out_store, *rows))

    @pl.when(image == pl.num_programs(0) - 1)
    def _():
        turn_scr[...] = gdn_scr[...].T * 0.5
        for owner, part, low in down_blocks(shard):
            pack_scr[owner * shard : (owner + 1) * shard, part * D : (part + 1) * D] = turn_scr[
                low : low + shard, :
            ]
        bup_ref[...] *= 0.5
        bias = bup_ref[0:1, :]
        grad = gup_scr[...] * 0.5
        terms = weight_terms(grad, w_ref[:, D : D + FF].astype(F32), bias)
        out_bias = jnp.sum(sums_ref[1], axis=0, keepdims=True)
        terms += weight_terms(None, w_ref[:, :D].astype(F32), out_bias)
        for at, term in enumerate(terms):
            sums_ref[2 + at, 0:1, :] = term
        columns = s_ref[15:23, :].T
        grad = columns[:, 1:2] * grad + columns[:, 2:3] * bias
        pack_ref[:, :D] = gout_scr[...].astype(BF)
        pack_ref[:, D : D + FF] = grad.astype(BF)
        pack_ref[:, D + FF :] = pack_scr[...].astype(BF)


def small_spans(shard, narrow):
    count = D // shard
    own = shard * narrow
    rows = max((own * (i + 1) - 1) // HALF - own * i // HALF + 1 for i in range(count))
    return [(own * i // HALF, rows) for i in range(count)]


def back_kernel(
    spans,
    places,
    datt_ref,
    win_ref,
    e_ref,
    il_ref,
    o_ref,
    hat_ref,
    w_ref,
    s_ref,
    feed_ref,
    bup_ref,
    tap_ref,
    edge_ref,
    dqkv_ref,
    pack_ref,
    g_scr,
    kern_scr,
    bias_scr,
    datt_scr,
    grad_scr,
    turn_scr,
    pad_scr,
    back_scr,
    dqkv_scr,
    small_scr,
    pack_scr,
):
    image = pl.program_id(0)

    @pl.when(image == 0)
    def _():
        for ref in (g_scr, kern_scr, bias_scr, turn_scr, pad_scr, small_scr, pack_scr):
            ref[...] = jnp.zeros_like(ref)
        datt_scr[ROWS:, :] = jnp.zeros((LONG - ROWS, D), F32)
        dqkv_scr[TOK_IMG:, :] = jnp.zeros((ROWS - TOK_IMG, 3 * D), F32)

    for low, high in CHUNKS:
        datt_scr[low:high, :] = datt_ref[0, low:high, :].astype(F32)
    minus = two_heads(jnp.full((HALF, WIN), -1.0, BF), 0)
    none = jnp.zeros((WIN - QROWS, HALF), BF)

    def weigh(pair, state):
        for member in range(2):
            at = 2 * pair + member
            branch = branch_of(pair, member)
            lanes = slice(branch * HALF, (branch + 1) * HALF)
            if kind_of(pair) == 1:
                for source, target in pieces_of(pair, member):
                    turn_scr[at - 4, target : target + STRIPE, :] = datt_scr[
                        source : source + STRIPE, lanes
                    ]
                grad = turn_scr[at - 4]
            else:
                low = first_of(pair, member)
                grad = first_rows(datt_scr[low : low + QROWS, lanes], tokens_of(pair))
            grad_scr[at * QROWS : (at + 1) * QROWS, :] = grad
            v = win_ref[0, at, :, 2 * HALF :]
            pad_scr[at, EDGE : EDGE + QROWS, :] = first_rows(v.astype(F32), tokens_of(pair))
            dn = (grad * il_ref[0, at]).astype(BF)
            z = pltpu.roll(dn.astype(F32) * o_ref[0, at], HALF // 2, 1)
            high = z.astype(BF)
            rows = high * lane_half(True), high * lane_half(False)
            rest = (z - high.astype(F32)).astype(BF)
            v = jnp.concatenate([v, none], axis=0).T
            state[member] = grad, dn, by_two_heads(dn, rows, v, minus, rest)
            yield

    def score(pair, state):
        for member in range(2):
            grad, dn, weighed = state[member]
            e = e_ref[0, 2 * pair + member]
            ds = jnp.concatenate(weighed, axis=1).astype(BF) * e
            state[member] = grad, dn, ds, e
            yield

    def spread(pair, state):
        kind = kind_of(pair)
        taps = []
        for member in range(2):
            grad, dn, ds, e = state[member]
            at = 2 * pair + member
            kernel = taps_of(s_ref, branch_of(pair, member)).astype(BF)
            q = win_ref[0, at, :, 0:HALF]
            k = jnp.concatenate([win_ref[0, at, :, HALF : 2 * HALF], none], axis=0)
            dq = dot(ds, by_head(k))
            row = 2 * PAIRS * QROWS + 8 * at
            grad_scr[row : row + 8, :] = dq[:8]
            q_t, dn_t = q.T, dn.T
            dk, dv = [], []
            for half in range(2):
                lanes = slice(2 * half * WIN, 2 * (half + 1) * WIN)
                own = slice(2 * half * HEAD, 2 * (half + 1) * HEAD)
                for parts, left, right in ((dk, q_t, ds), (dv, dn_t, e)):
                    both = dot(left[own], right[:, lanes])
                    parts += [both[:HEAD, :WIN], both[HEAD:, WIN:]]
            state[member] = dq, dk, dv
            low = grad.astype(BF)
            taps.append(
                jnp.concatenate([low * kernel[8 - tap : 9 - tap] for tap in range(9)], axis=0)
            )
            yield
        state[2] = dot(tap_ref[kind], jnp.concatenate(taps, axis=1))
        yield

    def kernels(pair, state):
        kind = kind_of(pair)
        broad = shape_of(kind)[1]
        for member in range(2):
            at = 2 * pair + member
            base = pl.multiple_of(at * QROWS + image // 4096 * 8, 8)
            totals = [jnp.zeros((8, HALF), F32)] * 9
            for low in range(0, tokens_of(pair), 8):
                own = slice(low, low + 8)
                grad = grad_scr[pl.ds(pl.multiple_of(base + low, 8), 8), :]
                sides = {}
                for tap, (dy, dx) in enumerate(TAPS):
                    place = places.get((kind, 0 if kind < 2 else dy, dx))
                    if place not in sides:
                        mask = 1.0 if place is None else edge_ref[place, own, :]
                        sides[place] = grad * mask
                    start = EDGE + low + dy * broad + dx
                    totals[tap] = totals[tap] + sides[place] * pad_scr[at, start : start + 8, :]
            for tap in range(9):
                kern_scr[branch_of(pair, member), tap] += totals[tap]
            yield

    def put(pair, state):
        for member in range(2):
            at = 2 * pair + member
            branch = branch_of(pair, member)
            dq, dk, dv = state[member]
            dk = jnp.concatenate(dk, axis=0).T[:QROWS] * SCALE
            dv = jnp.concatenate(dv, axis=0).T[:QROWS]
            dv = dv + state[2][:, member * HALF : (member + 1) * HALF]
            for part, piece in enumerate((dq * SCALE, dk, dv)):
                lanes = slice(part * D + branch * HALF, part * D + (branch + 1) * HALF)
                if kind_of(pair) == 1:
                    back_scr[at - 4, part] = piece
                    for source, target in pieces_of(pair, member):
                        dqkv_scr[source : source + STRIPE, lanes] = back_scr[
                            at - 4, part, target : target + STRIPE, :
                        ]
                else:
                    low, count = first_of(pair, member), tokens_of(pair)
                    dqkv_scr[low : low + count, lanes] = piece[:count]
            yield

    pipelined(((3, kernels), (0, weigh), (1, score), (2, spread), (3, put)), ORDER)
    dqkv = dqkv_scr[...].astype(BF)
    dqkv_ref[0] = dqkv
    both = dot(with_ones(hat_ref[0].T), dqkv)
    g_scr[...] += both[:D]
    bias_scr[...] += both[D : D + 8]

    @pl.when(image == pl.num_programs(0) - 1)
    def _():
        def put(row, terms):
            for at in range(0, terms.shape[1], HALF):
                small_scr[row : row + 1, :] = terms[:, at : at + HALF]
                row += 1

        total = lambda terms: jnp.sum(terms, axis=0, keepdims=True)
        bias = bias_scr[0:1, :]
        gain, shift = weight_terms(g_scr[...], w_ref[:, : 3 * D].astype(F32), bias)
        put(0, gain)
        put(2, shift)
        put(4, bias)
        for tap in range(9):
            for branch in range(2):
                put(10 + 2 * tap + branch, total(kern_scr[branch, tap]))
        for row, entry in ((30, 1), (44, 0)):
            put(row, total(feed_ref[entry]))
        for row, entry in ((32, 2), (34, 3), (28, 4)):
            put(row, feed_ref[entry, 0:1, :])
        put(36, bup_ref[0:1, :])
        for owner, (row, rows) in enumerate(spans):
            shard = D // len(spans)
            pack_scr[owner * shard : owner * shard + rows, :] = small_scr[row : row + rows, :]
        columns = s_ref[0:8, :].T
        grad = columns[:, 0:1] * g_scr[...] + columns[:, 1:2] * bias
        pack_ref[:, : 3 * D] = grad.astype(BF)
        pack_ref[:, 3 * D :] = pack_scr[...].astype(BF)


def input_kernel(x_ref, dqkv_ref, dx_ref, w_ref, s_ref, *out_refs):
    out_ref = out_refs[-1]
    for low, high in CHUNKS:
        dh = dot_nt(dqkv_ref[0, low:high, :], w_ref[:, : 3 * D])
        hat, scale = normalise(rows_of(x_ref, low, high))
        grad = rows_of(dx_ref, low, high) + norm_back(dh * s_ref[0:1, :], hat, scale)
        store_rows(out_ref, low, high, grad)


def whole(shape):
    return pl.BlockSpec(shape, lambda i, *_: (0,) * len(shape))


def image_of(shape):
    return pl.BlockSpec((1,) + shape, lambda i, *_: (i,) + (0,) * len(shape))


def tokens():
    return pl.BlockSpec((TOK_IMG, D), lambda i, *_: (i, 0))


def params(room=0):
    return pltpu.CompilerParams(
        vmem_limit_bytes=VMEM - room * 1024 * 1024, dimension_semantics=("arbitrary",)
    )


def sds(shape, dtype):
    return jax.ShapeDtypeStruct(shape, dtype)


def run_norm(tokens_in, wide, down, count):
    rows = TOK_IMG * 2
    block = pl.BlockSpec((rows, D), lambda i: (i, 0))
    late = (count, wide.shape[0], D + 2 * FF)
    return pl.pallas_call(
        norm_kernel,
        grid=(tokens_in.shape[0] // rows,),
        in_specs=[block, whole(wide.shape), whole(down.shape)],
        out_specs=[block, whole(late)],
        out_shape=[sds(tokens_in.shape, F32), sds(late, BF)],
        compiler_params=params(),
        name="norm",
    )(tokens_in, wide, down)


def run_attend(tokens_in, w_qkv, table, side):
    images = tokens_in.shape[0] // TOK_IMG
    mrow, mkey = mask_operands()
    consts = [table, side, bf(mrow), bf(mkey)]
    outs = [
        ((ROWS, D), BF),
        ((ROWS, D), BF),
        ((2 * PAIRS, QROWS, 3 * HALF), BF),
        ((2 * PAIRS, QROWS, HEADS * WIN), BF),
        ((2 * PAIRS, QROWS, HALF), F32),
        ((2 * PAIRS, QROWS, HALF), F32),
    ]
    return pl.pallas_call(
        attend_kernel,
        grid=(images,),
        in_specs=[tokens(), whole(w_qkv.shape)] + [whole(c.shape) for c in consts],
        out_specs=[image_of(shape) for shape, _ in outs],
        out_shape=[sds((images,) + shape, dtype) for shape, dtype in outs],
        scratch_shapes=[
            pltpu.VMEM((2, LONG, 3 * HALF), F32),
            pltpu.VMEM((4, QROWS, 3 * HALF), F32),
            pltpu.VMEM((4, QROWS, HALF), F32),
            pltpu.VMEM((ROWS, D), F32),
        ],
        compiler_params=params(-3),
        name="attend",
    )(tokens_in, w_qkv, *consts)


def run_feed(shard, counts, tokens_in, cotangent, att, wide, table):
    images = tokens_in.shape[0] // TOK_IMG
    return pl.pallas_call(
        functools.partial(feed_kernel, shard),
        grid_spec=pltpu.PrefetchScalarGridSpec(
            num_scalar_prefetch=1,
            grid=(images,),
            in_specs=[
                tokens(),
                tokens(),
                image_of((ROWS, D)),
                whole(wide.shape),
                whole(table.shape),
            ],
            out_specs=[
                tokens(),
                tokens(),
                image_of((ROWS, D)),
                whole((D, D + 2 * FF)),
                whole((5, 8, D)),
                whole((8, FF)),
            ],
            scratch_shapes=[
                pltpu.VMEM((ROWS, 1), F32),
                pltpu.VMEM((ROWS, D), F32),
                pltpu.VMEM((D, FF), F32),
                pltpu.VMEM((D, FF), F32),
                pltpu.VMEM((D, D), F32),
                pltpu.VMEM((FF, D), F32),
                pltpu.VMEM((D, FF), F32),
                pltpu.VMEM((FF, D), BF),
            ],
        ),
        out_shape=[
            sds(tokens_in.shape, F32),
            sds(tokens_in.shape, F32),
            sds((images, ROWS, D), BF),
            sds((D, D + 2 * FF), BF),
            sds((5, 8, D), F32),
            sds((8, FF), F32),
        ],
        compiler_params=params(),
        name="feed",
    )(counts, tokens_in, cotangent, att, wide, table)


def run_back(spans, blocks, w_qkv, table, sums, b_up, side):
    images = blocks[0].shape[0]
    masks, places = edge_masks()
    consts = [w_qkv, table, sums, b_up, side, jnp.asarray(masks)]
    return pl.pallas_call(
        functools.partial(back_kernel, spans, places),
        grid=(images,),
        in_specs=[image_of(b.shape[1:]) for b in blocks] + [whole(c.shape) for c in consts],
        out_specs=[image_of((ROWS, 3 * D)), whole((D, 3 * D + HALF))],
        out_shape=[sds((images, ROWS, 3 * D), BF), sds((D, 3 * D + HALF), BF)],
        scratch_shapes=[
            pltpu.VMEM((D, 3 * D), F32),
            pltpu.VMEM((2, 9, 8, HALF), F32),
            pltpu.VMEM((8, 3 * D), F32),
            pltpu.VMEM((LONG, D), F32),
            pltpu.VMEM((2 * PAIRS * (QROWS + 8), HALF), F32),
            pltpu.VMEM((4, QROWS, HALF), F32),
            pltpu.VMEM((2 * PAIRS, QROWS + 2 * EDGE, HALF), F32),
            pltpu.VMEM((4, 3, QROWS, HALF), F32),
            pltpu.VMEM((ROWS, 3 * D), F32),
            pltpu.VMEM((56, HALF), F32),
            pltpu.VMEM((D, HALF), F32),
        ],
        compiler_params=params(),
        name="back",
    )(*blocks, *consts)


def run_input(tokens_in, dqkv, dx, w_qkv, table, low, high, out=None):
    own = pl.BlockSpec((TOK_IMG, D), lambda i: (low + i, 0))
    rows = pl.BlockSpec((1, ROWS, 3 * D), lambda i: (low + i, 0, 0))
    ends = [] if out is None else [out]
    return pl.pallas_call(
        input_kernel,
        grid=(high - low,),
        in_specs=[own, rows, own, whole(w_qkv.shape), whole(table.shape)]
        + [pl.BlockSpec(memory_space=pl.ANY) for _ in ends],
        out_specs=own,
        out_shape=sds(tokens_in.shape, F32),
        input_output_aliases={5: 0} if ends else {},
        compiler_params=params(),
        cost_estimate=pl.CostEstimate(
            flops=(high - low) * 2 * ROWS * 3 * D * D,
            bytes_accessed=(high - low) * ROWS * D * 18,
            transcendentals=0,
        ),
        name="input_grad",
    )(tokens_in, dqkv, dx, w_qkv, table, *ends)


def moments(grad, first, second):
    first_new = BETA_ONE * first + (1.0 - BETA_ONE) * grad
    second_new = BETA_TWO * second + (1.0 - BETA_TWO) * grad * grad
    direction = (
        first_new
        / (1.0 - BETA_ONE**STEP)
        / (jnp.sqrt(second_new / (1.0 - BETA_TWO**STEP)) + ADAM_EPS)
    )
    return (first_new, second_new, direction)


MATRICES = (slice(0, 3 * D), slice(3 * D, 4 * D), slice(4 * D, 4 * D + FF))


def lane_sums(values):
    column = jnp.sum(values * values, axis=0, keepdims=True)
    parts = [column[:, at : at + HALF] for at in range(0, column.shape[1], HALF)]
    return functools.reduce(jnp.add, parts)


def moment_kernel(
    gq_ref,
    gq_other_ref,
    gl_ref,
    gl_other_ref,
    ww_ref,
    wm_ref,
    wv_ref,
    dw_ref,
    dm_ref,
    dv_ref,
    wf_ref,
    ws_ref,
    wu_ref,
    df_ref,
    ds_ref,
    du_ref,
    copies_ref,
    sq_ref,
):
    for lanes, own, other in (
        (slice(0, 3 * D), gq_ref[:, : 3 * D], gq_other_ref[:, : 3 * D]),
        (slice(3 * D, 4 * D + FF), gl_ref[:, : D + FF], gl_other_ref[:, : D + FF]),
    ):
        first, second, way = moments(own + other, wm_ref[:, lanes], wv_ref[:, lanes])
        wf_ref[:, lanes] = first
        ws_ref[:, lanes] = second
        wu_ref[:, lanes] = way + DECAY * ww_ref[:, lanes]
    count = ww_ref.shape[0]
    for part in range(FF // D):
        lanes = slice(D + FF + part * D, D + FF + (part + 1) * D)
        own = slice(part * count, (part + 1) * count)
        grad = gl_ref[:, lanes] + gl_other_ref[:, lanes]
        first, second, way = moments(grad, dm_ref[own, :], dv_ref[own, :])
        df_ref[own, :] = first
        ds_ref[own, :] = second
        du_ref[own, :] = way + DECAY * dw_ref[own, :]
    for base, wide, down in ((0, ww_ref, dw_ref), (4, wu_ref, du_ref)):
        for at, lanes in enumerate(MATRICES):
            sq_ref[base + at : base + at + 1, :] = lane_sums(wide[:, lanes])
        sq_ref[base + 3 : base + 4, :] = lane_sums(down[...])
    copies_ref[...] = jnp.broadcast_to(sq_ref[...][None], copies_ref.shape)


def update_kernel(
    sq_ref,
    ww_ref,
    wu_ref,
    we_ref,
    dw_ref,
    du_ref,
    de_ref,
    wn_ref,
    wa_ref,
    dn_ref,
    da_ref,
    norm_ref,
):
    total = jnp.sum(jnp.sum(sq_ref[...], axis=0), axis=1, keepdims=True)
    norm = jnp.sqrt(total)
    row = lax.broadcasted_iota(jnp.int32, (8, HALF), 0)
    lane = lax.broadcasted_iota(jnp.int32, (8, HALF), 1)
    for half in range(2):
        own = jnp.where(row == lane + 4 * half, norm, 0.0)
        norm_ref[half : half + 1, :] = jnp.sum(own, axis=0, keepdims=True)[:, 0:4]
    ratio = norm[0:4] / norm[4:8]
    keep = min(EMA_CEILING, (1.0 + STEP) / (10.0 + STEP))
    for at, lanes in enumerate(MATRICES):
        new = ww_ref[:, lanes] - (RATE * ratio[at : at + 1]) * wu_ref[:, lanes]
        wn_ref[:, lanes] = new
        wa_ref[:, lanes] = keep * we_ref[:, lanes] + (1.0 - keep) * new
    new = dw_ref[...] - (RATE * ratio[3:4]) * du_ref[...]
    dn_ref[...] = new
    da_ref[...] = keep * de_ref[...] + (1.0 - keep) * new


def plain(kernel, name, out_shape, *operands, scratch=()):
    small = pltpu.CompilerParams(vmem_limit_bytes=8 * 1024 * 1024)
    return pl.pallas_call(
        kernel,
        out_shape=out_shape,
        scratch_shapes=scratch,
        compiler_params=small,
        name=name,
    )(*operands)


def to_other(values):
    return lax.ppermute(values, "dp", [(0, 1), (1, 0)])


def copies(values, count):
    return jnp.broadcast_to(values[None], (count,) + values.shape)


def send_terms(values, count):
    return lax.all_to_all(values.reshape(count, -1, values.shape[-1]), "fsdp", 0, 0)


def add_terms(terms):
    return jnp.sum(terms.astype(F32), axis=0)


def on_device(
    count,
    tokens_in,
    cotangent,
    crop_count,
    wide_w,
    wide_m,
    wide_v,
    wide_ema,
    down_w,
    down_m,
    down_v,
    down_ema,
    small_p,
    small_m,
    small_v,
    small_ema,
):
    rows = wide_w.shape[0]
    narrow = small_p.shape[0] // rows
    small_low = jnp.pad(small_p.astype(BF).reshape(rows, narrow), ((0, 0), (0, HALF - narrow)))
    first = jnp.concatenate([wide_w[:, : 3 * D].astype(BF), small_low], axis=1)
    core = lax.axis_index("dp")
    half = lax.dynamic_slice_in_dim(first, core * (rows // 2), rows // 2, axis=0)
    half = send_terms(copies(half, count), count)
    hat, late_all = run_norm(tokens_in, wide_w, down_w, count)
    half, late_all, hat = lax.optimization_barrier((half, late_all, hat))
    late_all = send_terms(late_all, count).reshape(D, -1)
    other = to_other(half)
    first = [jnp.where(core == at, half, other) for at in range(2)]
    first = jnp.stack(first, axis=1).reshape(D, -1)
    table = first[:, 3 * D : 3 * D + narrow].astype(F32).reshape(-1, D)
    side = np.stack([tap_matrix(kind) for kind in range(3)])
    side = bf(side.transpose(0, 2, 1, 3).reshape(3, QROWS, 9 * QROWS))
    hat, att, win, e, il, o = run_attend(hat, first, table, side)
    block_out, dx, datt, g_late, sums, b_up = run_feed(
        rows, crop_count, tokens_in, cotangent, att, late_all, table
    )
    late = send_terms(g_late, count)
    spans = small_spans(rows, narrow)
    dqkv, g_last = run_back(
        spans, [datt, win, e, il, o, hat], first, table, sums, b_up, side
    )
    late, g_last = lax.optimization_barrier((late, g_last))
    late = add_terms(late)
    last = send_terms(g_last, count)
    late_other = to_other(late)
    late_other, dqkv = lax.optimization_barrier((late_other, dqkv))
    images = dqkv.shape[0]
    begin = images * 5 // 8
    grad_in = run_input(tokens_in, dqkv, dx, first, table, 0, begin)
    last, grad_in = lax.optimization_barrier((last, grad_in))
    last = add_terms(last)
    last_other = to_other(last)
    wide_like, down_like = sds(wide_w.shape, F32), sds(down_w.shape, F32)
    wide_first, wide_second, wide_upd, down_first, down_second, down_upd, squares = plain(
        moment_kernel,
        "moment",
        [wide_like] * 3 + [down_like] * 3 + [sds((count, 8, HALF), F32)],
        *(last, last_other, late, late_other),
        *(wide_w, wide_m, wide_v, down_w, down_m, down_v),
        scratch=[pltpu.VMEM((8, HALF), F32)],
    )
    squares, grad_in = lax.optimization_barrier((squares, grad_in))
    squares = send_terms(squares, count)
    grad_in = run_input(tokens_in, dqkv, dx, first, table, begin, images, grad_in)
    squares, grad_in = lax.optimization_barrier((squares, grad_in))
    wide_new, wide_avg, down_new, down_avg, norms = plain(
        update_kernel,
        "update",
        [wide_like] * 2 + [down_like] * 2 + [sds((2, 4), F32)],
        *(squares, wide_w, wide_upd, wide_ema, down_w, down_upd, down_ema),
    )
    shard_small = (last + last_other)[: spans[0][1], 3 * D :].reshape(-1)
    offset = lax.axis_index("fsdp") * (rows * narrow) % HALF
    shard_small = lax.dynamic_slice(shard_small, (offset,), (rows * narrow,))
    small_first, small_second, small_dir = moments(shard_small, small_m, small_v)
    small_new = small_p - RATE * small_dir
    ema_keep = min(EMA_CEILING, (1.0 + STEP) / (10.0 + STEP))
    small_avg = ema_keep * small_ema + (1.0 - ema_keep) * small_new
    return (
        block_out,
        grad_in,
        wide_new,
        wide_first,
        wide_second,
        wide_avg,
        down_new,
        down_first,
        down_second,
        down_avg,
        small_new,
        small_first,
        small_second,
        small_avg,
        norms,
    )


def solution(mesh):
    tok, row, vec = P(("dp", "fsdp"), None), P("fsdp", None), P("fsdp")
    in_specs = (tok, tok, P(("dp", "fsdp"))) + (row,) * 8 + (vec,) * 4
    out_specs = (tok, tok) + (row,) * 8 + (vec,) * 4 + (P(),)
    return jax.shard_map(
        functools.partial(on_device, mesh.shape["fsdp"]),
        mesh=mesh,
        in_specs=in_specs,
        out_specs=out_specs,
        check_vma=False,
    )
```

```python
import functools

import jax
import jax.numpy as jnp
import numpy as np
from jax import lax
from jax.experimental import pallas as pl
from jax.experimental.pallas import tpu as pltpu
from jax.sharding import PartitionSpec as P

D = 256
FF = 1024
HEAD = 32
STRIPE = 7
GRID_L = 14
GRID_S = 6
SMALL = 8
STEP = 10
TOK_IMG = 680

EPSILON = 1e-05
BETA_ONE = 0.9
BETA_TWO = 0.999
ADAM_EPS = 1e-06
DECAY = 0.05
RATE = 0.25
EMA_CEILING = 0.9999

ROWS = 688
BIG = 2 * GRID_L * GRID_L
PAIRS = 7
WIN = 128
QROWS = 112
HALF = 128
HEADS = 4
SCALE = HEAD**-0.5
LOG2E = 1.4426950408889634
CHUNKS = ((0, 240), (240, 464), (464, 688))
LONG = 744
EDGE = 16
COPIES = (3, 3, 2)
TAPS = tuple((dy, dx) for dy in (-1, 0, 1) for dx in (-1, 0, 1))
ORDER = (0, 2, 1, 3, 4, 5, 6)
VMEM = 60 * 1024 * 1024

BF = jnp.bfloat16
F32 = jnp.float32


def kind_of(pair):
    return 0 if pair < 2 else 1 if pair < 4 else 2


def branch_of(pair, member):
    return 0 if pair < 2 else 1 if pair < 4 else member


def first_of(pair, member):
    if pair < 2:
        return pair * GRID_L * GRID_L + member * STRIPE * GRID_L
    if pair < 4:
        return (pair - 2) * GRID_L * GRID_L + member * STRIPE
    return BIG + (pair - 4) * COPIES[0] * GRID_S * GRID_S


def tokens_of(pair):
    return STRIPE * GRID_L if pair < 4 else COPIES[pair - 4] * GRID_S * GRID_S


def shape_of(kind):
    return ((STRIPE, GRID_L), (GRID_L, STRIPE), (GRID_S, GRID_S))[kind]


def edge_masks():
    masks, places = [], {}
    for kind in range(3):
        high, broad = shape_of(kind)
        size = high * broad
        for dy, dx in TAPS:
            if (dy, dx) == (0, 0) or (kind < 2 and (dy != 0 or dx == 0)):
                continue
            mask = np.zeros((QROWS, HALF), np.float32)
            for at in range(size * (1 if kind < 2 else COPIES[0])):
                r, c = divmod(at % size, broad)
                mask[at] = 0 <= r + dy < high and 0 <= c + dx < broad
            places[kind, dy, dx] = len(masks)
            masks.append(mask)
    return np.stack(masks), places


def tap_matrix(kind):
    shape = shape_of(kind)
    copies = 1 if kind < 2 else COPIES[0]
    size = shape[0] * shape[1]
    out = np.zeros((9, QROWS, QROWS), np.float32)
    for copy in range(copies):
        for r in range(shape[0]):
            for c in range(shape[1]):
                for tap in range(9):
                    rr, cc = r + tap // 3 - 1, c + tap % 3 - 1
                    if 0 <= rr < shape[0] and 0 <= cc < shape[1]:
                        out[tap, copy * size + r * shape[1] + c, copy * size + rr * shape[1] + cc] = 1
    return out


def mask_operands():
    size = GRID_S * GRID_S
    rows = np.zeros((3, 2, QROWS, HALF), np.float32)
    keys = np.zeros((3, HALF // 2, WIN), np.float32)
    for kind, crops in ((0, 1), (1, 3), (2, 2)):
        count = STRIPE * GRID_L if kind == 0 else crops * size
        each = count // crops
        for at in range(QROWS):
            rows[kind, 0, at, HALF // 2 + (at // each if at < count else 0)] = 1
        for at in range(WIN):
            for crop in range(crops):
                if at >= count or at // each != crop:
                    keys[kind, crop, at] = -1e30
    rows[:, 1, :, : HALF // 2] = rows[:, 0, :, HALF // 2 :]
    return rows, np.tile(keys, (1, 1, 2))


def bf(array):
    return jnp.asarray(array, BF)


def dot(left, right):
    return jnp.dot(left, right, preferred_element_type=F32)


def dot_nt(left, right):
    return lax.dot_general(left, right, (((1,), (1,)), ((), ())), preferred_element_type=F32)


def dot_tn(left, right):
    return lax.dot_general(left, right, (((0,), (0,)), ((), ())), preferred_element_type=F32)


def normalise(values):
    center = values - jnp.mean(values, axis=-1, keepdims=True)
    spread = jnp.mean(center * center, axis=-1, keepdims=True)
    scale = lax.rsqrt(spread + EPSILON)
    return center * scale, scale


def norm_back(grad_hat, hat, scale):
    mean_grad = jnp.mean(grad_hat, axis=-1, keepdims=True)
    mean_dot = jnp.mean(grad_hat * hat, axis=-1, keepdims=True)
    return scale * (grad_hat - mean_grad - hat * mean_dot)


def rows_of(ref, low, high):
    if high <= TOK_IMG:
        return ref[low:high, :]
    tail = jnp.zeros((high - TOK_IMG, ref.shape[1]), F32)
    return jnp.concatenate([ref[low:TOK_IMG, :], tail], axis=0)


def store_rows(ref, low, high, values):
    last = min(high, TOK_IMG)
    ref[low:last, :] = values[: last - low]


def with_ones(turned):
    return jnp.concatenate([turned, jnp.ones((16, turned.shape[1]), turned.dtype)], axis=0)


def fold(values):
    return jnp.sum(values.reshape(values.shape[0] // 8, 8, values.shape[1]), axis=0)


def head_lanes(head):
    lanes = lax.broadcasted_iota(jnp.int32, (1, HALF), 1)
    return jnp.where(lanes // HEAD == head, 1.0, 0.0).astype(BF)


def by_head(values):
    return jnp.concatenate([values * head_lanes(h) for h in range(HEADS)], axis=0)


def two_heads(turned, pair):
    low = pair * 2 * HEAD
    none = jnp.zeros((HEAD, WIN), turned.dtype)
    first = jnp.concatenate([turned[low : low + HEAD], none], axis=1)
    second = jnp.concatenate([none, turned[low + HEAD : low + 2 * HEAD]], axis=1)
    return jnp.concatenate([first, second], axis=0)


def by_two_heads(left, other, turned, added, rest=None):
    none = jnp.zeros_like(added)
    first = [two_heads(turned, 0), added, none, added]
    second = [added, two_heads(turned, 1), added, none]
    upper = lax.broadcasted_iota(jnp.int32, left.shape, 1) >= HALF // 2
    lefts = [jnp.where(upper, other[0], left), jnp.where(upper, left, other[1])]
    if rest is None:
        first, second = first[:2], second[:2]
    else:
        lefts = [jnp.concatenate([part, rest], axis=1) for part in lefts]
    first = dot(lefts[0], jnp.concatenate(first, axis=0))
    second = dot(lefts[1], jnp.concatenate(second, axis=0))
    return [first[:, :WIN], first[:, WIN:], second[:, :WIN], second[:, WIN:]]


def taps_of(table, branch):
    return table[5:14, branch * HALF : (branch + 1) * HALF]


def first_rows(values, count):
    low = count // 16 * 16
    if low >= values.shape[0]:
        return values
    row = lax.broadcasted_iota(jnp.int32, (values.shape[0] - low, 1), 0)
    tail = jnp.where(row < count - low, values[low:], 0.0)
    return jnp.concatenate([values[:low], tail], axis=0)


def pieces_of(pair, member):
    low = first_of(pair, member)
    return [(low + r * GRID_L, r * STRIPE) for r in range(GRID_L)]


def pipelined(stages, order, extra=()):
    extra = dict(extra)
    state = {item: {} for item in order}
    for turn in range(len(order) + max(lag for lag, _ in stages)):
        if turn in extra:
            extra[turn]()
        running = []
        for lag, stage in stages:
            if 0 <= turn - lag < len(order):
                item = order[turn - lag]
                running.append(stage(item, state[item]))
        while running:
            running = [stage for stage in running if next(stage, True) is None]


def norm_kernel(x_ref, wide_ref, down_ref, hat_ref, late_ref):
    for low in range(0, x_ref.shape[0], TOK_IMG // 5):
        hat_ref[low : low + TOK_IMG // 5, :] = normalise(x_ref[low : low + TOK_IMG // 5, :])[0]

    @pl.when(pl.program_id(0) == 0)
    def _():
        rows = wide_ref.shape[0]
        pieces = [wide_ref[:, 3 * D :]]
        pieces += [down_ref[at : at + rows, :] for at in range(0, down_ref.shape[0], rows)]
        late = jnp.concatenate(pieces, axis=1).astype(BF)
        for owner in range(late_ref.shape[0]):
            late_ref[owner] = late


def attend_kernel(
    x_ref,
    w_ref,
    s_ref,
    tap_ref,
    mrow_ref,
    mkey_ref,
    hat_ref,
    att_ref,
    win_ref,
    e_ref,
    il_ref,
    o_ref,
    qkv_scr,
    turn_scr,
    back_scr,
    att_scr,
):
    @pl.when(pl.program_id(0) == 0)
    def _():
        for branch in range(2):
            qkv_scr[branch, ROWS:, :] = jnp.zeros((LONG - ROWS, 3 * HALF), F32)
        turn_scr[...] = jnp.zeros_like(turn_scr)
        att_scr[TOK_IMG:, :] = jnp.zeros((ROWS - TOK_IMG, D), F32)

    gain, shift = s_ref[0:1, :], s_ref[1:2, :]
    ones = jnp.concatenate(
        [jnp.broadcast_to(head_lanes(h), (WIN, HALF)) for h in range(HEADS)], axis=0
    )

    def project(chunk):
        low, high = CHUNKS[chunk]
        hat = rows_of(x_ref, low, high)
        hat_ref[0, low:high, :] = hat.astype(BF)
        a = (hat * gain + shift).astype(BF)
        for part in range(3):
            lanes = slice(part * D, (part + 1) * D)
            piece = dot(a, w_ref[:, lanes]) + s_ref[2 + part : 3 + part, :]
            for branch in range(2):
                qkv_scr[branch, low:high, part * HALF : (part + 1) * HALF] = piece[
                    :, branch * HALF : (branch + 1) * HALF
                ]

    none = jnp.zeros((WIN - QROWS, HALF), BF)

    def cut(pair, state):
        for member in range(2):
            at = 2 * pair + member
            if kind_of(pair) == 1:
                for source, target in pieces_of(pair, member):
                    turn_scr[at - 4, target : target + STRIPE, :] = qkv_scr[
                        1, source : source + STRIPE, :
                    ]
                window = turn_scr[at - 4, :QROWS, :]
            else:
                low = first_of(pair, member)
                window = qkv_scr[branch_of(pair, member), low : low + QROWS, :]
            window = window.astype(BF)
            win_ref[0, at] = window
            state[member] = [window[:, part * HALF : (part + 1) * HALF] for part in range(3)]
            yield

    def score(pair, state):
        mask = 0 if pair < 4 else 1 if pair < 6 else 2
        for member in range(2):
            q, k, v = state[member]
            k = jnp.concatenate([k, none], axis=0).T
            rows = mrow_ref[mask, 0], mrow_ref[mask, 1]
            state[member] = v, by_two_heads(q, rows, k, mkey_ref[mask])
            yield

    def soften(pair, state):
        for member in range(2):
            v, scores = state[member]
            exps = []
            for part in scores:
                peak = jnp.max(part, axis=-1, keepdims=True)
                exps.append(jnp.exp2((part - peak) * (SCALE * LOG2E)).astype(BF))
            e = jnp.concatenate(exps, axis=1)
            e_ref[0, 2 * pair + member] = e
            state[member] = v, e
            yield

    def mix(pair, state):
        taps = []
        for member in range(2):
            v, e = state[member]
            low = taps_of(s_ref, branch_of(pair, member)).astype(BF)
            keys = jnp.concatenate([v, none], axis=0)
            state[member] = dot(e, jnp.concatenate([by_head(keys), ones], axis=1))
            taps.append(jnp.concatenate([v * low[tap : tap + 1] for tap in range(9)], axis=0))
            yield
        state[2] = dot(tap_ref[kind_of(pair)], jnp.concatenate(taps, axis=1))
        yield

    def put(pair, state):
        for member in range(2):
            at = 2 * pair + member
            branch = branch_of(pair, member)
            lanes = slice(branch * HALF, (branch + 1) * HALF)
            both = state[member]
            inv = 1.0 / both[:, HALF:]
            o = both[:, :HALF] * inv
            il_ref[0, at] = inv
            o_ref[0, at] = o
            conv = state[2][:, member * HALF : (member + 1) * HALF]
            piece = o + s_ref[14:15, lanes] + conv
            if kind_of(pair) == 1:
                back_scr[at - 4] = piece
                for source, target in pieces_of(pair, member):
                    att_scr[source : source + STRIPE, lanes] = back_scr[
                        at - 4, target : target + STRIPE, :
                    ]
            else:
                low, count = first_of(pair, member), tokens_of(pair)
                att_scr[low : low + count, lanes] = piece[:count]
            yield

    project(0)
    extra = {1: functools.partial(project, 1), 3: functools.partial(project, 2)}
    stages = enumerate((cut, score, soften, mix, put))
    pipelined(tuple(stages), ORDER, extra)
    att_ref[0] = att_scr[...].astype(BF)


def gelu_parts(u):
    above = lax.erf(u * 2**-0.5) + 1.0
    decay = jnp.exp2((u * u) * (-0.5 * LOG2E))
    return u * above, above + (u * decay) * (2 / np.pi) ** 0.5


def beside(*streams):
    left = [[list(stream), 0] for stream in streams]
    total = max((len(steps) for steps, _ in left), default=0)
    for at in range(total):
        for entry in left:
            steps, done = entry
            goal = -(-len(steps) * (at + 1) // total)
            for step in steps[done:goal]:
                step()
            entry[1] = goal


def weight_terms(grad, weight, bias):
    terms = []
    for value in (weight * bias,) if grad is None else (weight * grad, weight * bias):
        column = jnp.sum(value, axis=1, keepdims=True)
        terms.append(jnp.broadcast_to(column, (D, HALF)).T[0:1, :])
    return terms


def down_blocks(shard):
    parts = FF // D
    return [(i, part, (i * parts + part) * shard) for i in range(D // shard) for part in range(parts)]


def feed_kernel(
    shard,
    cnt_ref,
    x_ref,
    c_ref,
    att_ref,
    w_ref,
    s_ref,
    out_ref,
    dx_ref,
    datt_ref,
    pack_ref,
    sums_ref,
    bup_ref,
    rs_scr,
    x1_scr,
    gup_scr,
    gdn_scr,
    gout_scr,
    turn_scr,
    pack_scr,
    down_scr,
):
    image = pl.program_id(0)

    @pl.when(image == 0)
    def _():
        for ref in (gup_scr, gdn_scr, gout_scr, sums_ref, bup_ref):
            ref[...] = jnp.zeros_like(ref)
        pack_scr[...] = w_ref[:, D + FF :].astype(F32)
        for owner, part, low in down_blocks(shard):
            turn_scr[low : low + shard, :] = pack_scr[
                owner * shard : (owner + 1) * shard, part * D : (part + 1) * D
            ]
        down_scr[...] = turn_scr[...].astype(BF)

    bound = BIG + GRID_S * GRID_S * cnt_ref[image]
    bias_out, gain, shift = s_ref[15:16, :], s_ref[16:17, :], s_ref[17:18, :]
    lanes_of = [slice(part * D, (part + 1) * D) for part in range(FF // D)]
    count = 16
    rows = range(0, ROWS, count)
    biases = [s_ref[18 + part : 19 + part, :] for part in range(FF // D)]
    sums = {}
    held = {}

    def add_sum(key, values, at, ref, *index):
        sums[key] = sums[key] + fold(values) if key in sums else fold(values)
        if at + count >= ROWS:
            ref[index] += sums[key]

    def keep(key, at, values):
        held.setdefault(key, []).append(values)
        if at + count >= ROWS:
            held[key] = jnp.concatenate(held[key], axis=0)

    def masked(at):
        row = at + lax.broadcasted_iota(jnp.int32, (count, 1), 0)
        return jnp.where(row < bound, rows_of(c_ref, at, at + count), 0.0)

    def cot(at):
        dy = masked(at)
        keep("dy", at, dy.astype(BF))
        add_sum("dy", dy, at, sums_ref, 0)

    def project():
        held["x1"] = dot(att_ref[0], w_ref[:, :D])

    def norm(at):
        own = slice(at, at + count)
        x1 = rows_of(x_ref, at, at + count) + held["x1"][own] + bias_out
        x1_scr[own, :] = x1
        hat, scale = normalise(x1)
        rs_scr[own, :] = scale
        keep("hat", at, hat.astype(BF))
        keep("h2", at, (hat * gain + shift).astype(BF))

    def hidden(part):
        cols = slice(D + part * D, D + (part + 1) * D)
        held["v", part] = dot(held["h2"], w_ref[:, cols])

    def hidden_back(part):
        held["dg", part] = dot_nt(held["dy"], down_scr[lanes_of[part], :])

    def gelu(part, at):
        own = slice(at, at + count)
        v = held["v", part][own] + biases[part]
        g, slope = gelu_parts(v)
        keep(("g", part), at, g.astype(BF))
        du = held["dg", part][own] * slope
        keep(("du", part), at, du.astype(BF))

    def gelus(part):
        return [functools.partial(gelu, part, at) for at in rows]

    def grad_up(part):
        both = dot(held["hat_t"], held["du", part])
        gup_scr[:, lanes_of[part]] += both[:D]
        bup_ref[:, lanes_of[part]] += both[D : D + 8]

    def grad_down(part):
        gdn_scr[:, lanes_of[part]] += dot(held["dy_t"], held["g", part])

    def joined(key, *parts):
        return jnp.concatenate([held[key, part] for part in parts], axis=1)

    half = FF // 2

    def out_first():
        held["out"] = dot(joined("g", 0, 1), down_scr[:half, :])

    def out_last():
        held["out"] += dot(joined("g", 2, 3), down_scr[half:, :])

    def out_store(at):
        own = slice(at, at + count)
        out = x1_scr[own, :] + held["out"][own] * 0.5 + s_ref[22:23, :]
        store_rows(out_ref, at, at + count, out)

    def back_first():
        held["dh"] = dot_nt(joined("du", 0, 1), w_ref[:, D : D + half])

    def back_last():
        held["dh"] += dot_nt(joined("du", 2, 3), w_ref[:, D + half : D + FF])

    def norm_grad(at):
        own = slice(at, at + count)
        hat = held["hat"][own].astype(F32)
        dx = masked(at) + norm_back(held["dh"][own] * (gain * 0.5), hat, rs_scr[own, :])
        store_rows(dx_ref, at, at + count, dx)
        keep("dz", at, dx.astype(BF))
        add_sum("dz", dx, at, sums_ref, 1)

    def attention():
        datt = dot_nt(held["dz"], w_ref[:, :D])
        datt_ref[0] = datt.astype(BF)

    def grad_out():
        gout_scr[...] += dot_tn(att_ref[0], held["dz"])

    def each(step, *parts):
        return [functools.partial(step, part) for part in parts]

    def turn(key):
        held[key + "_t"] = held[key].T

    beside(each(cot, *rows), [project])
    turn("dy")
    beside(each(norm, *rows), each(hidden_back, 0, 1, 2, 3))
    turn("hat")
    held["hat_t"] = with_ones(held["hat_t"])
    hidden(0)
    beside(each(hidden, 1, 2, 3), gelus(0))
    beside(each(grad_up, 0) + each(grad_down, 0), gelus(1))
    beside([back_first] + each(grad_up, 1) + each(grad_down, 1), gelus(2))
    beside([out_first] + each(grad_up, 2) + each(grad_down, 2), gelus(3))
    back_last()
    beside([out_last] + each(grad_up, 3) + each(grad_down, 3), each(norm_grad, *rows))
    beside([attention, grad_out], each(out_store, *rows))

    @pl.when(image == pl.num_programs(0) - 1)
    def _():
        turn_scr[...] = gdn_scr[...].T * 0.5
        for owner, part, low in down_blocks(shard):
            pack_scr[owner * shard : (owner + 1) * shard, part * D : (part + 1) * D] = turn_scr[
                low : low + shard, :
            ]
        bup_ref[...] *= 0.5
        bias = bup_ref[0:1, :]
        grad = gup_scr[...] * 0.5
        terms = weight_terms(grad, w_ref[:, D : D + FF].astype(F32), bias)
        out_bias = jnp.sum(sums_ref[1], axis=0, keepdims=True)
        terms += weight_terms(None, w_ref[:, :D].astype(F32), out_bias)
        for at, term in enumerate(terms):
            sums_ref[2 + at, 0:1, :] = term
        columns = s_ref[15:23, :].T
        grad = columns[:, 1:2] * grad + columns[:, 2:3] * bias
        pack_ref[:, :D] = gout_scr[...].astype(BF)
        pack_ref[:, D : D + FF] = grad.astype(BF)
        pack_ref[:, D + FF :] = pack_scr[...].astype(BF)


def small_spans(shard, narrow):
    count = D // shard
    own = shard * narrow
    rows = max((own * (i + 1) - 1) // HALF - own * i // HALF + 1 for i in range(count))
    return [(own * i // HALF, rows) for i in range(count)]


def back_kernel(
    spans,
    places,
    datt_ref,
    win_ref,
    e_ref,
    il_ref,
    o_ref,
    hat_ref,
    w_ref,
    s_ref,
    feed_ref,
    bup_ref,
    tap_ref,
    edge_ref,
    dqkv_ref,
    pack_ref,
    g_scr,
    kern_scr,
    bias_scr,
    datt_scr,
    grad_scr,
    turn_scr,
    pad_scr,
    back_scr,
    dqkv_scr,
    small_scr,
    pack_scr,
):
    image = pl.program_id(0)

    @pl.when(image == 0)
    def _():
        for ref in (g_scr, kern_scr, bias_scr, turn_scr, pad_scr, small_scr, pack_scr):
            ref[...] = jnp.zeros_like(ref)
        datt_scr[ROWS:, :] = jnp.zeros((LONG - ROWS, D), F32)
        dqkv_scr[TOK_IMG:, :] = jnp.zeros((ROWS - TOK_IMG, 3 * D), F32)

    for low, high in CHUNKS:
        datt_scr[low:high, :] = datt_ref[0, low:high, :].astype(F32)
    minus = two_heads(jnp.full((HALF, WIN), -1.0, BF), 0)
    none = jnp.zeros((WIN - QROWS, HALF), BF)

    def weigh(pair, state):
        for member in range(2):
            at = 2 * pair + member
            branch = branch_of(pair, member)
            lanes = slice(branch * HALF, (branch + 1) * HALF)
            if kind_of(pair) == 1:
                for source, target in pieces_of(pair, member):
                    turn_scr[at - 4, target : target + STRIPE, :] = datt_scr[
                        source : source + STRIPE, lanes
                    ]
                grad = turn_scr[at - 4]
            else:
                low = first_of(pair, member)
                grad = first_rows(datt_scr[low : low + QROWS, lanes], tokens_of(pair))
            grad_scr[at * QROWS : (at + 1) * QROWS, :] = grad
            v = win_ref[0, at, :, 2 * HALF :]
            pad_scr[at, EDGE : EDGE + QROWS, :] = first_rows(v.astype(F32), tokens_of(pair))
            dn = (grad * il_ref[0, at]).astype(BF)
            z = pltpu.roll(dn.astype(F32) * o_ref[0, at], HALF // 2, 1)
            high = z.astype(BF)
            rows = high, high
            rest = (z - high.astype(F32)).astype(BF)
            v = jnp.concatenate([v, none], axis=0).T
            state[member] = grad, dn, by_two_heads(dn, rows, v, minus, rest)
            yield

    def score(pair, state):
        for member in range(2):
            grad, dn, weighed = state[member]
            e = e_ref[0, 2 * pair + member]
            ds = jnp.concatenate(weighed, axis=1).astype(BF) * e
            state[member] = grad, dn, ds, e
            yield

    def spread(pair, state):
        kind = kind_of(pair)
        taps = []
        for member in range(2):
            grad, dn, ds, e = state[member]
            at = 2 * pair + member
            kernel = taps_of(s_ref, branch_of(pair, member)).astype(BF)
            q = win_ref[0, at, :, 0:HALF]
            k = jnp.concatenate([win_ref[0, at, :, HALF : 2 * HALF], none], axis=0)
            dq = dot(ds, by_head(k))
            row = 2 * PAIRS * QROWS + 8 * at
            grad_scr[row : row + 8, :] = dq[:8]
            q_t, dn_t = q.T, dn.T
            dk, dv = [], []
            for half in range(2):
                lanes = slice(2 * half * WIN, 2 * (half + 1) * WIN)
                own = slice(2 * half * HEAD, 2 * (half + 1) * HEAD)
                for parts, left, right in ((dk, q_t, ds), (dv, dn_t, e)):
                    both = dot(left[own], right[:, lanes])
                    parts += [both[:HEAD, :WIN], both[HEAD:, WIN:]]
            state[member] = dq, dk, dv
            low = grad.astype(BF)
            taps.append(
                jnp.concatenate([low * kernel[8 - tap : 9 - tap] for tap in range(9)], axis=0)
            )
            yield
        state[2] = dot(tap_ref[kind], jnp.concatenate(taps, axis=1))
        yield

    def kernels(pair, state):
        kind = kind_of(pair)
        broad = shape_of(kind)[1]
        for member in range(2):
            at = 2 * pair + member
            base = pl.multiple_of(at * QROWS + image // 4096 * 8, 8)
            totals = [jnp.zeros((8, HALF), F32)] * 9
            for low in range(0, tokens_of(pair), 8):
                own = slice(low, low + 8)
                grad = grad_scr[pl.ds(pl.multiple_of(base + low, 8), 8), :]
                sides = {}
                for tap, (dy, dx) in enumerate(TAPS):
                    place = places.get((kind, 0 if kind < 2 else dy, dx))
                    if place not in sides:
                        mask = 1.0 if place is None else edge_ref[place, own, :]
                        sides[place] = grad * mask
                    start = EDGE + low + dy * broad + dx
                    totals[tap] = totals[tap] + sides[place] * pad_scr[at, start : start + 8, :]
            for tap in range(9):
                kern_scr[branch_of(pair, member), tap] += totals[tap]
            yield

    def put(pair, state):
        for member in range(2):
            at = 2 * pair + member
            branch = branch_of(pair, member)
            dq, dk, dv = state[member]
            dk = jnp.concatenate(dk, axis=0).T[:QROWS] * SCALE
            dv = jnp.concatenate(dv, axis=0).T[:QROWS]
            dv = dv + state[2][:, member * HALF : (member + 1) * HALF]
            for part, piece in enumerate((dq * SCALE, dk, dv)):
                lanes = slice(part * D + branch * HALF, part * D + (branch + 1) * HALF)
                if kind_of(pair) == 1:
                    back_scr[at - 4, part] = piece
                    for source, target in pieces_of(pair, member):
                        dqkv_scr[source : source + STRIPE, lanes] = back_scr[
                            at - 4, part, target : target + STRIPE, :
                        ]
                else:
                    low, count = first_of(pair, member), tokens_of(pair)
                    dqkv_scr[low : low + count, lanes] = piece[:count]
            yield

    pipelined(((3, kernels), (0, weigh), (1, score), (2, spread), (3, put)), ORDER)
    dqkv = dqkv_scr[...].astype(BF)
    dqkv_ref[0] = dqkv
    both = dot(with_ones(hat_ref[0].T), dqkv)
    g_scr[...] += both[:D]
    bias_scr[...] += both[D : D + 8]

    @pl.when(image == pl.num_programs(0) - 1)
    def _():
        def put(row, terms):
            for at in range(0, terms.shape[1], HALF):
                small_scr[row : row + 1, :] = terms[:, at : at + HALF]
                row += 1

        total = lambda terms: jnp.sum(terms, axis=0, keepdims=True)
        bias = bias_scr[0:1, :]
        gain, shift = weight_terms(g_scr[...], w_ref[:, : 3 * D].astype(F32), bias)
        put(0, gain)
        put(2, shift)
        put(4, bias)
        for tap in range(9):
            for branch in range(2):
                put(10 + 2 * tap + branch, total(kern_scr[branch, tap]))
        for row, entry in ((30, 1), (44, 0)):
            put(row, total(feed_ref[entry]))
        for row, entry in ((32, 2), (34, 3), (28, 4)):
            put(row, feed_ref[entry, 0:1, :])
        put(36, bup_ref[0:1, :])
        for owner, (row, rows) in enumerate(spans):
            shard = D // len(spans)
            pack_scr[owner * shard : owner * shard + rows, :] = small_scr[row : row + rows, :]
        columns = s_ref[0:8, :].T
        grad = columns[:, 0:1] * g_scr[...] + columns[:, 1:2] * bias
        pack_ref[:, : 3 * D] = grad.astype(BF)
        pack_ref[:, 3 * D :] = pack_scr[...].astype(BF)


def input_kernel(x_ref, dqkv_ref, dx_ref, w_ref, s_ref, *out_refs):
    out_ref = out_refs[-1]
    for low, high in CHUNKS:
        dh = dot_nt(dqkv_ref[0, low:high, :], w_ref[:, : 3 * D])
        hat, scale = normalise(rows_of(x_ref, low, high))
        grad = rows_of(dx_ref, low, high) + norm_back(dh * s_ref[0:1, :], hat, scale)
        store_rows(out_ref, low, high, grad)


def whole(shape):
    return pl.BlockSpec(shape, lambda i, *_: (0,) * len(shape))


def image_of(shape):
    return pl.BlockSpec((1,) + shape, lambda i, *_: (i,) + (0,) * len(shape))


def tokens():
    return pl.BlockSpec((TOK_IMG, D), lambda i, *_: (i, 0))


def params(room=0):
    return pltpu.CompilerParams(
        vmem_limit_bytes=VMEM - room * 1024 * 1024, dimension_semantics=("arbitrary",)
    )


def sds(shape, dtype):
    return jax.ShapeDtypeStruct(shape, dtype)


def run_norm(tokens_in, wide, down, count):
    rows = TOK_IMG * 2
    block = pl.BlockSpec((rows, D), lambda i: (i, 0))
    late = (count, wide.shape[0], D + 2 * FF)
    return pl.pallas_call(
        norm_kernel,
        grid=(tokens_in.shape[0] // rows,),
        in_specs=[block, whole(wide.shape), whole(down.shape)],
        out_specs=[block, whole(late)],
        out_shape=[sds(tokens_in.shape, F32), sds(late, BF)],
        compiler_params=params(),
        name="norm",
    )(tokens_in, wide, down)


def run_attend(tokens_in, w_qkv, table, side):
    images = tokens_in.shape[0] // TOK_IMG
    mrow, mkey = mask_operands()
    consts = [table, side, bf(mrow), bf(mkey)]
    outs = [
        ((ROWS, D), BF),
        ((ROWS, D), BF),
        ((2 * PAIRS, QROWS, 3 * HALF), BF),
        ((2 * PAIRS, QROWS, HEADS * WIN), BF),
        ((2 * PAIRS, QROWS, HALF), F32),
        ((2 * PAIRS, QROWS, HALF), F32),
    ]
    return pl.pallas_call(
        attend_kernel,
        grid=(images,),
        in_specs=[tokens(), whole(w_qkv.shape)] + [whole(c.shape) for c in consts],
        out_specs=[image_of(shape) for shape, _ in outs],
        out_shape=[sds((images,) + shape, dtype) for shape, dtype in outs],
        scratch_shapes=[
            pltpu.VMEM((2, LONG, 3 * HALF), F32),
            pltpu.VMEM((4, QROWS, 3 * HALF), F32),
            pltpu.VMEM((4, QROWS, HALF), F32),
            pltpu.VMEM((ROWS, D), F32),
        ],
        compiler_params=params(-3),
        name="attend",
    )(tokens_in, w_qkv, *consts)


def run_feed(shard, counts, tokens_in, cotangent, att, wide, table):
    images = tokens_in.shape[0] // TOK_IMG
    return pl.pallas_call(
        functools.partial(feed_kernel, shard),
        grid_spec=pltpu.PrefetchScalarGridSpec(
            num_scalar_prefetch=1,
            grid=(images,),
            in_specs=[
                tokens(),
                tokens(),
                image_of((ROWS, D)),
                whole(wide.shape),
                whole(table.shape),
            ],
            out_specs=[
                tokens(),
                tokens(),
                image_of((ROWS, D)),
                whole((D, D + 2 * FF)),
                whole((5, 8, D)),
                whole((8, FF)),
            ],
            scratch_shapes=[
                pltpu.VMEM((ROWS, 1), F32),
                pltpu.VMEM((ROWS, D), F32),
                pltpu.VMEM((D, FF), F32),
                pltpu.VMEM((D, FF), F32),
                pltpu.VMEM((D, D), F32),
                pltpu.VMEM((FF, D), F32),
                pltpu.VMEM((D, FF), F32),
                pltpu.VMEM((FF, D), BF),
            ],
        ),
        out_shape=[
            sds(tokens_in.shape, F32),
            sds(tokens_in.shape, F32),
            sds((images, ROWS, D), BF),
            sds((D, D + 2 * FF), BF),
            sds((5, 8, D), F32),
            sds((8, FF), F32),
        ],
        compiler_params=params(),
        name="feed",
    )(counts, tokens_in, cotangent, att, wide, table)


def run_back(spans, blocks, w_qkv, table, sums, b_up, side):
    images = blocks[0].shape[0]
    masks, places = edge_masks()
    consts = [w_qkv, table, sums, b_up, side, jnp.asarray(masks)]
    return pl.pallas_call(
        functools.partial(back_kernel, spans, places),
        grid=(images,),
        in_specs=[image_of(b.shape[1:]) for b in blocks] + [whole(c.shape) for c in consts],
        out_specs=[image_of((ROWS, 3 * D)), whole((D, 3 * D + HALF))],
        out_shape=[sds((images, ROWS, 3 * D), BF), sds((D, 3 * D + HALF), BF)],
        scratch_shapes=[
            pltpu.VMEM((D, 3 * D), F32),
            pltpu.VMEM((2, 9, 8, HALF), F32),
            pltpu.VMEM((8, 3 * D), F32),
            pltpu.VMEM((LONG, D), F32),
            pltpu.VMEM((2 * PAIRS * (QROWS + 8), HALF), F32),
            pltpu.VMEM((4, QROWS, HALF), F32),
            pltpu.VMEM((2 * PAIRS, QROWS + 2 * EDGE, HALF), F32),
            pltpu.VMEM((4, 3, QROWS, HALF), F32),
            pltpu.VMEM((ROWS, 3 * D), F32),
            pltpu.VMEM((56, HALF), F32),
            pltpu.VMEM((D, HALF), F32),
        ],
        compiler_params=params(),
        name="back",
    )(*blocks, *consts)


def run_input(tokens_in, dqkv, dx, w_qkv, table, low, high, out=None):
    own = pl.BlockSpec((TOK_IMG, D), lambda i: (low + i, 0))
    rows = pl.BlockSpec((1, ROWS, 3 * D), lambda i: (low + i, 0, 0))
    ends = [] if out is None else [out]
    return pl.pallas_call(
        input_kernel,
        grid=(high - low,),
        in_specs=[own, rows, own, whole(w_qkv.shape), whole(table.shape)]
        + [pl.BlockSpec(memory_space=pl.ANY) for _ in ends],
        out_specs=own,
        out_shape=sds(tokens_in.shape, F32),
        input_output_aliases={5: 0} if ends else {},
        compiler_params=params(),
        cost_estimate=pl.CostEstimate(
            flops=(high - low) * 2 * ROWS * 3 * D * D,
            bytes_accessed=(high - low) * ROWS * D * 18,
            transcendentals=0,
        ),
        name="input_grad",
    )(tokens_in, dqkv, dx, w_qkv, table, *ends)


def moments(grad, first, second):
    first_new = BETA_ONE * first + (1.0 - BETA_ONE) * grad
    second_new = BETA_TWO * second + (1.0 - BETA_TWO) * grad * grad
    direction = (
        first_new
        / (1.0 - BETA_ONE**STEP)
        / (jnp.sqrt(second_new / (1.0 - BETA_TWO**STEP)) + ADAM_EPS)
    )
    return (first_new, second_new, direction)


MATRICES = (slice(0, 3 * D), slice(3 * D, 4 * D), slice(4 * D, 4 * D + FF))


def lane_sums(values):
    column = jnp.sum(values * values, axis=0, keepdims=True)
    parts = [column[:, at : at + HALF] for at in range(0, column.shape[1], HALF)]
    return functools.reduce(jnp.add, parts)


def moment_kernel(
    gq_ref,
    gq_other_ref,
    gl_ref,
    gl_other_ref,
    ww_ref,
    wm_ref,
    wv_ref,
    dw_ref,
    dm_ref,
    dv_ref,
    wf_ref,
    ws_ref,
    wu_ref,
    df_ref,
    ds_ref,
    du_ref,
    copies_ref,
    sq_ref,
):
    for lanes, own, other in (
        (slice(0, 3 * D), gq_ref[:, : 3 * D], gq_other_ref[:, : 3 * D]),
        (slice(3 * D, 4 * D + FF), gl_ref[:, : D + FF], gl_other_ref[:, : D + FF]),
    ):
        first, second, way = moments(own + other, wm_ref[:, lanes], wv_ref[:, lanes])
        wf_ref[:, lanes] = first
        ws_ref[:, lanes] = second
        wu_ref[:, lanes] = way + DECAY * ww_ref[:, lanes]
    count = ww_ref.shape[0]
    for part in range(FF // D):
        lanes = slice(D + FF + part * D, D + FF + (part + 1) * D)
        own = slice(part * count, (part + 1) * count)
        grad = gl_ref[:, lanes] + gl_other_ref[:, lanes]
        first, second, way = moments(grad, dm_ref[own, :], dv_ref[own, :])
        df_ref[own, :] = first
        ds_ref[own, :] = second
        du_ref[own, :] = way + DECAY * dw_ref[own, :]
    for base, wide, down in ((0, ww_ref, dw_ref), (4, wu_ref, du_ref)):
        for at, lanes in enumerate(MATRICES):
            sq_ref[base + at : base + at + 1, :] = lane_sums(wide[:, lanes])
        sq_ref[base + 3 : base + 4, :] = lane_sums(down[...])
    copies_ref[...] = jnp.broadcast_to(sq_ref[...][None], copies_ref.shape)


def update_kernel(
    sq_ref,
    ww_ref,
    wu_ref,
    we_ref,
    dw_ref,
    du_ref,
    de_ref,
    wn_ref,
    wa_ref,
    dn_ref,
    da_ref,
    norm_ref,
):
    total = jnp.sum(jnp.sum(sq_ref[...], axis=0), axis=1, keepdims=True)
    norm = jnp.sqrt(total)
    row = lax.broadcasted_iota(jnp.int32, (8, HALF), 0)
    lane = lax.broadcasted_iota(jnp.int32, (8, HALF), 1)
    for half in range(2):
        own = jnp.where(row == lane + 4 * half, norm, 0.0)
        norm_ref[half : half + 1, :] = jnp.sum(own, axis=0, keepdims=True)[:, 0:4]
    ratio = norm[0:4] / norm[4:8]
    keep = min(EMA_CEILING, (1.0 + STEP) / (10.0 + STEP))
    for at, lanes in enumerate(MATRICES):
        new = ww_ref[:, lanes] - (RATE * ratio[at : at + 1]) * wu_ref[:, lanes]
        wn_ref[:, lanes] = new
        wa_ref[:, lanes] = keep * we_ref[:, lanes] + (1.0 - keep) * new
    new = dw_ref[...] - (RATE * ratio[3:4]) * du_ref[...]
    dn_ref[...] = new
    da_ref[...] = keep * de_ref[...] + (1.0 - keep) * new


def plain(kernel, name, out_shape, *operands, scratch=()):
    small = pltpu.CompilerParams(vmem_limit_bytes=8 * 1024 * 1024)
    return pl.pallas_call(
        kernel,
        out_shape=out_shape,
        scratch_shapes=scratch,
        compiler_params=small,
        name=name,
    )(*operands)


def to_other(values):
    return lax.ppermute(values, "dp", [(0, 1), (1, 0)])


def copies(values, count):
    return jnp.broadcast_to(values[None], (count,) + values.shape)


def send_terms(values, count):
    return lax.all_to_all(values.reshape(count, -1, values.shape[-1]), "fsdp", 0, 0)


def add_terms(terms):
    return jnp.sum(terms.astype(F32), axis=0)


def on_device(
    count,
    tokens_in,
    cotangent,
    crop_count,
    wide_w,
    wide_m,
    wide_v,
    wide_ema,
    down_w,
    down_m,
    down_v,
    down_ema,
    small_p,
    small_m,
    small_v,
    small_ema,
):
    rows = wide_w.shape[0]
    narrow = small_p.shape[0] // rows
    small_low = jnp.pad(small_p.astype(BF).reshape(rows, narrow), ((0, 0), (0, HALF - narrow)))
    first = jnp.concatenate([wide_w[:, : 3 * D].astype(BF), small_low], axis=1)
    core = lax.axis_index("dp")
    half = lax.dynamic_slice_in_dim(first, core * (rows // 2), rows // 2, axis=0)
    half = send_terms(copies(half, count), count)
    hat, late_all = run_norm(tokens_in, wide_w, down_w, count)
    half, late_all, hat = lax.optimization_barrier((half, late_all, hat))
    late_all = send_terms(late_all, count).reshape(D, -1)
    other = to_other(half)
    first = [jnp.where(core == at, half, other) for at in range(2)]
    first = jnp.stack(first, axis=1).reshape(D, -1)
    table = first[:, 3 * D : 3 * D + narrow].astype(F32).reshape(-1, D)
    side = np.stack([tap_matrix(kind) for kind in range(3)])
    side = bf(side.transpose(0, 2, 1, 3).reshape(3, QROWS, 9 * QROWS))
    hat, att, win, e, il, o = run_attend(hat, first, table, side)
    block_out, dx, datt, g_late, sums, b_up = run_feed(
        rows, crop_count, tokens_in, cotangent, att, late_all, table
    )
    late = send_terms(g_late, count)
    spans = small_spans(rows, narrow)
    dqkv, g_last = run_back(
        spans, [datt, win, e, il, o, hat], first, table, sums, b_up, side
    )
    late, g_last = lax.optimization_barrier((late, g_last))
    late = add_terms(late)
    last = send_terms(g_last, count)
    late_other = to_other(late)
    late_other, dqkv = lax.optimization_barrier((late_other, dqkv))
    images = dqkv.shape[0]
    begin = images * 5 // 8
    grad_in = run_input(tokens_in, dqkv, dx, first, table, 0, begin)
    last, grad_in = lax.optimization_barrier((last, grad_in))
    last = add_terms(last)
    last_other = to_other(last)
    wide_like, down_like = sds(wide_w.shape, F32), sds(down_w.shape, F32)
    wide_first, wide_second, wide_upd, down_first, down_second, down_upd, squares = plain(
        moment_kernel,
        "moment",
        [wide_like] * 3 + [down_like] * 3 + [sds((count, 8, HALF), F32)],
        *(last, last_other, late, late_other),
        *(wide_w, wide_m, wide_v, down_w, down_m, down_v),
        scratch=[pltpu.VMEM((8, HALF), F32)],
    )
    squares, grad_in = lax.optimization_barrier((squares, grad_in))
    squares = send_terms(squares, count)
    grad_in = run_input(tokens_in, dqkv, dx, first, table, begin, images, grad_in)
    squares, grad_in = lax.optimization_barrier((squares, grad_in))
    wide_new, wide_avg, down_new, down_avg, norms = plain(
        update_kernel,
        "update",
        [wide_like] * 2 + [down_like] * 2 + [sds((2, 4), F32)],
        *(squares, wide_w, wide_upd, wide_ema, down_w, down_upd, down_ema),
    )
    shard_small = (last + last_other)[: spans[0][1], 3 * D :].reshape(-1)
    offset = lax.axis_index("fsdp") * (rows * narrow) % HALF
    shard_small = lax.dynamic_slice(shard_small, (offset,), (rows * narrow,))
    small_first, small_second, small_dir = moments(shard_small, small_m, small_v)
    small_new = small_p - RATE * small_dir
    ema_keep = min(EMA_CEILING, (1.0 + STEP) / (10.0 + STEP))
    small_avg = ema_keep * small_ema + (1.0 - ema_keep) * small_new
    return (
        block_out,
        grad_in,
        wide_new,
        wide_first,
        wide_second,
        wide_avg,
        down_new,
        down_first,
        down_second,
        down_avg,
        small_new,
        small_first,
        small_second,
        small_avg,
        norms,
    )


def solution(mesh):
    tok, row, vec = P(("dp", "fsdp"), None), P("fsdp", None), P("fsdp")
    in_specs = (tok, tok, P(("dp", "fsdp"))) + (row,) * 8 + (vec,) * 4
    out_specs = (tok, tok) + (row,) * 8 + (vec,) * 4 + (P(),)
    return jax.shard_map(
        functools.partial(on_device, mesh.shape["fsdp"]),
        mesh=mesh,
        in_specs=in_specs,
        out_specs=out_specs,
        check_vma=False,
    )
```
